32 devices in a mesh: grp: 2 (over x), samp: 16 (over z, y, core).
Axes of the slice: x: 2, y: 2, z: 4, core: 2. Of those that a mesh axis runs over, the one named last changes fastest.
Arguments:
- tokens: bfloat16 [2, 1536, 8, 512], P('grp', 'samp'), may hold values from -6 to 6
- segments: int32 [2, 1536], P('grp', 'samp'), may hold values from -1 to 3, as said below
- cotangent: bfloat16 [2, 1536, 8, 512], P('grp', 'samp'), may hold values from -6 to 6
- first_gain: float32 [512], replicated, may hold values from 0.1 to 1.9
- first_shift: float32 [512], replicated, may hold values from -3 to 3
- sample_qkv: bfloat16 [512, 1536], replicated, may hold values from -0.25 to 0.25
- sample_out: bfloat16 [512, 512], replicated, may hold values from -0.75 to 0.75
- second_gain: float32 [512], replicated, may hold values from 0.1 to 1.9
- second_shift: float32 [512], replicated, may hold values from -3 to 3
- feature_qkv: bfloat16 [512, 1536], replicated, may hold values from -0.25 to 0.25
- feature_out: bfloat16 [512, 512], replicated, may hold values from -0.75 to 0.75
- third_gain: float32 [512], replicated, may hold values from 0.1 to 1.9
- third_shift: float32 [512], replicated, may hold values from -3 to 3
- up_weight: bfloat16 [512, 2048], replicated, may hold values from -0.25 to 0.25
- up_bias: float32 [2048], replicated, may hold values from -3 to 3
- down_weight: bfloat16 [2048, 512], replicated, may hold values from -0.125 to 0.125
- down_bias: float32 [512], replicated, may hold values from -3 to 3
Outputs:
- output: bfloat16 [2, 1536, 8, 512], P('grp', 'samp')
- grad_tokens: float32 [2, 1536, 8, 512], P('grp', 'samp')
- grad_first_gain: float32 [512], P('samp')
- grad_first_shift: float32 [512], P('samp')
- grad_sample_qkv: float32 [512, 1536], P('samp')
- grad_sample_out: float32 [512, 512], P('samp')
- grad_second_gain: float32 [512], P('samp')
- grad_second_shift: float32 [512], P('samp')
- grad_feature_qkv: float32 [512, 1536], P('samp')
- grad_feature_out: float32 [512, 512], P('samp')
- grad_third_gain: float32 [512], P('samp')
- grad_third_shift: float32 [512], P('samp')
- grad_up_weight: float32 [512, 2048], P('samp')
- grad_up_bias: float32 [2048], P('samp')
- grad_down_weight: float32 [2048, 512], P('samp')
- grad_down_bias: float32 [512], P('samp')
The draws below stay inside these ranges and needn't reach their ends.
Inputs may be any that keep to these rules, and one draw needn't show every extreme that they name: `segments`: -1 marks a padding slot, other values name a sample's task.
All inputs are finite; a program needn't handle non-finite values.
Results may differ from the reference program's by a relative error of at most 0.023.
Values may be sent and summed in bfloat16 or wider, within the bound.
No kernel may reach another device: no remote copies, remote signals or barrier semaphores. Data moves between devices by JAX's collectives and lax.ppermute only.
A program may use at most 512 MiB of HBM per device.

```python
import jax
import jax.numpy as jnp
from jax import lax

D = 512
H = 8
HD = 64
FF = 2048
F = 8
TASKS = 4
S_DEV = 96
SAMPLES = 1536
GROUPS = 2


def draw_segments(key, part):
    key = jax.random.fold_in(key, 7)
    first_key, second_key = jax.random.split(key)
    free_ids = jax.random.randint(first_key, (GROUPS, SAMPLES), -1, TASKS)
    spanning = jax.random.randint(second_key, (GROUPS, 1), 0, TASKS)
    leaders = (jnp.arange(SAMPLES, dtype=jnp.int32) % S_DEV == 0)[None, :]
    return jnp.where(leaders, spanning, free_ids).astype(jnp.int32)


def levels(own_key, extent, shards, low, largest):
    level, own = 1.0, jax.random.fold_in(own_key, 6)
    for dim, blocks in shards:
        draws = jnp.exp(jax.random.uniform(jax.random.fold_in(own, dim), (blocks,), jnp.float32, low / len(shards), largest / len(shards)))
        level = level * jnp.repeat(draws, extent[dim] // blocks).reshape([-1 if axis == dim else 1 for axis in range(len(extent))])
    return level


def centred(key, shape, spread, bound, cuts=(), kind=jnp.bfloat16):
    entries = spread * jax.random.normal(key, shape, jnp.float32)
    if cuts:
        entries = entries * levels(key, shape, cuts, -0.22, 0.18)
    return jnp.clip(entries, -bound, bound).astype(kind)


def setup_inputs(seed: int = 0) -> dict:
    seeds = jax.random.split(jax.random.key(seed), 18)
    tokens = centred(seeds[0], (GROUPS, SAMPLES, F, D), 1.0, 6.0, ((0, 2), (1, 16)))
    segments = draw_segments(jax.random.fold_in(seeds[17], 71), 0)
    cotangent = centred(seeds[2], (GROUPS, SAMPLES, F, D), 1.0, 6.0, ((0, 2), (1, 16)))
    first_gain = jnp.clip(1.0 + 0.18 * jax.random.normal(seeds[3], (D,), jnp.float32), 0.1, 1.9)
    first_shift = centred(seeds[4], (D,), 0.3, 3.0, (), jnp.float32)
    sample_qkv = centred(seeds[5], (D, 3 * D), D ** -0.5, 0.25)
    sample_out = centred(seeds[6], (D, D), (D // 8) ** -0.5, 0.75)
    second_gain = jnp.clip(1.0 + 0.18 * jax.random.normal(seeds[7], (D,), jnp.float32), 0.1, 1.9)
    second_shift = centred(seeds[8], (D,), 0.3, 3.0, (), jnp.float32)
    feature_qkv = centred(seeds[9], (D, 3 * D), D ** -0.5, 0.25)
    feature_out = centred(seeds[10], (D, D), (D // 8) ** -0.5, 0.75)
    third_gain = jnp.clip(1.0 + 0.18 * jax.random.normal(seeds[11], (D,), jnp.float32), 0.1, 1.9)
    third_shift = centred(seeds[12], (D,), 0.3, 3.0, (), jnp.float32)
    up_weight = centred(seeds[13], (D, FF), D ** -0.5, 0.25)
    up_bias = centred(seeds[14], (FF,), 0.3, 3.0, (), jnp.float32)
    down_weight = centred(seeds[15], (FF, D), FF ** -0.5, 0.125)
    down_bias = centred(seeds[16], (D,), 0.3, 3.0, (), jnp.float32)
    return {"tokens": tokens, "segments": segments, "cotangent": cotangent, "first_gain": first_gain, "first_shift": first_shift, "sample_qkv": sample_qkv, "sample_out": sample_out, "second_gain": second_gain, "second_shift": second_shift, "feature_qkv": feature_qkv, "feature_out": feature_out, "third_gain": third_gain, "third_shift": third_shift, "up_weight": up_weight, "up_bias": up_bias, "down_weight": down_weight, "down_bias": down_bias}


EPSILON = 1e-05
SCALING = 0.125
NEGATIVE = -1e+30
HIGHEST = lax.Precision.HIGHEST

@jax.custom_vjp
def low(v):
    return lax.optimization_barrier(v.astype(jnp.bfloat16)).astype(jnp.float32)

@jax.custom_vjp
def low_back(v):
    return v

def low_keep(v):
    return (low(v), None)

def low_pass(kept, grad):
    return (grad,)

def back_keep(v):
    return (v, None)

def back_low(kept, grad):
    return (low(grad),)
low.defvjp(low_keep, low_pass)
low_back.defvjp(back_keep, back_low)

def norm_rows(values, gain, shift):
    centre = values - lax.optimization_barrier(jnp.mean(values, -1, keepdims=True))
    factor = lax.rsqrt(lax.optimization_barrier(jnp.mean(centre * centre, -1, keepdims=True)) + EPSILON)
    return centre * factor * gain + shift

def matmul(left, right):
    return jnp.dot(left, right, precision=HIGHEST)

def softmax_last(scores):
    shifted = scores - lax.optimization_barrier(jnp.max(scores, -1, keepdims=True))
    expo = jnp.exp(shifted)
    return expo / lax.optimization_barrier(jnp.sum(expo, -1, keepdims=True))

def gelu_fn(values):
    return jax.nn.gelu(values, approximate=True)

def sample_heads(query, keys, values, allowed):
    scores = low_back(jnp.einsum('ihd,jhd->hij', query, keys, precision=HIGHEST) * SCALING)
    scores = jnp.where(allowed[None], scores, NEGATIVE)
    probs = softmax_last(scores)
    return jnp.einsum('hij,jhd->ihd', low(probs), values, precision=HIGHEST)

def group_forward(params, slab, seg_ids):
    first_gain, first_shift, sample_qkv, sample_out, second_gain, second_shift, feature_qkv, feature_out, third_gain, third_shift, up_weight, up_bias, down_weight, down_bias = params
    rows_all = slab.reshape(SAMPLES * F, D)
    first_normed = low(norm_rows(rows_all, first_gain, first_shift))
    first_proj = low(low_back(matmul(first_normed, low(sample_qkv))))
    query = first_proj[:, :D].reshape(SAMPLES, F, H, HD).transpose(1, 0, 2, 3)
    keys = first_proj[:, D:2 * D].reshape(SAMPLES, F, H, HD).transpose(1, 0, 2, 3)
    values = first_proj[:, 2 * D:].reshape(SAMPLES, F, H, HD).transpose(1, 0, 2, 3)
    places = jnp.arange(SAMPLES, dtype=jnp.int32)
    allowed = (seg_ids[:, None] == seg_ids[None, :]) & (seg_ids[None, :] >= 0) | (places[:, None] == places[None, :])

    def per_feature(triple):
        return sample_heads(triple[0], triple[1], triple[2], allowed)
    mixed = lax.map(jax.checkpoint(per_feature), (query, keys, values))
    first_attn = low(low_back(mixed.transpose(1, 0, 2, 3).reshape(SAMPLES * F, D)))
    after_first = rows_all + low_back(matmul(first_attn, low(sample_out)))
    second_normed = low(norm_rows(after_first, second_gain, second_shift))
    second_proj = low(low_back(matmul(second_normed, low(feature_qkv))))
    query_two = second_proj[:, :D].reshape(SAMPLES, F, H, HD)
    keys_two = second_proj[:, D:2 * D].reshape(SAMPLES, F, H, HD)
    values_two = second_proj[:, 2 * D:].reshape(SAMPLES, F, H, HD)
    scores_two = low_back(jnp.einsum('ifhd,ighd->ihfg', query_two, keys_two, precision=HIGHEST) * SCALING)
    probs_two = softmax_last(scores_two)
    mixed_two = jnp.einsum('ihfg,ighd->ifhd', low(probs_two), values_two, precision=HIGHEST)
    second_attn = low(low_back(mixed_two.reshape(SAMPLES * F, D)))
    after_second = after_first + low_back(matmul(second_attn, low(feature_out)))
    third_normed = low(norm_rows(after_second, third_gain, third_shift))
    hidden_pre = low_back(matmul(third_normed, low(up_weight)) + up_bias)
    hidden = low(gelu_fn(hidden_pre))
    result = after_second + low_back(matmul(hidden, low(down_weight)) + down_bias)
    return result.reshape(SAMPLES, F, D)

def reference(tokens, segments, cotangent, first_gain, first_shift, sample_qkv, sample_out, second_gain, second_shift, feature_qkv, feature_out, third_gain, third_shift, up_weight, up_bias, down_weight, down_bias):
    params = (first_gain.astype(jnp.float32), first_shift.astype(jnp.float32), sample_qkv.astype(jnp.float32), sample_out.astype(jnp.float32), second_gain.astype(jnp.float32), second_shift.astype(jnp.float32), feature_qkv.astype(jnp.float32), feature_out.astype(jnp.float32), third_gain.astype(jnp.float32), third_shift.astype(jnp.float32), up_weight.astype(jnp.float32), up_bias.astype(jnp.float32), down_weight.astype(jnp.float32), down_bias.astype(jnp.float32))
    inputs = tokens.astype(jnp.float32)

    def forward(slabs, weights):

        def one_slab(pair):
            return group_forward(weights, pair[0], pair[1])
        return lax.map(jax.checkpoint(one_slab), (slabs, segments))
    result, pull = jax.vjp(forward, inputs, params)
    grad_inputs, grads = pull(cotangent.astype(jnp.float32))
    return (result.astype(jnp.bfloat16), grad_inputs, grads[0], grads[1], grads[2], grads[3], grads[4], grads[5], grads[6], grads[7], grads[8], grads[9], grads[10], grads[11], grads[12], grads[13])
```

```python
import functools
import math

import jax
import jax.numpy as jnp
from jax import lax
from jax.experimental import pallas as pl
from jax.experimental.pallas import tpu as pltpu
from jax.sharding import PartitionSpec as P

H = 8
HD = 64
EPSILON = 1e-05
SCALING = 0.125
NEGATIVE = -1e30
BF = jnp.bfloat16
F32 = jnp.float32
TILE = 256
LANES = 128
PAD = 8
GELU_C = math.sqrt(2.0 / math.pi)
GELU_A = 0.044715
VMEM_LIMIT = 60 * 1024 * 1024
CLASSES = 5


def dot(a, b):
    return jnp.dot(a, b, preferred_element_type=F32)


def dot_nt(a, b):
    return lax.dot_general(a, b, (((1,), (1,)), ((), ())), preferred_element_type=F32)


def dot_tn(a, b):
    return lax.dot_general(a, b, (((0,), (0,)), ((), ())), preferred_element_type=F32)


def ln_parts(v):
    c = v - jnp.mean(v, -1, keepdims=True)
    r = lax.rsqrt(jnp.mean(c * c, -1, keepdims=True) + EPSILON)
    return c * r, r


def ln_back(dh, n, r, g):
    e = dh * g
    return r * (e - jnp.mean(e, -1, keepdims=True) - n * jnp.mean(e * n, -1, keepdims=True))


def flip(v):
    return jnp.transpose(v)


def lay(scr, v):
    for a in range(scr.shape[0]):
        scr[a] = v[:, a * LANES : (a + 1) * LANES]


def lift(scr):
    return jnp.concatenate([scr[a] for a in range(scr.shape[0])], -1)


def take(scr, first, count, step):
    return jnp.concatenate(
        [scr[a, pl.ds(first, count, stride=step), :] for a in range(scr.shape[0])], -1
    )


def place(scr, first, count, step, v):
    for a in range(scr.shape[0]):
        scr[a, pl.ds(first, count, stride=step), :] = v[:, a * LANES : (a + 1) * LANES]


def iota(shape, dim):
    return lax.broadcasted_iota(jnp.int32, shape, dim).astype(F32)


def call(fn, outs, scratch, *args, smem=(), smem_out=(), cost=None):
    def spec(space):
        return pl.BlockSpec(memory_space=space)

    in_specs = [spec(pltpu.SMEM if i in smem else pltpu.VMEM) for i in range(len(args))]
    out_specs = [spec(pltpu.SMEM if i in smem_out else pltpu.VMEM) for i in range(len(outs))]
    return pl.pallas_call(
        fn,
        out_shape=[jax.ShapeDtypeStruct(*o) for o in outs],
        in_specs=in_specs,
        out_specs=out_specs,
        scratch_shapes=scratch,
        compiler_params=pltpu.CompilerParams(vmem_limit_bytes=VMEM_LIMIT),
        cost_estimate=cost,
    )(*args)


def pack_kernel(tok, seg, out, scr):
    count, feats, width = tok.shape
    lay(scr, tok[...].astype(F32).reshape(count * feats, width))
    row = seg[...].astype(F32)
    for f in range(feats):
        out[f, :count, :] = take(scr, f, count, feats).astype(BF)
        out[f, count:, :] = jnp.zeros((PAD, width), BF)
        out[f, count:, :count] = jnp.broadcast_to(row, (PAD, count)).astype(BF)


def codes(pos, starts):
    cls = jnp.zeros_like(pos)
    for st in starts:
        cls = cls + jnp.where(pos >= st, 1.0, 0.0)
    return jnp.where(cls >= CLASSES - 1, pos + CLASSES, cls)


def tile_range(start_ref, first, total):
    last = first + TILE - 1
    lo = jnp.int32(0)
    hi = start_ref[1]
    for c in range(1, CLASSES - 1):
        st = start_ref[c]
        lo = jnp.where(first >= st, st, lo)
        hi = jnp.where(last >= st, start_ref[c + 1], hi)
    pad = start_ref[CLASSES - 1]
    lo = jnp.where(first >= pad, first, lo)
    hi = jnp.where(last >= pad, first + TILE, hi)
    return lo // TILE, (hi + TILE - 1) // TILE


def permute_block(rank_row, first, rows, total):
    pos = iota((rows, LANES), 0) + first.astype(F32)
    parts = []
    for j in range(total // LANES):
        hit = rank_row[0:1, j * LANES : (j + 1) * LANES] == pos
        parts.append(jnp.where(hit, 1.0, 0.0).astype(BF))
    return jnp.concatenate(parts, -1)


def unpermute_block(rank_col, total):
    rows = rank_col.shape[0]
    parts = []
    for j in range(total // LANES):
        pos = iota((1, LANES), 1) + float(j * LANES)
        parts.append(jnp.where(rank_col == pos, 1.0, 0.0).astype(BF))
    return jnp.concatenate(parts, -1)


def fwd_kernel(hpd, hl, r_ref, *refs):
    xparts = refs[:hpd]
    (g1, b1, wqt, wk, wvt) = refs[hpd : hpd + 5]
    (o_send, xs_out, ot_out, lse_out, rank_row, rank_col, start_ref) = refs[hpd + 5 : hpd + 12]
    (x_scr, seg_scr, qtz, k_scr, vt, o_scr, code_col, code_row, acc, top) = refs[hpd + 12 :]
    feats = xparts[0].shape[0]
    count = xparts[0].shape[1] - PAD
    total = x_scr.shape[0]
    cl = hl * HD
    r = r_ref[0]
    chunks = total // LANES

    for s in range(hpd):
        for k in range(feats):
            at = (s * feats + k) * count
            x_scr[at : at + count, :] = xparts[s][k, :count, :]
            row = xparts[s][k, count : count + PAD, :LANES].astype(F32)[0:1]
            col = jnp.transpose(jnp.broadcast_to(row, (LANES, LANES)))
            seg_scr[at : at + count, :] = col[:count, :]

    seg = seg_scr[...]
    cls = jnp.where(seg < 0.0, float(CLASSES - 1), seg)
    seg_scr[...] = cls * 8192.0 + iota((total, LANES), 0)
    key_rows = []
    for j in range(chunks):
        blk = seg_scr[j * LANES : (j + 1) * LANES, :]
        key_rows.append(jnp.transpose(blk)[0:8, :])

    def count_less(i, carry):
        blk = seg_scr[pl.ds(pl.multiple_of(i * 64, 64), 64), :]
        out = []
        for j in range(chunks):
            less = jnp.where(blk < key_rows[j][0:1], 1.0, 0.0)
            out.append(carry[j] + jnp.sum(less.reshape(8, 8, LANES), 0))
        return tuple(out)

    ranks = lax.fori_loop(
        0, total // 64, count_less, tuple(jnp.zeros((8, LANES), F32) for _ in range(chunks))
    )
    for j in range(chunks):
        row = jnp.sum(ranks[j], 0, keepdims=True)
        rank_row[:, j * LANES : (j + 1) * LANES] = jnp.broadcast_to(row, (8, LANES))
        rank_col[j * LANES : (j + 1) * LANES, :] = jnp.transpose(
            jnp.broadcast_to(row, (LANES, LANES))
        )
    starts = []
    keys = jnp.concatenate([k[0:1] for k in key_rows], 0)
    for c in range(1, CLASSES):
        st = jnp.sum(jnp.where(keys < c * 8192.0, 1.0, 0.0))
        starts.append(st)
        start_ref[c] = st.astype(jnp.int32)
    start_ref[0] = jnp.int32(0)
    for c in range(CLASSES, 8):
        start_ref[c] = jnp.int32(total)
    code_col[...] = codes(iota((total, LANES), 0), starts)
    code_row[...] = codes(iota((8, total), 1), starts)

    qtz[...] = jnp.zeros_like(qtz)
    ones = jnp.where(iota((16, total), 0) == 0.0, 1.0, 0.0).astype(BF)
    for h in range(hl):
        vt[h, HD:, :] = ones

    def project(b, _):
        at = pl.multiple_of(b * TILE, TILE)
        block = dot(permute_block(rank_row, at, TILE, total), x_scr[...])
        xs_out[pl.ds(at, TILE), :] = block.astype(BF)
        n, _r = ln_parts(block)
        h1 = (n * g1[...] + b1[...]).astype(BF)
        qt = dot_nt(wqt[...], h1).astype(BF)
        k_scr[pl.ds(at, TILE), :] = dot(h1, wk[...]).astype(BF)
        vv = dot_nt(wvt[...], h1).astype(BF)
        for h in range(hl):
            sub = (h % 2) * HD
            qtz[h, sub : sub + HD, pl.ds(at, TILE)] = qt[h * HD : (h + 1) * HD]
            vt[h, :HD, pl.ds(at, TILE)] = vv[h * HD : (h + 1) * HD]
        return 0

    lax.fori_loop(0, total // TILE, project, 0)

    def attend(b, _):
        at = pl.multiple_of(b * TILE, TILE)
        t0, t1 = tile_range(start_ref, at, total)
        acc[...] = jnp.zeros_like(acc)
        top[...] = jnp.full_like(top, NEGATIVE)
        crow = code_row[0:1, pl.ds(at, TILE)]

        def step(t, _):
            kt = pl.multiple_of(t * TILE, TILE)
            ccol = code_col[pl.ds(kt, TILE), :]
            ccol = jnp.concatenate([ccol] * (TILE // LANES), -1)
            seen = ccol == crow
            for h in range(hl):
                pair = (h // 2) * LANES
                s = dot(k_scr[pl.ds(kt, TILE), pair : pair + LANES], qtz[h, :, pl.ds(at, TILE)])
                s = jnp.where(seen, s, NEGATIVE)
                old = top[h, 0:1, :]
                new = jnp.maximum(old, jnp.max(s, 0, keepdims=True))
                p = jnp.exp(s - new).astype(BF)
                o = dot(vt[h, :, pl.ds(kt, TILE)], p)
                acc[h] = acc[h] * jnp.exp(old - new) + o
                top[h] = jnp.broadcast_to(new, (8, TILE))
            return 0

        lax.fori_loop(t0, t1, step, 0)
        outs = []
        for h in range(hl):
            total_h = acc[h, HD : HD + 1, :]
            outs.append(acc[h, :HD, :] / total_h)
            lse_out[h : h + 1, pl.ds(at, TILE)] = top[h, 0:1, :] + jnp.log(total_h)
        ot = jnp.concatenate(outs, 0)
        ot_out[:, pl.ds(at, TILE)] = ot.astype(BF)
        o_scr[pl.ds(at, TILE), :] = jnp.transpose(ot).astype(BF)
        return 0

    lax.fori_loop(0, total // TILE, attend, 0)

    group = feats // 2
    for blk in range(total // (group * count)):
        at = blk * group * count
        hot = unpermute_block(rank_col[at : at + group * count, :], total)
        o = dot(hot, o_scr[...]).astype(BF)
        for j in range(group):
            s, k = divmod(blk * group + j, feats)
            dest = k * hpd + lax.rem(r - s + hpd, hpd)
            o_send[dest] = o[j * count : (j + 1) * count]


def prep_kernel(hl, xs, g1, b1, wqt, wq, wk, wkt, wv, k_out, kt_out, v_out, qtz, qz, h1t):
    total = xs.shape[0]
    cl = hl * HD
    qtz[...] = jnp.zeros_like(qtz)
    lane = iota((1, LANES), 1)

    def project(b, _):
        at = pl.multiple_of(b * TILE, TILE)
        n, _r = ln_parts(xs[pl.ds(at, TILE), :].astype(F32))
        h1f = n * g1[...] + b1[...]
        h1 = h1f.astype(BF)
        h1t[:, pl.ds(at, TILE)] = jnp.transpose(h1f).astype(BF)
        qt = dot_nt(wqt[...], h1).astype(BF)
        q = dot(h1, wq[...])
        k_out[pl.ds(at, TILE), :] = dot(h1, wk[...]).astype(BF)
        v_out[pl.ds(at, TILE), :] = dot(h1, wv[...]).astype(BF)
        kt_out[:, pl.ds(at, TILE)] = dot_nt(wkt[...], h1).astype(BF)
        for h in range(hl):
            sub = (h % 2) * HD
            pair = (h // 2) * LANES
            qtz[h, sub : sub + HD, pl.ds(at, TILE)] = qt[h * HD : (h + 1) * HD]
            mine = (lane >= sub) & (lane < sub + HD)
            qz[h, pl.ds(at, TILE), :] = jnp.where(mine, q[:, pair : pair + LANES], 0.0).astype(BF)
        return 0

    lax.fori_loop(0, total // TILE, project, 0)


def bwd_kernel(
    hpd,
    hl,
    r_ref,
    f_ref,
    start_ref,
    do_recv,
    xs,
    k_in,
    kt_in,
    v_in,
    qtz,
    qz,
    h1t,
    w3,
    ot,
    lse,
    rank_row,
    rank_col,
    *refs,
):
    feats = do_recv.shape[0] // hpd
    count = do_recv.shape[1]
    total = xs.shape[0]
    width = xs.shape[1]
    cl = hl * HD
    dh_outs = refs[:hpd]
    g_keep, g_send = refs[hpd : hpd + 2]
    (do_scr, dotz, doz, dots, dqt, dqkv, dh_scr, dw_scr, code_col, code_row, dv_acc, dk_acc) = refs[
        hpd + 2 :
    ]
    r = r_ref[0]
    f = f_ref[0]
    lane = iota((1, LANES), 1)

    for s in range(hpd):
        for k in range(feats):
            at = (s * feats + k) * count
            do_scr[at : at + count, :] = do_recv[k * hpd + lax.rem(r - s + hpd, hpd)]
    starts = [start_ref[c].astype(F32) for c in range(1, CLASSES)]
    code_col[...] = codes(iota((total, LANES), 0), starts)
    code_row[...] = codes(iota((8, total), 1), starts)
    dotz[...] = jnp.zeros_like(dotz)

    def arrange(b, _):
        at = pl.multiple_of(b * TILE, TILE)
        block = dot(permute_block(rank_row, at, TILE, total), do_scr[...])
        blockt = jnp.transpose(block)
        prod = blockt * ot[:, pl.ds(at, TILE)].astype(F32)
        for h in range(hl):
            sub = (h % 2) * HD
            pair = (h // 2) * LANES
            mine = (lane >= sub) & (lane < sub + HD)
            dotz[h, sub : sub + HD, pl.ds(at, TILE)] = blockt[h * HD : (h + 1) * HD].astype(BF)
            doz[h, pl.ds(at, TILE), :] = jnp.where(mine, block[:, pair : pair + LANES], 0.0).astype(BF)
            dots[h : h + 1, pl.ds(at, TILE)] = jnp.sum(prod[h * HD : (h + 1) * HD], 0, keepdims=True)
        return 0

    lax.fori_loop(0, total // TILE, arrange, 0)
    dqt[...] = jnp.zeros_like(dqt)

    def keys(b, _):
        kt = pl.multiple_of(b * TILE, TILE)
        t0, t1 = tile_range(start_ref, kt, total)
        ccol = code_col[pl.ds(kt, TILE), :]
        ccol = jnp.concatenate([ccol] * (TILE // LANES), -1)
        dv_acc[...] = jnp.zeros_like(dv_acc)
        dk_acc[...] = jnp.zeros_like(dk_acc)

        def step(t, _):
            at = pl.multiple_of(t * TILE, TILE)
            seen = ccol == code_row[0:1, pl.ds(at, TILE)]
            for h in range(hl):
                pair = (h // 2) * LANES
                kb = k_in[pl.ds(kt, TILE), pair : pair + LANES]
                vb = v_in[pl.ds(kt, TILE), pair : pair + LANES]
                s = dot(kb, qtz[h, :, pl.ds(at, TILE)])
                p = jnp.where(seen, jnp.exp(s - lse[h : h + 1, pl.ds(at, TILE)]), 0.0)
                dp = dot(vb, dotz[h, :, pl.ds(at, TILE)])
                ds = (p * (dp - dots[h : h + 1, pl.ds(at, TILE)])).astype(BF)
                dv_acc[h // 2] += dot(p.astype(BF), doz[h, pl.ds(at, TILE), :])
                dk_acc[h // 2] += dot(ds, qz[h, pl.ds(at, TILE), :])
                rows = slice(h * HD, (h + 1) * HD)
                dqt[rows, pl.ds(at, TILE)] += dot(kt_in[rows, pl.ds(kt, TILE)], ds)
            return 0

        lax.fori_loop(t0, t1, step, 0)
        for p2 in range((hl + 1) // 2):
            lo = p2 * LANES
            dqkv[pl.ds(kt, TILE), cl + lo : cl + lo + LANES] = dk_acc[p2].astype(BF)
            dqkv[pl.ds(kt, TILE), 2 * cl + lo : 2 * cl + lo + LANES] = dv_acc[p2].astype(BF)
        return 0

    lax.fori_loop(0, total // TILE, keys, 0)

    def finish(b, carry):
        at = pl.multiple_of(b * TILE, TILE)
        dq = jnp.transpose(dqt[:, pl.ds(at, TILE)]) * SCALING
        dqkv[pl.ds(at, TILE), :cl] = dq.astype(BF)
        dh = dot_nt(dqkv[pl.ds(at, TILE), :], w3[...])
        n, _r = ln_parts(xs[pl.ds(at, TILE), :].astype(F32))
        dh_scr[pl.ds(at, TILE), :] = dh.astype(BF)
        return (
            carry[0] + jnp.sum((dh * n).reshape(TILE // 8, 8, width), 0),
            carry[1] + jnp.sum(dh.reshape(TILE // 8, 8, width), 0),
        )

    zero = jnp.zeros((8, width), F32)
    gg, gb = lax.fori_loop(0, total // TILE, finish, (zero, zero))

    for c in range(3):
        dw_scr[:, c * cl : (c + 1) * cl] = dot(h1t[...], dqkv[:, c * cl : (c + 1) * cl]).astype(BF)
    rows = width // feats
    extra = jnp.concatenate([jnp.sum(gg, 0, keepdims=True), jnp.sum(gb, 0, keepdims=True)], 0)
    extra = jnp.concatenate([extra, jnp.zeros((6, width), F32)], 0).astype(BF)
    half = feats // 2
    for e in range(feats):
        ref, at = (g_keep, e) if e < half else (g_send, e - half)
        src = pl.multiple_of(lax.bitwise_xor(f, e) * rows, rows)
        ref[at, :rows, :] = dw_scr[pl.ds(src, rows), :]
        for c in range(0, width, cl):
            ref[at, rows + 8 * (c // cl) : rows + 8 * (c // cl) + 8, :cl] = extra[:, c : c + cl]
        for c in range(0, width, cl):
            ref[at, rows + 8 * (c // cl) : rows + 8 * (c // cl) + 8, cl:] = jnp.zeros((8, 2 * cl), BF)

    group = feats // 2
    for blk in range(total // (group * count)):
        at = blk * group * count
        hot = unpermute_block(rank_col[at : at + group * count, :], total)
        o = dot(hot, dh_scr[...]).astype(BF)
        for j in range(group):
            s, k = divmod(blk * group + j, feats)
            dh_outs[s][k] = o[j * count : (j + 1) * count]


def norm_kernel(hpd, *refs):
    parts = refs[:hpd]
    x, g1, out = refs[hpd:]
    feats, count, _w = parts[0].shape
    for k in range(feats):
        dh = parts[0][k].astype(F32)
        for s in range(1, hpd):
            dh = dh + parts[s][k].astype(F32)
        n, r = ln_parts(x[k, :count, :].astype(F32))
        out[k] = ln_back(dh, n, r, g1[...]).astype(BF)


def final_kernel(dx1, dv, out, scr):
    feats, count, width = dv.shape
    for f in range(feats):
        val = dx1[f * count : (f + 1) * count, :] + dv[f].astype(F32)
        place(scr, f, count, feats, val)
    out[...] = lift(scr).reshape(count, feats, width)


def rows_kernel(
    hpd,
    order,
    me_ref,
    o_recv,
    xt,
    cot,
    g2,
    b2,
    g3,
    b3,
    ub,
    db,
    wso,
    wfq,
    wfo,
    wup,
    wdn,
    out,
    dx1,
    do_send,
    g_keep,
    g_send,
    wide,
    ct,
    o1,
    x1,
    h2,
    qkv,
    o2,
    x2,
    h3,
    u,
    dz,
    dx2,
    do2,
    dqkv,
    pscr,
    tr,
    wblk,
    ubg,
    wdn_scr,
):
    feats = xt.shape[0]
    count = xt.shape[1] - PAD
    width = xt.shape[2]
    rows = feats * count
    hidden = wup.shape[1]
    n = o_recv.shape[0]
    cl = o_recv.shape[2]
    half = rows // 2
    me = me_ref[0]
    lane = iota((1, LANES), 1)
    part = 16
    tiles = count // part
    size = feats * part

    lay(wide, cot[...].astype(F32).reshape(rows, width))
    for f in range(feats):
        ct[f * count : (f + 1) * count, :] = take(wide, f, count, feats).astype(BF)
        for c in range(hpd):
            o1[f * count : (f + 1) * count, c * cl : (c + 1) * cl] = o_recv[f * hpd + c]

    for b in range(2):
        at = slice(b * half, (b + 1) * half)
        x = xt[b * feats // 2 : (b + 1) * feats // 2, :count, :].astype(F32).reshape(half, width)
        v = x + dot(o1[at, :], wso[...])
        x1[at, :] = v
        nn, _r = ln_parts(v)
        h2[at, :] = (nn * g2[...] + b2[...]).astype(BF)

    qkv3 = qkv

    def qkv_step(c, _):
        cols = pl.ds(pl.multiple_of(c * TILE, TILE), TILE)
        scale = jnp.where(c < width // TILE, SCALING, 1.0)
        y = dot(h2[...], wfq[:, cols])
        qkv3[:, :, cols] = (y * scale).astype(BF).reshape(feats, count, TILE)
        return 0

    lax.fori_loop(0, 3 * width // TILE, qkv_step, 0)

    ri = lax.broadcasted_iota(jnp.int32, (size, size), 0)
    ci = lax.broadcasted_iota(jnp.int32, (size, size), 1)
    same = lax.rem(ri, part) == lax.rem(ci, part)

    def masked(v, h):
        sub = (h % 2) * HD
        return jnp.where((lane >= sub) & (lane < sub + HD), v, 0.0).astype(BF)

    def feat_fwd(t, _):
        at = pl.ds(pl.multiple_of(t * part, part), part)
        for p2 in range(H // 2):
            lo = p2 * LANES
            q = qkv3[:, at, lo : lo + LANES].reshape(size, LANES)
            k = qkv3[:, at, width + lo : width + lo + LANES].reshape(size, LANES)
            v = qkv3[:, at, 2 * width + lo : 2 * width + lo + LANES].reshape(size, LANES)
            o = jnp.zeros((size, LANES), F32)
            for h in (2 * p2, 2 * p2 + 1):
                s = dot_nt(q, masked(k, h))
                s = jnp.where(same, s, NEGATIVE)
                e = jnp.exp(s - jnp.max(s, -1, keepdims=True))
                p = (e / jnp.sum(e, -1, keepdims=True)).astype(BF)
                pscr[t, h] = p
                o = o + dot(p, masked(v, h))
            o2[:, at, lo : lo + LANES] = o.astype(BF).reshape(feats, part, LANES)
        return 0

    lax.fori_loop(0, tiles, feat_fwd, 0)

    for b in range(2):
        at = slice(b * half, (b + 1) * half)
        o = o2[b * feats // 2 : (b + 1) * feats // 2, :, :].reshape(half, width)
        v = x1[at, :] + dot(o, wfo[...])
        x2[at, :] = v
        nn, _r = ln_parts(v)
        h3[at, :] = (nn * g3[...] + b3[...]).astype(BF)

    def ffn(c, _):
        cols = pl.ds(pl.multiple_of(c * TILE, TILE), TILE)
        total = jnp.zeros((8, TILE), F32)
        for b in range(2):
            at = slice(b * half, (b + 1) * half)
            z = dot(h3[at, :], wup[:, cols]) + ub[0:1, cols]
            zz = z * z
            th = jnp.tanh(GELU_C * z * (1.0 + GELU_A * zz))
            h1p = 0.5 * (1.0 + th)
            u[at, cols] = (z * h1p).astype(BF)
            slope = h1p + 0.5 * z * (1.0 - th * th) * (GELU_C * (1.0 + 3.0 * GELU_A * zz))
            du = dot_nt(ct[at, :], wdn[cols, :])
            d = (du * slope).astype(BF)
            dz[at, cols] = d
            total = total + jnp.sum(d.astype(F32).reshape(half // 8, 8, TILE), 0)
        ubg[:, cols] = total
        return 0

    lax.fori_loop(0, hidden // TILE, ffn, 0)

    vectors = []
    gg = jnp.zeros((1, width), F32)
    gb = jnp.zeros((1, width), F32)
    gd = jnp.zeros((1, width), F32)
    for b in range(2):
        at = slice(b * half, (b + 1) * half)
        y = x2[at, :] + dot(u[at, :], wdn[...]) + db[...]
        for j in range(feats // 2):
            f = b * (feats // 2) + j
            place(wide, f, count, feats, y[j * count : (j + 1) * count])
        dh = dot_nt(dz[at, :], wup[...])
        nn, r = ln_parts(x2[at, :])
        c = ct[at, :].astype(F32)
        gg = gg + jnp.sum(dh * nn, 0, keepdims=True)
        gb = gb + jnp.sum(dh, 0, keepdims=True)
        gd = gd + jnp.sum(c, 0, keepdims=True)
        v = c + ln_back(dh, nn, r, g3[...])
        dx2[at, :] = v
        do2[b * feats // 2 : (b + 1) * feats // 2, :, :] = (
            dot_nt(v.astype(BF), wfo[...]).astype(BF).reshape(feats // 2, count, width)
        )
    out[...] = lift(wide).reshape(count, feats, width).astype(BF)
    vectors = [gg, gb, gd]

    def feat_bwd(t, _):
        at = pl.ds(pl.multiple_of(t * part, part), part)
        for p2 in range(H // 2):
            lo = p2 * LANES
            q = qkv3[:, at, lo : lo + LANES].reshape(size, LANES)
            k = qkv3[:, at, width + lo : width + lo + LANES].reshape(size, LANES)
            v = qkv3[:, at, 2 * width + lo : 2 * width + lo + LANES].reshape(size, LANES)
            g = do2[:, at, lo : lo + LANES].reshape(size, LANES)
            dq = jnp.zeros((size, LANES), F32)
            dk = jnp.zeros((size, LANES), F32)
            dv = jnp.zeros((size, LANES), F32)
            for h in (2 * p2, 2 * p2 + 1):
                p = pscr[t, h]
                pf = p.astype(F32)
                dp = dot_nt(g, masked(v, h))
                ds = pf * (dp - jnp.sum(pf * dp, -1, keepdims=True))
                dst = jnp.transpose(ds).astype(BF)
                pt = jnp.transpose(pf).astype(BF)
                dq = dq + dot(ds.astype(BF), masked(k, h))
                dk = dk + dot(dst, masked(q, h))
                dv = dv + dot(pt, masked(g, h))
            dqkv[:, at, lo : lo + LANES] = (dq * SCALING).astype(BF).reshape(feats, part, LANES)
            dqkv[:, at, width + lo : width + lo + LANES] = dk.astype(BF).reshape(feats, part, LANES)
            dqkv[:, at, 2 * width + lo : 2 * width + lo + LANES] = dv.astype(BF).reshape(
                feats, part, LANES
            )
        return 0

    lax.fori_loop(0, tiles, feat_bwd, 0)

    gg = jnp.zeros((1, width), F32)
    gb = jnp.zeros((1, width), F32)
    for b in range(2):
        at = slice(b * half, (b + 1) * half)
        d = dqkv[b * feats // 2 : (b + 1) * feats // 2, :, :].reshape(half, 3 * width)
        dh = dot_nt(d, wfq[...])
        nn, r = ln_parts(x1[at, :])
        gg = gg + jnp.sum(dh * nn, 0, keepdims=True)
        gb = gb + jnp.sum(dh, 0, keepdims=True)
        v = dx2[at, :] + ln_back(dh, nn, r, g2[...])
        dx1[at, :] = v
        g = dot_nt(v.astype(BF), wso[...]).astype(BF)
        for j in range(feats // 2):
            f = b * (feats // 2) + j
            for c in range(hpd):
                do_send[f * hpd + c] = g[j * count : (j + 1) * count, c * cl : (c + 1) * cl]
    vectors = [gg, gb] + vectors

    bits = len(order)

    def slot(pos):
        rel = 0
        for i, bit in enumerate(order):
            if (pos >> (bits - 1 - i)) & 1:
                rel |= 1 << bit
        ref, at = (g_keep, pos) if pos < n // 2 else (g_send, pos - n // 2)
        return ref, at, lax.bitwise_xor(me, rel)

    piece = width // n
    fpiece = hidden // n

    def spread(base):
        for pos in range(n):
            ref, at, d = slot(pos)
            src = pl.multiple_of(d * piece, piece)
            ref[at, base : base + piece, :] = wblk[pl.ds(src, piece), :]

    base = 0
    for b in range(hidden // width):
        tr[...] = flip(u[:, b * width : (b + 1) * width])
        wdn_scr[b * width : (b + 1) * width, :] = dot(tr[...], ct[...]).astype(BF)
    for pos in range(n):
        ref, at, d = slot(pos)
        src = pl.multiple_of(d * fpiece, fpiece)
        ref[at, base : base + fpiece, :] = wdn_scr[pl.ds(src, fpiece), :]
    base += fpiece
    tr[...] = flip(h3[...])
    for b in range(hidden // width):
        wblk[...] = dot(tr[...], dz[:, b * width : (b + 1) * width]).astype(BF)
        spread(base)
        base += piece
    tr[...] = flip(h2[...])
    for b in range(3):
        d = dqkv[:, :, b * width : (b + 1) * width].reshape(rows, width)
        wblk[...] = dot(tr[...], d).astype(BF)
        spread(base)
        base += piece
    tr[...] = flip(o2[...].reshape(rows, width))
    wblk[...] = dot(tr[...], dx2[...].astype(BF)).astype(BF)
    spread(base)
    base += piece
    tr[...] = flip(o1[...])
    wblk[...] = dot(tr[...], dx1[...].astype(BF)).astype(BF)
    spread(base)
    base += piece
    ubs = jnp.sum(ubg[...], 0, keepdims=True)
    vectors = vectors + [ubs[:, b * width : (b + 1) * width] for b in range(hidden // width)]
    vec = jnp.concatenate(vectors + [jnp.zeros((16 - len(vectors), width), F32)], 0).astype(BF)
    for pos in range(n):
        ref, at, _d = slot(pos)
        ref[at, base : base + 16, :] = vec


def solution(mesh):
    n = mesh.shape["samp"]
    groups = mesh.shape["grp"]
    bits = n.bit_length() - 1
    order = [b for b in (0, 1) if b < bits] + list(range(bits - 1, 1, -1))

    def flip_perm(bit):
        return [(d, d ^ (1 << bit)) for d in range(n)]

    def add(a, b):
        return (a.astype(F32) + b.astype(F32)).astype(BF)

    def halve(keep, send, perms):
        for i, perm in enumerate(perms):
            got = lax.ppermute(send, "samp", perm)
            both = add(keep, got)
            if i + 1 < len(perms):
                h = both.shape[0] // 2
                keep, send = both[:h], both[h:]
        return both

    def across(v):
        step = 1
        while step < groups:
            got = lax.ppermute(v, "grp", [(d, d ^ step) for d in range(groups)])
            v = add(v, got)
            step *= 2
        return v

    def body(
        tokens,
        segments,
        cotangent,
        first_gain,
        first_shift,
        sample_qkv,
        sample_out,
        second_gain,
        second_shift,
        feature_qkv,
        feature_out,
        third_gain,
        third_shift,
        up_weight,
        up_bias,
        down_weight,
        down_bias,
    ):
        count, feats, width = tokens.shape[1:]
        hidden = up_weight.shape[1]
        rows = count * feats
        hpd = n // feats
        hl = H // hpd
        cl = hl * HD
        total = n * count
        heads8 = 8
        me = lax.axis_index("samp")
        r = lax.rem(me, hpd)
        f = me // hpd
        r1, f1, me1 = (v.reshape(1).astype(jnp.int32) for v in (r, f, me))
        peers = [[q + hpd * k for k in range(feats)] for q in range(hpd)]
        g1, b1, g2, b2, g3, b3, ub, db = (
            v.reshape(1, -1)
            for v in (
                first_gain,
                first_shift,
                second_gain,
                second_shift,
                third_gain,
                third_shift,
                up_bias,
                down_bias,
            )
        )

        def shift(s):
            return [(d, d // hpd * hpd + (d % hpd + s) % hpd) for d in range(n)]

        (xt,) = call(
            pack_kernel,
            [((feats, count + PAD, width), BF)],
            [pltpu.VMEM((width // LANES, rows, LANES), F32)],
            tokens[0],
            segments,
        )
        mine = lax.all_to_all(xt, "samp", 0, 0, tiled=True, axis_index_groups=peers)
        xparts = [mine] + [lax.ppermute(mine, "samp", shift(s)) for s in range(1, hpd)]

        def columns(c):
            return lax.dynamic_slice_in_dim(sample_qkv, c * width + r * cl, cl, 1)

        wq = columns(0) * BF(SCALING)
        wk = columns(1)
        wv = columns(2)
        w3 = jnp.concatenate([columns(0), wk, wv], 1)

        o_send, xs, ot, lse, rank_row, rank_col, starts = call(
            functools.partial(fwd_kernel, hpd, hl),
            [
                ((n, count, cl), BF),
                ((total, width), BF),
                ((cl, total), BF),
                ((heads8, total), F32),
                ((8, total), F32),
                ((total, LANES), F32),
                ((8,), jnp.int32),
            ],
            [
                pltpu.VMEM((total, width), BF),
                pltpu.VMEM((total, LANES), F32),
                pltpu.VMEM((hl, LANES, total), BF),
                pltpu.VMEM((total, cl), BF),
                pltpu.VMEM((hl, HD + 16, total), BF),
                pltpu.VMEM((total, cl), BF),
                pltpu.VMEM((total, LANES), F32),
                pltpu.VMEM((8, total), F32),
                pltpu.VMEM((hl, HD + 16, TILE), F32),
                pltpu.VMEM((hl, 8, TILE), F32),
            ],
            r1,
            *xparts,
            g1,
            b1,
            wq.T,
            wk,
            wv.T,
            smem=(0,),
            smem_out=(6,),
        )
        o_recv = lax.all_to_all(o_send, "samp", 0, 0, tiled=True)

        pieces = hidden // n + width // n * (hidden // width + 5) + 16
        vm = pltpu.VMEM
        out, dx1, do_send, g_keep, g_send = call(
            functools.partial(rows_kernel, hpd, order),
            [
                ((count, feats, width), BF),
                ((rows, width), F32),
                ((n, count, cl), BF),
                ((n // 2, pieces, width), BF),
                ((n // 2, pieces, width), BF),
            ],
            [
                vm((width // LANES, rows, LANES), F32),
                vm((rows, width), BF),
                vm((rows, width), BF),
                vm((rows, width), F32),
                vm((rows, width), BF),
                vm((feats, count, 3 * width), BF),
                vm((feats, count, width), BF),
                vm((rows, width), F32),
                vm((rows, width), BF),
                vm((rows, hidden), BF),
                vm((rows, hidden), BF),
                vm((rows, width), F32),
                vm((feats, count, width), BF),
                vm((feats, count, 3 * width), BF),
                vm((count // 16, H, 16 * feats, 16 * feats), BF),
                vm((width, rows), BF),
                vm((width, width), BF),
                vm((8, hidden), F32),
                vm((hidden, width), BF),
            ],
            me1,
            o_recv,
            xt,
            cotangent[0],
            g2,
            b2,
            g3,
            b3,
            ub,
            db,
            sample_out,
            feature_qkv,
            feature_out,
            up_weight,
            down_weight,
            smem=(0,),
        )
        do_recv = lax.all_to_all(do_send, "samp", 0, 0, tiled=True)
        upper = across(halve(g_keep, g_send, [flip_perm(b) for b in order])[0])

        k_all, kt_all, v_all, qtz, qz, h1t = call(
            functools.partial(prep_kernel, hl),
            [
                ((total, cl), BF),
                ((cl, total), BF),
                ((total, cl), BF),
                ((hl, LANES, total), BF),
                ((hl, total, LANES), BF),
                ((width, total), BF),
            ],
            [],
            xs,
            g1,
            b1,
            wq.T,
            wq,
            wk,
            wk.T,
            wv,
        )
        extra = 8 * (width // cl)
        res = call(
            functools.partial(bwd_kernel, hpd, hl),
            [((feats, count, width), BF)] * hpd
            + [((feats // 2, width // feats + extra, 3 * cl), BF)] * 2,
            [
                vm((total, cl), BF),
                vm((hl, LANES, total), BF),
                vm((hl, total, LANES), BF),
                vm((8, total), F32),
                vm((cl, total), F32),
                vm((total, 3 * cl), BF),
                vm((total, width), BF),
                vm((width, 3 * cl), BF),
                vm((total, LANES), F32),
                vm((8, total), F32),
                vm(((hl + 1) // 2, TILE, LANES), F32),
                vm(((hl + 1) // 2, TILE, LANES), F32),
            ],
            r1,
            f1,
            starts,
            do_recv,
            xs,
            k_all,
            kt_all,
            v_all,
            qtz,
            qz,
            h1t,
            w3,
            ot,
            lse,
            rank_row,
            rank_col,
            smem=(0, 1, 2),
        )
        dhs, (q_keep, q_send) = res[:hpd], res[hpd:]
        parts = [dhs[0]] + [lax.ppermute(dhs[s], "samp", shift(-s)) for s in range(1, hpd)]
        (dv,) = call(
            functools.partial(norm_kernel, hpd),
            [((feats, count, width), BF)],
            [],
            *parts,
            mine,
            g1,
        )
        dv = lax.all_to_all(dv, "samp", 0, 0, tiled=True, axis_index_groups=peers)
        (grad_tokens,) = call(
            final_kernel,
            [((count, feats, width), F32)],
            [vm((width // LANES, rows, LANES), F32)],
            dx1,
            dv,
        )

        step0 = hpd.bit_length() - 1
        lower = across(halve(q_keep, q_send, [flip_perm(b) for b in range(bits - 1, step0 - 1, -1)])[0])
        piece = width // n
        main = lower[: width // feats].reshape(hpd, piece, 3, cl)
        tail = lower[width // feats :]
        vecs = [tail[8 * c : 8 * c + 8, :cl] for c in range(width // cl)]
        vec = jnp.concatenate(vecs, 1)
        cols = jnp.zeros((piece, 3, hpd, cl), BF)
        for s in range(hpd):
            give = lax.dynamic_index_in_dim(main, lax.rem(r + s, hpd), 0, keepdims=False)
            if s:
                give = lax.ppermute(give, "samp", shift(s))
            src = lax.rem(r - s + hpd, hpd)
            cols = lax.dynamic_update_slice(cols, give[:, :, None], (0, 0, src, 0))
        grad_sample_qkv = cols.reshape(piece, 3 * width).astype(F32)
        vec_sum = vec.astype(F32)
        for s in range(1, hpd):
            vec_sum = vec_sum + lax.ppermute(vec, "samp", shift(s)).astype(F32)

        def own(v):
            return lax.dynamic_slice_in_dim(v, me * (v.shape[0] // n), v.shape[0] // n, 0)

        fpiece = hidden // n
        base = fpiece
        up32 = upper.astype(F32)
        grad_down = up32[:fpiece]

        def blocks(m):
            nonlocal base
            got = [up32[base + i * piece : base + (i + 1) * piece] for i in range(m)]
            base += m * piece
            return jnp.concatenate(got, 1)

        grad_up = blocks(hidden // width)
        grad_fqkv = blocks(3)
        grad_fout = blocks(1)
        grad_sout = blocks(1)
        vu = up32[base:]
        return (
            out[None],
            grad_tokens[None],
            own(vec_sum[0]),
            own(vec_sum[1]),
            grad_sample_qkv,
            grad_sout,
            own(vu[0]),
            own(vu[1]),
            grad_fqkv,
            grad_fout,
            own(vu[2]),
            own(vu[3]),
            grad_up,
            own(vu[5 : 5 + hidden // width].reshape(-1)),
            grad_down,
            own(vu[4]),
        )

    rep = P()
    data = P("grp", "samp", None, None)
    line = P("samp")
    flat = P("samp", None)
    in_specs = (data, P("grp", "samp"), data) + (rep,) * 14
    out_specs = (
        data,
        data,
        line,
        line,
        flat,
        flat,
        line,
        line,
        flat,
        flat,
        line,
        line,
        flat,
        line,
        flat,
        line,
    )
    return jax.shard_map(body, mesh=mesh, in_specs=in_specs, out_specs=out_specs, check_vma=False)
```

```python
import functools
import math

import jax
import jax.numpy as jnp
from jax import lax
from jax.experimental import pallas as pl
from jax.experimental.pallas import tpu as pltpu
from jax.sharding import PartitionSpec as P

H = 8
HD = 64
EPSILON = 1e-05
SCALING = 0.125
NEGATIVE = -1e30
BF = jnp.bfloat16
F32 = jnp.float32
TILE = 256
PB = 512
KB = 256
QB = 256
TQ = 256
TK = 256
LANES = 128
PAD = 8
GELU_C = math.sqrt(2.0 / math.pi)
GELU_A = 0.044715
VMEM_LIMIT = 60 * 1024 * 1024
CLASSES = 5


def dot(a, b):
    return jnp.dot(a, b, preferred_element_type=F32)


def dot_nt(a, b):
    return lax.dot_general(a, b, (((1,), (1,)), ((), ())), preferred_element_type=F32)


def dot_tn(a, b):
    return lax.dot_general(a, b, (((0,), (0,)), ((), ())), preferred_element_type=F32)


def ln_parts(v):
    c = v - jnp.mean(v, -1, keepdims=True)
    r = lax.rsqrt(jnp.mean(c * c, -1, keepdims=True) + EPSILON)
    return c * r, r


def ln_back(dh, n, r, g):
    e = dh * g
    return r * (e - jnp.mean(e, -1, keepdims=True) - n * jnp.mean(e * n, -1, keepdims=True))


def flip(v):
    return jnp.transpose(v)


def head_columns(w, r, cl, which):
    first = which * (w.shape[1] // 3) + r * cl
    return w[:, pl.ds(pl.multiple_of(first, LANES), cl)]


def lay(scr, v):
    for a in range(scr.shape[0]):
        scr[a] = v[:, a * LANES : (a + 1) * LANES]


def lift(scr):
    return jnp.concatenate([scr[a] for a in range(scr.shape[0])], -1)


def take(scr, first, count, step):
    return jnp.concatenate(
        [scr[a, pl.ds(first, count, stride=step), :] for a in range(scr.shape[0])], -1
    )


def place(scr, first, count, step, v):
    for a in range(scr.shape[0]):
        scr[a, pl.ds(first, count, stride=step), :] = v[:, a * LANES : (a + 1) * LANES]


def iota(shape, dim):
    return lax.broadcasted_iota(jnp.int32, shape, dim).astype(F32)


def call(fn, outs, scratch, *args, smem=(), smem_out=()):
    def spec(space):
        return pl.BlockSpec(memory_space=space)

    in_specs = [spec(pltpu.SMEM if i in smem else pltpu.VMEM) for i in range(len(args))]
    out_specs = [spec(pltpu.SMEM if i in smem_out else pltpu.VMEM) for i in range(len(outs))]
    return pl.pallas_call(
        fn,
        out_shape=[jax.ShapeDtypeStruct(*o) for o in outs],
        in_specs=in_specs,
        out_specs=out_specs,
        scratch_shapes=scratch,
        compiler_params=pltpu.CompilerParams(vmem_limit_bytes=VMEM_LIMIT),
        cost_estimate=pl.CostEstimate(flops=0, bytes_accessed=0, transcendentals=0),
    )(*args)


def pack_kernel(tok, seg, out, scr):
    count, feats, width = tok.shape
    lay(scr, tok[...].astype(F32).reshape(count * feats, width))
    row = seg[...].astype(F32)
    for f in range(feats):
        out[f, :count, :] = take(scr, f, count, feats).astype(BF)
        out[f, count:, :] = jnp.zeros((PAD, width), BF)
        out[f, count:, :count] = jnp.broadcast_to(row, (PAD, count)).astype(BF)


def codes(pos, starts):
    cls = jnp.zeros_like(pos)
    for st in starts:
        cls = cls + jnp.where(pos >= st, 1.0, 0.0)
    return jnp.where(cls >= CLASSES - 1, pos + CLASSES, cls)


def tile_range(start_ref, first, size, tile):
    last = first + size - 1
    lo = jnp.int32(0)
    hi = start_ref[1]
    for c in range(1, CLASSES - 1):
        st = start_ref[c]
        lo = jnp.where(first >= st, st, lo)
        hi = jnp.where(last >= st, start_ref[c + 1], hi)
    pad = start_ref[CLASSES - 1]
    lo = jnp.where(first >= pad, first, lo)
    hi = jnp.where(last >= pad, first + size, hi)
    return lo // tile, (hi + tile - 1) // tile


def permute_block(rank_row, first, rows, total):
    pos = iota((rows, LANES), 0) + first.astype(F32)
    parts = []
    for j in range(total // LANES):
        hit = rank_row[0:1, j * LANES : (j + 1) * LANES] == pos
        parts.append(jnp.where(hit, 1.0, 0.0).astype(BF))
    return jnp.concatenate(parts, -1)


def unpermute_block(rank_col, total):
    rows = rank_col.shape[0]
    parts = []
    for j in range(total // LANES):
        pos = iota((1, LANES), 1) + float(j * LANES)
        parts.append(jnp.where(rank_col == pos, 1.0, 0.0).astype(BF))
    return jnp.concatenate(parts, -1)


def fwd_kernel(hpd, hl, r_ref, *refs):
    xparts = refs[:hpd]
    (g1, b1, w_in) = refs[hpd : hpd + 3]
    (o_send, xs_out, ot_out, lse_out, rank_row, rank_col, start_ref) = refs[hpd + 3 : hpd + 10]
    (x_scr, seg_scr, qtz, k_scr, vt, o_scr, code_col, code_row, acc, top, s_scr) = refs[
        hpd + 10 : hpd + 21
    ]
    wqt, wvt = refs[hpd + 21 :]
    feats = xparts[0].shape[0]
    count = xparts[0].shape[1] - PAD
    total = x_scr.shape[0]
    cl = hl * HD
    r = r_ref[0]
    chunks = total // LANES
    wqt[...] = flip(head_columns(w_in, r, cl, 0)) * BF(SCALING)
    wvt[...] = flip(head_columns(w_in, r, cl, 2))

    for s in range(hpd):
        for k in range(feats):
            at = (s * feats + k) * count
            x_scr[at : at + count, :] = xparts[s][k, :count, :]
            row = xparts[s][k, count : count + PAD, :LANES].astype(F32)[0:1]
            col = jnp.transpose(jnp.broadcast_to(row, (LANES, LANES)))
            seg_scr[at : at + count, :] = col[:count, :]

    seg = seg_scr[...]
    cls = jnp.where(seg < 0.0, float(CLASSES - 1), seg)
    seg_scr[...] = cls * 8192.0 + iota((total, LANES), 0)
    key_rows = []
    for j in range(chunks):
        blk = seg_scr[j * LANES : (j + 1) * LANES, :]
        key_rows.append(jnp.transpose(blk)[0:8, :])

    def count_less(i, carry):
        blk = seg_scr[pl.ds(pl.multiple_of(i * 64, 64), 64), :]
        out = []
        for j in range(chunks):
            less = jnp.where(blk < key_rows[j][0:1], 1.0, 0.0)
            out.append(carry[j] + jnp.sum(less.reshape(8, 8, LANES), 0))
        return tuple(out)

    ranks = lax.fori_loop(
        0, total // 64, count_less, tuple(jnp.zeros((8, LANES), F32) for _ in range(chunks))
    )
    for j in range(chunks):
        row = jnp.sum(ranks[j], 0, keepdims=True)
        rank_row[:, j * LANES : (j + 1) * LANES] = jnp.broadcast_to(row, (8, LANES))
        rank_col[j * LANES : (j + 1) * LANES, :] = jnp.transpose(
            jnp.broadcast_to(row, (LANES, LANES))
        )
    starts = []
    keys = jnp.concatenate([k[0:1] for k in key_rows], 0)
    for c in range(1, CLASSES):
        st = jnp.sum(jnp.where(keys < c * 8192.0, 1.0, 0.0))
        starts.append(st)
        start_ref[c] = st.astype(jnp.int32)
    start_ref[0] = jnp.int32(0)
    for c in range(CLASSES, 8):
        start_ref[c] = jnp.int32(total)
    code_col[...] = codes(iota((total, LANES), 0), starts)
    code_row[...] = codes(iota((8, total), 1), starts)

    qtz[...] = jnp.zeros_like(qtz)
    ones = jnp.where(iota((16, total), 0) == 0.0, 1.0, 0.0).astype(BF)
    for h in range(hl):
        vt[h, HD:, :] = ones

    def project(b, _):
        at = pl.multiple_of(b * PB, PB)
        block = dot(permute_block(rank_row, at, PB, total), x_scr[...])
        xs_out[pl.ds(at, PB), :] = block.astype(BF)
        n, _r = ln_parts(block)
        h1 = (n * g1[...] + b1[...]).astype(BF)
        qt = dot_nt(wqt[...], h1).astype(BF)
        k_scr[pl.ds(at, PB), :] = dot(h1, head_columns(w_in, r, cl, 1)).astype(BF)
        vv = dot_nt(wvt[...], h1).astype(BF)
        for h in range(hl):
            sub = (h % 2) * HD
            qtz[h, sub : sub + HD, pl.ds(at, PB)] = qt[h * HD : (h + 1) * HD]
            vt[h, :HD, pl.ds(at, PB)] = vv[h * HD : (h + 1) * HD]
        return 0

    lax.fori_loop(0, total // PB, project, 0)

    def attend(b, _):
        at = pl.multiple_of(b * TQ, TQ)
        t0, t1 = tile_range(start_ref, at, TQ, TK)
        acc[...] = jnp.zeros_like(acc)
        top[...] = jnp.full_like(top, NEGATIVE)
        crow = code_row[0:1, pl.ds(at, TQ)]

        def score(t, _):
            kt = pl.multiple_of(t * TK, TK)
            ccol = code_col[pl.ds(kt, TK), :]
            ccol = jnp.concatenate([ccol] * (TQ // LANES), -1)
            seen = ccol == crow
            for h in range(hl):
                pair = (h // 2) * LANES
                s = dot(k_scr[pl.ds(kt, TK), pair : pair + LANES], qtz[h, :, pl.ds(at, TQ)])
                s = jnp.where(seen, s, NEGATIVE)
                s_scr[h, pl.ds(kt, TK), :] = s
                top[h] = jnp.maximum(top[h], jnp.max(s.reshape(TK // 8, 8, TQ), 0))
            return 0

        lax.fori_loop(t0, t1, score, 0)
        for h in range(hl):
            top[h] = jnp.broadcast_to(jnp.max(top[h], 0, keepdims=True), (8, TQ))

        def mix(t, _):
            kt = pl.multiple_of(t * TK, TK)
            for h in range(hl):
                p = jnp.exp(s_scr[h, pl.ds(kt, TK), :] - top[h, 0:1, :]).astype(BF)
                acc[h] += dot(vt[h, :, pl.ds(kt, TK)], p)
            return 0

        lax.fori_loop(t0, t1, mix, 0)
        outs = []
        for h in range(hl):
            total_h = acc[h, HD : HD + 1, :]
            outs.append(acc[h, :HD, :] / total_h)
            lse_out[h : h + 1, pl.ds(at, TQ)] = top[h, 0:1, :] + jnp.log(total_h)
        ot = jnp.concatenate(outs, 0)
        ot_out[:, pl.ds(at, TQ)] = ot.astype(BF)
        o_scr[pl.ds(at, TQ), :] = jnp.transpose(ot).astype(BF)
        return 0

    lax.fori_loop(0, total // TQ, attend, 0)

    group = feats // 2
    for blk in range(total // (group * count)):
        at = blk * group * count
        hot = unpermute_block(rank_col[at : at + group * count, :], total)
        o = dot(hot, o_scr[...]).astype(BF)
        for j in range(group):
            s, k = divmod(blk * group + j, feats)
            dest = k * hpd + lax.rem(r - s + hpd, hpd)
            o_send[dest] = o[j * count : (j + 1) * count]


def prep_kernel(
    hl,
    r_ref,
    xs,
    g1,
    b1,
    w_in,
    k_out,
    v_out,
    kt_out,
    qtz,
    nt,
    wqt,
    wkt,
):
    total = xs.shape[0]
    cl = hl * HD
    r = r_ref[0]
    wqt[...] = flip(head_columns(w_in, r, cl, 0)) * BF(SCALING)
    wkt[...] = flip(head_columns(w_in, r, cl, 1))
    qtz[...] = jnp.zeros_like(qtz)

    def project(b, _):
        at = pl.multiple_of(b * PB, PB)
        n, _r = ln_parts(xs[pl.ds(at, PB), :].astype(F32))
        h1 = (n * g1[...] + b1[...]).astype(BF)
        nt[:, pl.ds(at, PB)] = jnp.transpose(n.astype(BF))
        qt = dot_nt(wqt[...], h1).astype(BF)
        k_out[pl.ds(at, PB), :] = dot(h1, head_columns(w_in, r, cl, 1)).astype(BF)
        v_out[pl.ds(at, PB), :] = dot(h1, head_columns(w_in, r, cl, 2)).astype(BF)
        kt_out[:, pl.ds(at, PB)] = dot_nt(wkt[...], h1).astype(BF)
        for h in range(hl):
            sub = (h % 2) * HD
            qtz[h, sub : sub + HD, pl.ds(at, PB)] = qt[h * HD : (h + 1) * HD]
        return 0

    lax.fori_loop(0, total // PB, project, 0)


def add_all(terms):
    total = terms[0].astype(F32)
    for term in terms[1:]:
        total = total + term.astype(F32)
    return total.astype(BF)


def bwd_kernel(
    hpd,
    hl,
    r_ref,
    start_ref,
    do_recv,
    k_in,
    v_in,
    kt_in,
    qtz,
    ot,
    lse,
    rank_row,
    dt_out,
    do_scr,
    dotz,
    dots,
    code_col,
    code_row,
    dq_acc,
    dk_acc,
    dv_acc,
    p_scr,
    ds_scr,
    pairs,
):
    feats = do_recv.shape[0] // hpd
    count = do_recv.shape[1]
    total = do_scr.shape[0]
    cl = hl * HD
    r = r_ref[0]

    for s in range(hpd):
        for k in range(feats):
            at = (s * feats + k) * count
            do_scr[at : at + count, :] = do_recv[k * hpd + lax.rem(r - s + hpd, hpd)]
    starts = [start_ref[c].astype(F32) for c in range(1, CLASSES)]
    code_col[...] = codes(iota((total, LANES), 0), starts)
    code_row[...] = codes(iota((8, total), 1), starts)
    dotz[...] = jnp.zeros_like(dotz)

    def arrange(b, _):
        at = pl.multiple_of(b * PB, PB)
        block = jnp.transpose(dot(permute_block(rank_row, at, PB, total), do_scr[...]))
        prod = block * ot[:, pl.ds(at, PB)].astype(F32)
        for h in range(hl):
            sub = (h % 2) * HD
            rows = slice(h * HD, (h + 1) * HD)
            dotz[h, sub : sub + HD, pl.ds(at, PB)] = block[rows].astype(BF)
            dots[h : h + 1, pl.ds(at, PB)] = jnp.sum(prod[rows], 0, keepdims=True)
        return 0

    lax.fori_loop(0, total // PB, arrange, 0)
    dq_acc[...] = jnp.zeros_like(dq_acc)
    dk_acc[...] = jnp.zeros_like(dk_acc)
    dv_acc[...] = jnp.zeros_like(dv_acc)

    def list_keys(b, filled):
        t0, t1 = tile_range(start_ref, b * KB, KB, QB)

        def put(t, i):
            pairs[i] = b * 4096 + t
            return i + 1

        return lax.fori_loop(t0, t1, put, filled)

    filled = lax.fori_loop(0, total // KB, list_keys, jnp.int32(0))

    def places(i):
        b, t = pairs[i] // 4096, lax.rem(pairs[i], 4096)
        return pl.ds(pl.multiple_of(b * KB, KB), KB), pl.ds(pl.multiple_of(t * QB, QB), QB)

    def scores(i):
        kt, at = places(i)
        ccol = code_col[kt, :]
        seen = jnp.concatenate([ccol] * (QB // LANES), -1) == code_row[0:1, at]
        for h in range(hl):
            cols = slice(h // 2 * LANES, (h // 2 + 1) * LANES)
            s = dot(k_in[kt, cols], qtz[h, :, at])
            p = jnp.where(seen, jnp.exp(s - lse[h : h + 1, at]), 0.0)
            dp = dot(v_in[kt, cols], dotz[h, :, at])
            p_scr[h] = p.astype(BF)
            ds_scr[h] = (p * (dp - dots[h : h + 1, at])).astype(BF)

    def collect(i):
        kt, at = places(i)
        for h in range(hl):
            rows = slice(h * HD, (h + 1) * HD)
            own = slice((h % 2) * HD, (h % 2 + 1) * HD)
            ds = ds_scr[h]
            dv_acc[rows, kt] += dot_nt(dotz[h, own, at], p_scr[h])
            dk_acc[rows, kt] += dot_nt(qtz[h, own, at], ds)
            dq_acc[rows, at] += dot(kt_in[rows, kt], ds)

    def step(i, _):
        scores(i)
        collect(i)
        return 0

    lax.fori_loop(0, filled, step, 0)
    dt_out[:cl, :] = (dq_acc[...] * SCALING).astype(BF)
    dt_out[cl : 2 * cl, :] = dk_acc[...].astype(BF)
    dt_out[2 * cl :, :] = dv_acc[...].astype(BF)


def dh_kernel(hpd, r_ref, dt, w_in, rank_col, *refs):
    dh_outs, dht = refs[: 2 * hpd], refs[2 * hpd]
    half, count, width = dh_outs[0].shape
    feats = 2 * half
    total = dt.shape[1]
    cl = dt.shape[0] // 3
    w3 = jnp.concatenate([head_columns(w_in, r_ref[0], cl, j) for j in range(3)], 1)
    for b in range(total // PB):
        at = slice(b * PB, (b + 1) * PB)
        dht[:, at] = dot(w3, dt[:, at]).astype(BF)
    group = feats // 2
    for blk in range(total // (group * count)):
        at = blk * group * count
        hot = unpermute_block(rank_col[at : at + group * count, :], total)
        o = dot_nt(hot, dht[...]).astype(BF)
        for j in range(group):
            s, k = divmod(blk * group + j, feats)
            dh_outs[2 * s + k // half][k % half] = o[j * count : (j + 1) * count]


SUB = 16


def q_rows(cl, width):
    return SUB * (-(-6 * cl // width)) + SUB


def dw_kernel(r_ref, x_ref, dt, nt, w_in, g1, b1, q_keep, q_send, m_scr, dw_scr):
    x = x_ref[0]
    width, total = nt.shape
    cols = dt.shape[0]
    cl = cols // 3
    feats = q_keep.shape[0]
    for c in range(3):
        rows = slice(c * cl, (c + 1) * cl)
        m_scr[:, rows] = dot_nt(nt[...], dt[rows, :])
    ones = jnp.ones((8, total), BF)
    sums_row = dot_nt(ones, dt[...])[0:1]
    gcol = jnp.transpose(jnp.broadcast_to(g1[...], (LANES, width)))
    bcol = jnp.transpose(jnp.broadcast_to(b1[...], (LANES, width)))
    gg = jnp.zeros((width, LANES), F32)
    gb = jnp.zeros((width, LANES), F32)
    for j in range(cols // LANES):
        lanes = slice(j * LANES, (j + 1) * LANES)
        first = (j * LANES // cl) * width + r_ref[0] * cl + j * LANES % cl
        w = w_in[:, pl.ds(pl.multiple_of(first, LANES), LANES)].astype(F32)
        m = m_scr[:, lanes]
        gg = gg + w * m
        gb = gb + w * sums_row[:, lanes]
        dw_scr[:, lanes] = (m * gcol + bcol * sums_row[:, lanes]).astype(BF)
    gg = jnp.sum(jnp.transpose(gg), 0, keepdims=True)
    gb = jnp.sum(jnp.transpose(gb), 0, keepdims=True)
    vec = jnp.concatenate([gg, gb, jnp.zeros((SUB - 2, width), F32)], 0).astype(BF)
    per = width // cl
    last = q_keep.shape[1] - SUB
    for e in range(feats):
        for ref, side in ((q_keep, x), (q_send, 1 - x)):
            for s in range(6):
                j, b = divmod(s, 2)
                src = pl.multiple_of((e * 4 + b) * SUB + side * 2 * SUB, SUB)
                to = (s // per) * SUB
                ref[e, to : to + SUB, (s % per) * cl : (s % per + 1) * cl] = dw_scr[
                    pl.ds(src, SUB), j * cl : (j + 1) * cl
                ]
            used = 6 % per
            if used:
                ref[e, last - SUB : last, used * cl :] = jnp.zeros((SUB, width - used * cl), BF)
            ref[e, last:, :] = vec


def gather_kernel(hpd, r_ref, x_ref, *refs):
    same, other = refs[:hpd], refs[hpd : 2 * hpd]
    sums, got = refs[2 * hpd : 2 * hpd + 2]
    out, vec, down, up, fqkv, fout, sout, vectors = refs[2 * hpd + 2 :]
    piece = out.shape[0]
    rows, width = same[0].shape
    cl = width // hpd
    r, x = r_ref[0], x_ref[0]
    blocks = piece // SUB
    first = lax.rem(r * blocks, 2)
    from_same = r * blocks // 2 == x
    for s in range(hpd):
        owner = lax.rem(r - s + hpd, hpd)
        for j in range(3):
            lo = 2 * j // hpd * SUB
            to = pl.ds(pl.multiple_of(j * width + owner * cl, LANES), cl)
            for b in range(blocks):
                col = pl.multiple_of((2 * j % hpd + first + b) * cl, LANES)
                at = (slice(lo, lo + SUB), pl.ds(col, cl))
                picked = jnp.where(from_same, same[s][at].astype(F32), other[s][at].astype(F32))
                out[b * SUB : (b + 1) * SUB, to] = picked
    total = same[0][rows - SUB : rows, :].astype(F32)
    for s in range(1, hpd):
        total = total + same[s][rows - SUB : rows, :].astype(F32)
    vec[...] = total[:8]

    def both(first, size):
        at = slice(first, first + size)
        return sums[at, :].astype(F32) + got[at, :].astype(F32)

    down[...] = both(0, down.shape[0])
    base = down.shape[0]
    for ref in (up, fqkv, fout, sout):
        for b in range(ref.shape[1] // width):
            ref[:, b * width : (b + 1) * width] = both(base, piece)
            base += piece
    vectors[...] = both(base, vectors.shape[0])


def norm_kernel(hpd, *refs):
    parts = refs[: 2 * hpd]
    x, g1, q_keep, q_got, out = refs[2 * hpd :]
    half, count, _w = parts[0].shape
    feats = 2 * half
    for k in range(feats):
        dh = parts[k // half][k % half].astype(F32)
        for s in range(1, hpd):
            dh = dh + parts[2 * s + k // half][k % half].astype(F32)
        n, r = ln_parts(x[k, :count, :].astype(F32))
        out[k, :count, :] = ln_back(dh, n, r, g1[...]).astype(BF)
        out[k, count:, :] = add_all((q_keep[k], q_got[k]))


def final_kernel(dx1, both, out, q_sum, scr):
    feats = both.shape[0]
    count, _f, width = out.shape
    q_sum[...] = add_all([both[k, count:, :] for k in range(feats)])
    for f in range(feats):
        val = dx1[f * count : (f + 1) * count, :] + both[f, :count, :].astype(F32)
        place(scr, f, count, feats, val)
    out[...] = lift(scr).reshape(count, feats, width)


def rows_kernel(
    hpd,
    o_recv,
    xt,
    cot,
    g2,
    b2,
    g3,
    b3,
    ub,
    db,
    wso,
    wfq,
    wfo,
    wup,
    wdn,
    out,
    dx1,
    do_send,
    sums,
    wide,
    ct,
    o1,
    x1,
    h2,
    qkv,
    o2,
    x2,
    h3,
    u,
    dz,
    dx2,
    do2,
    dqkv,
    pscr,
    tr,
    wblk,
    ubg,
    wdn_scr,
):
    feats = xt.shape[0]
    count = xt.shape[1] - PAD
    width = xt.shape[2]
    rows = feats * count
    hidden = wup.shape[1]
    n = o_recv.shape[0]
    cl = o_recv.shape[2]
    half = rows // 2
    lane = iota((1, LANES), 1)
    part = 16
    tiles = count // part
    size = feats * part

    lay(wide, cot[...].astype(F32).reshape(rows, width))
    for f in range(feats):
        ct[f * count : (f + 1) * count, :] = take(wide, f, count, feats).astype(BF)
        for c in range(hpd):
            o1[f * count : (f + 1) * count, c * cl : (c + 1) * cl] = o_recv[f * hpd + c]

    for b in range(2):
        at = slice(b * half, (b + 1) * half)
        x = xt[b * feats // 2 : (b + 1) * feats // 2, :count, :].astype(F32).reshape(half, width)
        v = x + dot(o1[at, :], wso[...])
        x1[at, :] = v
        nn, _r = ln_parts(v)
        h2[at, :] = (nn * g2[...] + b2[...]).astype(BF)

    qkv3 = qkv

    def qkv_step(c, _):
        cols = pl.ds(pl.multiple_of(c * TILE, TILE), TILE)
        scale = jnp.where(c < width // TILE, SCALING, 1.0)
        y = dot(h2[...], wfq[:, cols])
        qkv3[:, :, cols] = (y * scale).astype(BF).reshape(feats, count, TILE)
        return 0

    lax.fori_loop(0, 3 * width // TILE, qkv_step, 0)

    ri = lax.broadcasted_iota(jnp.int32, (2 * size, size), 0)
    ci = lax.broadcasted_iota(jnp.int32, (2 * size, size), 1)
    same = lax.rem(ri, part) == lax.rem(ci, part)
    low_lane = jnp.where(iota((1, LANES), 1) < HD, 1.0, 0.0).astype(BF)
    high_lane = jnp.where(iota((1, LANES), 1) < HD, 0.0, 1.0).astype(BF)

    def tile_of(ref, at, lo):
        return ref[:, at, lo : lo + LANES].reshape(size, LANES)

    def by_head(v):
        return jnp.concatenate([v * low_lane, v * high_lane], 0)

    def by_head_t(v):
        vt = jnp.transpose(v)
        zero = jnp.zeros((HD, size), BF)
        return jnp.concatenate(
            [jnp.concatenate([vt[:HD], zero], 0), jnp.concatenate([zero, vt[HD:]], 0)], 1
        )

    def side(v):
        return jnp.concatenate([v[:size], v[size:]], 1)

    def per_head(v, fn):
        return jnp.concatenate(
            [jnp.broadcast_to(fn(v[i * size : (i + 1) * size]), (size, size)) for i in (0, 1)], 0
        )

    def feat_fwd(t, _):
        at = pl.ds(pl.multiple_of(t * part, part), part)
        for p2 in range(H // 2):
            lo = p2 * LANES
            q = tile_of(qkv3, at, lo)
            k = tile_of(qkv3, at, width + lo)
            v = tile_of(qkv3, at, 2 * width + lo)
            s = jnp.where(same, dot_nt(by_head(k), q), NEGATIVE)
            e = jnp.exp(s - per_head(s, lambda w: jnp.max(w, 0, keepdims=True)))
            p = (e * per_head(e, lambda w: 1.0 / jnp.sum(w, 0, keepdims=True))).astype(BF)
            pscr[t, p2] = p
            ot = dot(by_head_t(v), p)
            o2[:, at, lo : lo + LANES] = jnp.transpose(ot).astype(BF).reshape(feats, part, LANES)
        return 0

    lax.fori_loop(0, tiles, feat_fwd, 0, unroll=True)

    for b in range(2):
        at = slice(b * half, (b + 1) * half)
        o = o2[b * feats // 2 : (b + 1) * feats // 2, :, :].reshape(half, width)
        v = x1[at, :] + dot(o, wfo[...])
        x2[at, :] = v
        nn, _r = ln_parts(v)
        h3[at, :] = (nn * g3[...] + b3[...]).astype(BF)

    def ffn(c, _):
        cols = pl.ds(pl.multiple_of(c * TILE, TILE), TILE)
        total = jnp.zeros((8, TILE), F32)
        for b in range(2):
            at = slice(b * half, (b + 1) * half)
            z = dot(h3[at, :], wup[:, cols]) + ub[0:1, cols]
            w = GELU_C * GELU_A * (z * z) + GELU_C
            cdf = 0.5 * jnp.tanh(z * w) + 0.5
            g = z * cdf
            u[at, cols] = g.astype(BF)
            slope = cdf + g * (1.0 - cdf) * (6.0 * w - 4.0 * GELU_C)
            d = dot_nt(ct[at, :], wdn[cols, :]) * slope
            dz[at, cols] = d.astype(BF)
            total = total + jnp.sum(d.reshape(half // 8, 8, TILE), 0)
        ubg[:, cols] = total
        return 0

    lax.fori_loop(0, hidden // TILE, ffn, 0)

    vectors = []
    gg = jnp.zeros((1, width), F32)
    gb = jnp.zeros((1, width), F32)
    gd = jnp.zeros((1, width), F32)
    for b in range(2):
        at = slice(b * half, (b + 1) * half)
        y = x2[at, :] + dot(u[at, :], wdn[...]) + db[...]
        for j in range(feats // 2):
            f = b * (feats // 2) + j
            place(wide, f, count, feats, y[j * count : (j + 1) * count])
        dh = dot_nt(dz[at, :], wup[...])
        nn, r = ln_parts(x2[at, :])
        c = ct[at, :].astype(F32)
        gg = gg + jnp.sum(dh * nn, 0, keepdims=True)
        gb = gb + jnp.sum(dh, 0, keepdims=True)
        gd = gd + jnp.sum(c, 0, keepdims=True)
        v = c + ln_back(dh, nn, r, g3[...])
        dx2[at, :] = v
        do2[b * feats // 2 : (b + 1) * feats // 2, :, :] = (
            dot_nt(v.astype(BF), wfo[...]).astype(BF).reshape(feats // 2, count, width)
        )
    out[...] = lift(wide).reshape(count, feats, width).astype(BF)
    vectors = [gg, gb, gd]

    def feat_bwd(t, _):
        at = pl.ds(pl.multiple_of(t * part, part), part)
        for p2 in range(H // 2):
            lo = p2 * LANES
            q = tile_of(qkv3, at, lo)
            k = tile_of(qkv3, at, width + lo)
            v = tile_of(qkv3, at, 2 * width + lo)
            g = tile_of(do2, at, lo)
            p = pscr[t, p2]
            pf = p.astype(F32)
            dp = dot_nt(by_head(v), g)
            ds = pf * (dp - per_head(pf * dp, lambda w: jnp.sum(w, 0, keepdims=True)))
            ds = ds.astype(BF)
            dv = dot(side(p), by_head(g))
            dk = dot(side(ds), by_head(q))
            dq = jnp.transpose(dot(by_head_t(k), ds)) * SCALING
            for j, d in enumerate((dq, dk, dv)):
                dqkv[:, at, j * width + lo : j * width + lo + LANES] = d.astype(BF).reshape(
                    feats, part, LANES
                )
        return 0

    lax.fori_loop(0, tiles, feat_bwd, 0, unroll=True)

    gg = jnp.zeros((1, width), F32)
    gb = jnp.zeros((1, width), F32)
    for b in range(2):
        at = slice(b * half, (b + 1) * half)
        d = dqkv[b * feats // 2 : (b + 1) * feats // 2, :, :].reshape(half, 3 * width)
        dh = dot_nt(d, wfq[...])
        nn, r = ln_parts(x1[at, :])
        gg = gg + jnp.sum(dh * nn, 0, keepdims=True)
        gb = gb + jnp.sum(dh, 0, keepdims=True)
        v = dx2[at, :] + ln_back(dh, nn, r, g2[...])
        dx1[at, :] = v
        g = dot_nt(v.astype(BF), wso[...]).astype(BF)
        for j in range(feats // 2):
            f = b * (feats // 2) + j
            for c in range(hpd):
                do_send[f * hpd + c] = g[j * count : (j + 1) * count, c * cl : (c + 1) * cl]
    vectors = [gg, gb] + vectors

    piece = width // n
    fpiece = hidden // n

    def spread(base):
        for d in range(n):
            sums[d, base : base + piece, :] = wblk[d * piece : (d + 1) * piece, :]

    base = 0
    for b in range(hidden // width):
        tr[...] = flip(u[:, b * width : (b + 1) * width])
        wdn_scr[b * width : (b + 1) * width, :] = dot(tr[...], ct[...]).astype(BF)
    for d in range(n):
        sums[d, base : base + fpiece, :] = wdn_scr[d * fpiece : (d + 1) * fpiece, :]
    base += fpiece
    tr[...] = flip(h3[...])
    for b in range(hidden // width):
        wblk[...] = dot(tr[...], dz[:, b * width : (b + 1) * width]).astype(BF)
        spread(base)
        base += piece
    tr[...] = flip(h2[...])
    for b in range(3):
        d = dqkv[:, :, b * width : (b + 1) * width].reshape(rows, width)
        wblk[...] = dot(tr[...], d).astype(BF)
        spread(base)
        base += piece
    tr[...] = flip(o2[...].reshape(rows, width))
    wblk[...] = dot(tr[...], dx2[...].astype(BF)).astype(BF)
    spread(base)
    base += piece
    tr[...] = flip(o1[...])
    wblk[...] = dot(tr[...], dx1[...].astype(BF)).astype(BF)
    spread(base)
    base += piece
    ubs = jnp.sum(ubg[...], 0, keepdims=True)
    vectors = vectors + [ubs[:, b * width : (b + 1) * width] for b in range(hidden // width)]
    vec = jnp.concatenate(vectors + [jnp.zeros((16 - len(vectors), width), F32)], 0).astype(BF)
    for d in range(n):
        sums[d, base : base + 16, :] = vec


def solution(mesh):
    n = mesh.shape["samp"]
    groups = mesh.shape["grp"]
    gbits = groups.bit_length() - 1
    tie = lax.optimization_barrier

    def swap_grp(v, bit=0):
        return lax.ppermute(v, "grp", [(d, d ^ (1 << bit)) for d in range(groups)])

    def rest_of_grp(v):
        for bit in range(1, gbits):
            v = (v.astype(F32) + swap_grp(v, bit).astype(F32)).astype(BF)
        return v

    def body(
        tokens,
        segments,
        cotangent,
        first_gain,
        first_shift,
        sample_qkv,
        sample_out,
        second_gain,
        second_shift,
        feature_qkv,
        feature_out,
        third_gain,
        third_shift,
        up_weight,
        up_bias,
        down_weight,
        down_bias,
    ):
        count, feats, width = tokens.shape[1:]
        hidden = up_weight.shape[1]
        rows = count * feats
        hpd = n // feats
        hl = H // hpd
        cl = hl * HD
        total = n * count
        heads8 = 8
        me = lax.axis_index("samp")
        r = lax.rem(me, hpd)
        x = lax.rem(lax.axis_index("grp"), 2)
        r1, x1 = (v.reshape(1).astype(jnp.int32) for v in (r, x))
        peers = [[q + hpd * k for k in range(feats)] for q in range(hpd)]
        g1, b1, g2, b2, g3, b3, ub, db = (
            v.reshape(1, -1)
            for v in (
                first_gain,
                first_shift,
                second_gain,
                second_shift,
                third_gain,
                third_shift,
                up_bias,
                down_bias,
            )
        )

        def shift(s):
            return [(d, d // hpd * hpd + (d % hpd + s) % hpd) for d in range(n)]

        (xt,) = call(
            pack_kernel,
            [((feats, count + PAD, width), BF)],
            [pltpu.VMEM((width // LANES, rows, LANES), F32)],
            tokens[0],
            segments,
        )
        mine = lax.all_to_all(xt, "samp", 0, 0, tiled=True, axis_index_groups=peers)
        xparts = [mine] + [lax.ppermute(mine, "samp", shift(s)) for s in range(1, hpd)]

        o_send, xs, ot, lse, rank_row, rank_col, starts = call(
            functools.partial(fwd_kernel, hpd, hl),
            [
                ((n, count, cl), BF),
                ((total, width), BF),
                ((cl, total), BF),
                ((heads8, total), F32),
                ((8, total), F32),
                ((total, LANES), F32),
                ((8,), jnp.int32),
            ],
            [
                pltpu.VMEM((total, width), BF),
                pltpu.VMEM((total, LANES), F32),
                pltpu.VMEM((hl, LANES, total), BF),
                pltpu.VMEM((total, cl), BF),
                pltpu.VMEM((hl, HD + 16, total), BF),
                pltpu.VMEM((total, cl), BF),
                pltpu.VMEM((total, LANES), F32),
                pltpu.VMEM((8, total), F32),
                pltpu.VMEM((hl, HD + 16, TQ), F32),
                pltpu.VMEM((hl, 8, TQ), F32),
                pltpu.VMEM((hl, total, TQ), F32),
                pltpu.VMEM((cl, width), BF),
                pltpu.VMEM((cl, width), BF),
            ],
            r1,
            *xparts,
            g1,
            b1,
            sample_qkv,
            smem=(0,),
            smem_out=(6,),
        )
        o_recv = lax.all_to_all(o_send, "samp", 0, 0, tiled=True)

        piece = width // n
        fpiece = hidden // n
        pieces = fpiece + piece * (hidden // width + 5) + 16
        vm = pltpu.VMEM
        out, dx1, do_send, sums = call(
            functools.partial(rows_kernel, hpd),
            [
                ((count, feats, width), BF),
                ((rows, width), F32),
                ((n, count, cl), BF),
                ((n, pieces, width), BF),
            ],
            [
                vm((width // LANES, rows, LANES), F32),
                vm((rows, width), BF),
                vm((rows, width), BF),
                vm((rows, width), F32),
                vm((rows, width), BF),
                vm((feats, count, 3 * width), BF),
                vm((feats, count, width), BF),
                vm((rows, width), F32),
                vm((rows, width), BF),
                vm((rows, hidden), BF),
                vm((rows, hidden), BF),
                vm((rows, width), F32),
                vm((feats, count, width), BF),
                vm((feats, count, 3 * width), BF),
                vm((count // 16, H // 2, 32 * feats, 16 * feats), BF),
                vm((width, rows), BF),
                vm((width, width), BF),
                vm((8, hidden), F32),
                vm((hidden, width), BF),
            ],
            o_recv,
            xt,
            cotangent[0],
            g2,
            b2,
            g3,
            b3,
            ub,
            db,
            sample_out,
            feature_qkv,
            feature_out,
            up_weight,
            down_weight,
        )
        sums = lax.psum_scatter(sums, "samp", scatter_dimension=0, tiled=True)[0]
        do_recv = lax.all_to_all(do_send, "samp", 0, 0, tiled=True)

        qr = q_rows(cl, width)
        k_all, v_all, kt_all, qtz, nt = call(
            functools.partial(prep_kernel, hl),
            [
                ((total, cl), BF),
                ((total, cl), BF),
                ((cl, total), BF),
                ((hl, LANES, total), BF),
                ((width, total), BF),
            ],
            [vm((cl, width), BF), vm((cl, width), BF)],
            r1,
            xs,
            g1,
            b1,
            sample_qkv,
            smem=(0,),
        )
        (dt,) = call(
            functools.partial(bwd_kernel, hpd, hl),
            [((3 * cl, total), BF)],
            [
                vm((total, cl), BF),
                vm((hl, LANES, total), BF),
                vm((8, total), F32),
                vm((total, LANES), F32),
                vm((8, total), F32),
                vm((cl, total), F32),
                vm((cl, total), F32),
                vm((cl, total), F32),
                vm((hl, KB, QB), BF),
                vm((hl, KB, QB), BF),
                pltpu.SMEM(((total // KB) * (total // QB),), jnp.int32),
            ],
            r1,
            starts,
            do_recv,
            k_all,
            v_all,
            kt_all,
            qtz,
            ot,
            lse,
            rank_row,
            smem=(0, 1),
        )
        q_keep, q_send = call(
            dw_kernel,
            [((feats, qr, width), BF)] * 2,
            [vm((width, 3 * cl), F32), vm((width, 3 * cl), BF)],
            r1,
            x1,
            dt,
            nt,
            sample_qkv,
            g1,
            b1,
            smem=(0, 1),
        )
        dt, _ = tie((dt, q_send))
        dhs = call(
            functools.partial(dh_kernel, hpd),
            [((feats // 2, count, width), BF)] * (2 * hpd),
            [vm((width, total), BF)],
            r1,
            dt,
            sample_qkv,
            rank_col,
            smem=(0,),
        )
        parts = list(dhs[:2])
        for s in range(1, hpd):
            parts += [lax.ppermute(v, "samp", shift(-s)) for v in dhs[2 * s : 2 * s + 2]]
        (both,) = call(
            functools.partial(norm_kernel, hpd),
            [((feats, count + qr, width), BF)],
            [],
            *parts,
            mine,
            g1,
            q_keep,
            swap_grp(q_send),
        )
        both_send = both
        both = lax.all_to_all(both, "samp", 0, 0, tiled=True, axis_index_groups=peers)
        dx1, _ = tie((dx1, both_send))
        sums, _ = tie((sums, both_send))
        sums = rest_of_grp(sums)
        sums_got = swap_grp(sums)
        grad_tokens, q_sum = call(
            final_kernel,
            [((count, feats, width), F32), ((qr, width), BF)],
            [vm((width // LANES, rows, LANES), F32)],
            dx1,
            both,
        )
        q_sum = rest_of_grp(q_sum)

        def from_peer(s, other):
            if not s and not other:
                return q_sum
            pairs = [
                (g * n + d, (g ^ other) * n + e) for g in range(groups) for d, e in shift(s)
            ]
            return lax.ppermute(q_sum, ("grp", "samp"), pairs)

        peers_same = [from_peer(s, 0) for s in range(hpd)]
        peers_other = [from_peer(s, 1) for s in range(hpd)]
        grad_sample_qkv, vec_sum, grad_down, grad_up, grad_fqkv, grad_fout, grad_sout, vu = call(
            functools.partial(gather_kernel, hpd),
            [
                ((piece, 3 * width), F32),
                ((8, width), F32),
                ((fpiece, width), F32),
                ((piece, hidden), F32),
                ((piece, 3 * width), F32),
                ((piece, width), F32),
                ((piece, width), F32),
                ((16, width), F32),
            ],
            [],
            r1,
            x1,
            *peers_same,
            *peers_other,
            sums,
            sums_got,
            smem=(0, 1),
        )

        def own(v):
            return lax.dynamic_slice_in_dim(v, me * (v.shape[0] // n), v.shape[0] // n, 0)

        def own_rows(v):
            return lax.dynamic_slice_in_dim(v, me * piece, piece, 1)

        five = own_rows(vu[:5])
        two = own_rows(vec_sum[:2])
        vectors = [five[i] for i in range(5)]
        vectors.append(own(vu[5 : 5 + hidden // width].reshape(-1)))
        return (
            out[None],
            grad_tokens[None],
            two[0],
            two[1],
            grad_sample_qkv,
            grad_sout,
            vectors[0],
            vectors[1],
            grad_fqkv,
            grad_fout,
            vectors[2],
            vectors[3],
            grad_up,
            vectors[5],
            grad_down,
            vectors[4],
        )

    rep = P()
    data = P("grp", "samp", None, None)
    line = P("samp")
    flat = P("samp", None)
    in_specs = (data, P("grp", "samp"), data) + (rep,) * 14
    out_specs = (
        data,
        data,
        line,
        line,
        flat,
        flat,
        line,
        line,
        flat,
        flat,
        line,
        line,
        flat,
        line,
        flat,
        line,
    )
    return jax.shard_map(body, mesh=mesh, in_specs=in_specs, out_specs=out_specs, check_vma=False)
```

```python
import functools
import math

import jax
import jax.numpy as jnp
from jax import lax
from jax.experimental import pallas as pl
from jax.experimental.pallas import tpu as pltpu
from jax.sharding import PartitionSpec as P

H = 8
HD = 64
EPSILON = 1e-05
SCALING = 0.125
NEGATIVE = -1e30
BF = jnp.bfloat16
F32 = jnp.float32
TILE = 256
FT = 512
PB = 512
KB = 256
QB = 256
TQ = 256
TK = 256
LANES = 128
PAD = 8
GELU_C = math.sqrt(2.0 / math.pi)
GELU_A = 0.044715
MIB = 1024 * 1024
CLASSES = 5


def dot(a, b):
    return jnp.dot(a, b, preferred_element_type=F32)


def dot_nt(a, b):
    return lax.dot_general(a, b, (((1,), (1,)), ((), ())), preferred_element_type=F32)


def dot_tn(a, b):
    return lax.dot_general(a, b, (((0,), (0,)), ((), ())), preferred_element_type=F32)


def ln_parts(v):
    c = v - jnp.mean(v, -1, keepdims=True)
    r = lax.rsqrt(jnp.mean(c * c, -1, keepdims=True) + EPSILON)
    return c * r, r


def ln_back(dh, n, r, g):
    e = dh * g
    return r * (e - jnp.mean(e, -1, keepdims=True) - n * jnp.mean(e * n, -1, keepdims=True))


def flip(v):
    return jnp.transpose(v)


def head_columns(w, r, cl, which):
    first = which * (w.shape[1] // 3) + r * cl
    return w[:, pl.ds(pl.multiple_of(first, LANES), cl)]


def lay(scr, v):
    for a in range(scr.shape[0]):
        scr[a] = v[:, a * LANES : (a + 1) * LANES]


def lift(scr):
    return jnp.concatenate([scr[a] for a in range(scr.shape[0])], -1)


def take(scr, first, count, step):
    return jnp.concatenate(
        [scr[a, pl.ds(first, count, stride=step), :] for a in range(scr.shape[0])], -1
    )


def place(scr, first, count, step, v):
    for a in range(scr.shape[0]):
        scr[a, pl.ds(first, count, stride=step), :] = v[:, a * LANES : (a + 1) * LANES]


def iota(shape, dim):
    return lax.broadcasted_iota(jnp.int32, shape, dim).astype(F32)


def call(fn, outs, scratch, *args, smem=(), smem_out=(), hbm=(), hbm_out=(), vmem=16):
    def spec(space):
        return pl.BlockSpec(memory_space=space)

    def place_of(i, scalars, far):
        return spec(pltpu.SMEM if i in scalars else pl.ANY if i in far else pltpu.VMEM)

    in_specs = [place_of(i, smem, hbm) for i in range(len(args))]
    out_specs = [place_of(i, smem_out, hbm_out) for i in range(len(outs))]
    return pl.pallas_call(
        fn,
        out_shape=[jax.ShapeDtypeStruct(*o) for o in outs],
        in_specs=in_specs,
        out_specs=out_specs,
        scratch_shapes=scratch,
        compiler_params=pltpu.CompilerParams(vmem_limit_bytes=vmem * MIB),
        cost_estimate=pl.CostEstimate(flops=0, bytes_accessed=0, transcendentals=0),
    )(*args)


def pack_kernel(tok, seg, out, scr):
    count, feats, width = tok.shape
    lay(scr, tok[...].astype(F32).reshape(count * feats, width))
    row = seg[...].astype(F32)
    for f in range(feats):
        out[f, :count, :] = take(scr, f, count, feats).astype(BF)
        out[f, count:, :] = jnp.zeros((PAD, width), BF)
        out[f, count:, :count] = jnp.broadcast_to(row, (PAD, count)).astype(BF)


def codes(pos, starts):
    cls = jnp.zeros_like(pos)
    for st in starts:
        cls = cls + jnp.where(pos >= st, 1.0, 0.0)
    return jnp.where(cls >= CLASSES - 1, pos + CLASSES, cls)


def tile_range(start_ref, first, size, tile):
    last = first + size - 1
    lo = jnp.int32(0)
    hi = start_ref[1]
    for c in range(1, CLASSES - 1):
        st = start_ref[c]
        lo = jnp.where(first >= st, st, lo)
        hi = jnp.where(last >= st, start_ref[c + 1], hi)
    pad = start_ref[CLASSES - 1]
    lo = jnp.where(first >= pad, first, lo)
    hi = jnp.where(last >= pad, first + size, hi)
    return lo // tile, (hi + tile - 1) // tile


def permute_block(rank_row, first, rows, total):
    pos = iota((rows, LANES), 0) + first.astype(F32)
    parts = []
    for j in range(total // LANES):
        hit = rank_row[0:1, j * LANES : (j + 1) * LANES] == pos
        parts.append(jnp.where(hit, 1.0, 0.0).astype(BF))
    return jnp.concatenate(parts, -1)


def unpermute_block(rank_col, total):
    rows = rank_col.shape[0]
    parts = []
    for j in range(total // LANES):
        pos = iota((1, LANES), 1) + float(j * LANES)
        parts.append(jnp.where(rank_col == pos, 1.0, 0.0).astype(BF))
    return jnp.concatenate(parts, -1)


def fwd_kernel(hpd, hl, r_ref, *refs):
    xparts = refs[:hpd]
    (g1, b1, w_in) = refs[hpd : hpd + 3]
    (o_send, xs_out, ot_out, lse_out, rank_row, rank_col, start_ref) = refs[hpd + 3 : hpd + 10]
    (x_scr, seg_scr, qtz, k_scr, vt, o_scr, code_col, code_row, acc, top, s_scr) = refs[
        hpd + 10 : hpd + 21
    ]
    wqt, wvt = refs[hpd + 21 :]
    feats = xparts[0].shape[0]
    count = xparts[0].shape[1] - PAD
    total = x_scr.shape[0]
    cl = hl * HD
    r = r_ref[0]
    chunks = total // LANES
    wqt[...] = flip(head_columns(w_in, r, cl, 0)) * BF(SCALING)
    wvt[...] = flip(head_columns(w_in, r, cl, 2))

    for s in range(hpd):
        for k in range(feats):
            at = (s * feats + k) * count
            x_scr[at : at + count, :] = xparts[s][k, :count, :]
            row = xparts[s][k, count : count + PAD, :LANES].astype(F32)[0:1]
            col = jnp.transpose(jnp.broadcast_to(row, (LANES, LANES)))
            seg_scr[at : at + count, :] = col[:count, :]

    seg = seg_scr[...]
    cls = jnp.where(seg < 0.0, float(CLASSES - 1), seg)
    seg_scr[...] = cls * 8192.0 + iota((total, LANES), 0)
    key_rows = []
    for j in range(chunks):
        blk = seg_scr[j * LANES : (j + 1) * LANES, :]
        key_rows.append(jnp.transpose(blk)[0:8, :])

    def count_less(i, carry):
        blk = seg_scr[pl.ds(pl.multiple_of(i * 64, 64), 64), :]
        out = []
        for j in range(chunks):
            less = jnp.where(blk < key_rows[j][0:1], 1.0, 0.0)
            out.append(carry[j] + jnp.sum(less.reshape(8, 8, LANES), 0))
        return tuple(out)

    ranks = lax.fori_loop(
        0, total // 64, count_less, tuple(jnp.zeros((8, LANES), F32) for _ in range(chunks))
    )
    for j in range(chunks):
        row = jnp.sum(ranks[j], 0, keepdims=True)
        rank_row[:, j * LANES : (j + 1) * LANES] = jnp.broadcast_to(row, (8, LANES))
        rank_col[j * LANES : (j + 1) * LANES, :] = jnp.transpose(
            jnp.broadcast_to(row, (LANES, LANES))
        )
    starts = []
    keys = jnp.concatenate([k[0:1] for k in key_rows], 0)
    for c in range(1, CLASSES):
        st = jnp.sum(jnp.where(keys < c * 8192.0, 1.0, 0.0))
        starts.append(st)
        start_ref[c] = st.astype(jnp.int32)
    start_ref[0] = jnp.int32(0)
    for c in range(CLASSES, 8):
        start_ref[c] = jnp.int32(total)
    code_col[...] = codes(iota((total, LANES), 0), starts)
    code_row[...] = codes(iota((8, total), 1), starts)

    qtz[...] = jnp.zeros_like(qtz)
    ones = jnp.where(iota((16, total), 0) == 0.0, 1.0, 0.0).astype(BF)
    for h in range(hl):
        vt[h, HD:, :] = ones

    def project(b, _):
        at = pl.multiple_of(b * PB, PB)
        block = dot(permute_block(rank_row, at, PB, total), x_scr[...])
        xs_out[pl.ds(at, PB), :] = block.astype(BF)
        n, _r = ln_parts(block)
        h1 = (n * g1[...] + b1[...]).astype(BF)
        qt = dot_nt(wqt[...], h1).astype(BF)
        k_scr[pl.ds(at, PB), :] = dot(h1, head_columns(w_in, r, cl, 1)).astype(BF)
        vv = dot_nt(wvt[...], h1).astype(BF)
        for h in range(hl):
            sub = (h % 2) * HD
            qtz[h, sub : sub + HD, pl.ds(at, PB)] = qt[h * HD : (h + 1) * HD]
            vt[h, :HD, pl.ds(at, PB)] = vv[h * HD : (h + 1) * HD]
        return 0

    lax.fori_loop(0, total // PB, project, 0)

    def attend(b, _):
        at = pl.multiple_of(b * TQ, TQ)
        t0, t1 = tile_range(start_ref, at, TQ, TK)
        acc[...] = jnp.zeros_like(acc)
        top[...] = jnp.full_like(top, NEGATIVE)
        crow = code_row[0:1, pl.ds(at, TQ)]

        def score(t, _):
            kt = pl.multiple_of(t * TK, TK)
            ccol = code_col[pl.ds(kt, TK), :]
            ccol = jnp.concatenate([ccol] * (TQ // LANES), -1)
            seen = ccol == crow
            for h in range(hl):
                pair = (h // 2) * LANES
                s = dot(k_scr[pl.ds(kt, TK), pair : pair + LANES], qtz[h, :, pl.ds(at, TQ)])
                s = jnp.where(seen, s, NEGATIVE)
                s_scr[h, pl.ds(kt, TK), :] = s
                top[h] = jnp.maximum(top[h], jnp.max(s.reshape(TK // 8, 8, TQ), 0))
            return 0

        lax.fori_loop(t0, t1, score, 0)
        for h in range(hl):
            top[h] = jnp.broadcast_to(jnp.max(top[h], 0, keepdims=True), (8, TQ))

        def mix(t, _):
            kt = pl.multiple_of(t * TK, TK)
            for h in range(hl):
                p = jnp.exp(s_scr[h, pl.ds(kt, TK), :] - top[h, 0:1, :]).astype(BF)
                acc[h] += dot(vt[h, :, pl.ds(kt, TK)], p)
            return 0

        lax.fori_loop(t0, t1, mix, 0)
        outs = []
        for h in range(hl):
            total_h = acc[h, HD : HD + 1, :]
            outs.append(acc[h, :HD, :] / total_h)
            lse_out[h : h + 1, pl.ds(at, TQ)] = top[h, 0:1, :] + jnp.log(total_h)
        ot = jnp.concatenate(outs, 0)
        ot_out[:, pl.ds(at, TQ)] = ot.astype(BF)
        o_scr[pl.ds(at, TQ), :] = jnp.transpose(ot).astype(BF)
        return 0

    lax.fori_loop(0, total // TQ, attend, 0)

    group = feats // 2
    for blk in range(total // (group * count)):
        at = blk * group * count
        hot = unpermute_block(rank_col[at : at + group * count, :], total)
        o = dot(hot, o_scr[...]).astype(BF)
        for j in range(group):
            s, k = divmod(blk * group + j, feats)
            dest = k * hpd + lax.rem(r - s + hpd, hpd)
            o_send[dest] = o[j * count : (j + 1) * count]


def prep_kernel(
    hl,
    r_ref,
    xs,
    g1,
    b1,
    w_in,
    k_out,
    v_out,
    kt_out,
    qtz,
    nt,
    wqt,
    wkt,
):
    total = xs.shape[0]
    cl = hl * HD
    r = r_ref[0]
    wqt[...] = flip(head_columns(w_in, r, cl, 0)) * BF(SCALING)
    wkt[...] = flip(head_columns(w_in, r, cl, 1))
    qtz[...] = jnp.zeros_like(qtz)

    def project(b, _):
        at = pl.multiple_of(b * PB, PB)
        n, _r = ln_parts(xs[pl.ds(at, PB), :].astype(F32))
        h1 = (n * g1[...] + b1[...]).astype(BF)
        nt[:, pl.ds(at, PB)] = jnp.transpose(n.astype(BF))
        qt = dot_nt(wqt[...], h1).astype(BF)
        k_out[pl.ds(at, PB), :] = dot(h1, head_columns(w_in, r, cl, 1)).astype(BF)
        v_out[pl.ds(at, PB), :] = dot(h1, head_columns(w_in, r, cl, 2)).astype(BF)
        kt_out[:, pl.ds(at, PB)] = dot_nt(wkt[...], h1).astype(BF)
        for h in range(hl):
            sub = (h % 2) * HD
            qtz[h, sub : sub + HD, pl.ds(at, PB)] = qt[h * HD : (h + 1) * HD]
        return 0

    lax.fori_loop(0, total // PB, project, 0)


def plus(a, b):
    return (a.astype(F32) + b.astype(F32)).astype(BF)


def first_sums(x_ref, y_ref, a_keep, a_got, c_keep, c_got, a_mine, a_other, c_mine, c_other):
    half = a_mine.shape[1]
    mine = pl.multiple_of(x_ref[0] * half, half)
    other = pl.multiple_of((1 - x_ref[0]) * half, half)

    def step(i, _):
        for ref, first in ((a_mine, mine), (a_other, other)):
            ref[i] = plus(a_keep[i, pl.ds(first, half), :], a_got[i, pl.ds(first, half), :])
        return 0

    lax.fori_loop(0, a_mine.shape[0], step, 0)
    split_y(y_ref[0], c_keep, c_got, c_mine, c_other)


def split_y(y, keep, got, mine, other):
    def step(i, _):
        for ref, at in ((mine, 2 * i + y), (other, 2 * i + 1 - y)):
            ref[i] = plus(keep[at], got[at])
        return 0

    lax.fori_loop(0, mine.shape[0], step, 0)


def top_split(z_ref, keep, got, mine, other):
    chunks = mine.shape[0]
    top = z_ref[0] // chunks
    for j in range(chunks):
        mine[j] = plus(keep[top * chunks + j], got[top * chunks + j])
        other[j] = plus(keep[(1 - top) * chunks + j], got[(1 - top) * chunks + j])


def middle_sums(z_ref, a_keep, a_got, c_keep, c_got, *pieces):
    count = a_keep.shape[0]
    pick_z(z_ref, a_keep, a_got, *pieces[:count])
    for c, ref in enumerate(pieces[count:]):
        at = lax.bitwise_xor(lax.rem(z_ref[0], count // 2), c)
        ref[...] = plus(c_keep[at], c_got[at])


def add_all(terms):
    total = terms[0].astype(F32)
    for term in terms[1:]:
        total = total + term.astype(F32)
    return total.astype(BF)


def pick_y(y_ref, keep, got, mine, other):
    split_y(y_ref[0], keep, got, mine, other)


def pick_z(z_ref, keep, got, *pieces):
    for c, ref in enumerate(pieces):
        at = lax.bitwise_xor(z_ref[0], c)
        ref[...] = plus(keep[at], got[at])


def sum_kernel(*refs):
    refs[-1][...] = add_all([ref[...] for ref in refs[:-1]])


def bwd_kernel(
    hpd,
    hl,
    r_ref,
    start_ref,
    do_recv,
    k_in,
    v_in,
    kt_in,
    qtz,
    ot,
    lse,
    rank_row,
    dt_out,
    do_scr,
    dotz,
    dots,
    code_col,
    code_row,
    dq_acc,
    dk_acc,
    dv_acc,
    p_scr,
    ds_scr,
    pairs,
):
    feats = do_recv.shape[0] // hpd
    count = do_recv.shape[1]
    total = do_scr.shape[0]
    cl = hl * HD
    r = r_ref[0]

    for s in range(hpd):
        for k in range(feats):
            at = (s * feats + k) * count
            do_scr[at : at + count, :] = do_recv[k * hpd + lax.rem(r - s + hpd, hpd)]
    starts = [start_ref[c].astype(F32) for c in range(1, CLASSES)]
    code_col[...] = codes(iota((total, LANES), 0), starts)
    code_row[...] = codes(iota((8, total), 1), starts)
    dotz[...] = jnp.zeros_like(dotz)

    def arrange(b, _):
        at = pl.multiple_of(b * PB, PB)
        block = jnp.transpose(dot(permute_block(rank_row, at, PB, total), do_scr[...]))
        prod = block * ot[:, pl.ds(at, PB)].astype(F32)
        for h in range(hl):
            sub = (h % 2) * HD
            rows = slice(h * HD, (h + 1) * HD)
            dotz[h, sub : sub + HD, pl.ds(at, PB)] = block[rows].astype(BF)
            dots[h : h + 1, pl.ds(at, PB)] = jnp.sum(prod[rows], 0, keepdims=True)
        return 0

    lax.fori_loop(0, total // PB, arrange, 0)
    dq_acc[...] = jnp.zeros_like(dq_acc)
    dk_acc[...] = jnp.zeros_like(dk_acc)
    dv_acc[...] = jnp.zeros_like(dv_acc)

    def list_keys(b, filled):
        t0, t1 = tile_range(start_ref, b * KB, KB, QB)

        def put(t, i):
            pairs[i] = b * 4096 + t
            return i + 1

        return lax.fori_loop(t0, t1, put, filled)

    filled = lax.fori_loop(0, total // KB, list_keys, jnp.int32(0))

    def places(i):
        b, t = pairs[i] // 4096, lax.rem(pairs[i], 4096)
        return pl.ds(pl.multiple_of(b * KB, KB), KB), pl.ds(pl.multiple_of(t * QB, QB), QB)

    def scores(i):
        kt, at = places(i)
        ccol = code_col[kt, :]
        seen = jnp.concatenate([ccol] * (QB // LANES), -1) == code_row[0:1, at]
        for h in range(hl):
            cols = slice(h // 2 * LANES, (h // 2 + 1) * LANES)
            s = dot(k_in[kt, cols], qtz[h, :, at])
            p = jnp.where(seen, jnp.exp(s - lse[h : h + 1, at]), 0.0)
            dp = dot(v_in[kt, cols], dotz[h, :, at])
            p_scr[h] = p.astype(BF)
            ds_scr[h] = (p * (dp - dots[h : h + 1, at])).astype(BF)

    def collect(i):
        kt, at = places(i)
        for h in range(hl):
            rows = slice(h * HD, (h + 1) * HD)
            own = slice((h % 2) * HD, (h % 2 + 1) * HD)
            ds = ds_scr[h]
            dv_acc[rows, kt] += dot_nt(dotz[h, own, at], p_scr[h])
            dk_acc[rows, kt] += dot_nt(qtz[h, own, at], ds)
            dq_acc[rows, at] += dot(kt_in[rows, kt], ds)

    def step(i, _):
        scores(i)
        collect(i)
        return 0

    lax.fori_loop(0, filled, step, 0)
    dt_out[:cl, :] = (dq_acc[...] * SCALING).astype(BF)
    dt_out[cl : 2 * cl, :] = dk_acc[...].astype(BF)
    dt_out[2 * cl :, :] = dv_acc[...].astype(BF)


def dh_kernel(hpd, r_ref, dt, w_in, rank_col, *refs):
    dh_outs, dht = refs[:-1], refs[-1]
    part, count, width = dh_outs[0].shape
    cuts = len(dh_outs) // hpd
    feats = cuts * part
    total = dt.shape[1]
    cl = dt.shape[0] // 3
    w3 = jnp.concatenate([head_columns(w_in, r_ref[0], cl, j) for j in range(3)], 1)
    for b in range(total // PB):
        at = slice(b * PB, (b + 1) * PB)
        dht[:, at] = dot(w3, dt[:, at]).astype(BF)
    group = feats // 2
    for blk in range(total // (group * count)):
        at = blk * group * count
        hot = unpermute_block(rank_col[at : at + group * count, :], total)
        o = dot_nt(hot, dht[...]).astype(BF)
        for j in range(group):
            s, k = divmod(blk * group + j, feats)
            dh_outs[cuts * s + k // part][k % part] = o[j * count : (j + 1) * count]


SUB = 16
CUTS = 4


def q_rows(cl, width):
    return SUB * (-(-6 * cl // width)) + SUB


def dw_kernel(r_ref, x_ref, y_ref, z_ref, dt, nt, w_in, g1, b1, *refs):
    x = x_ref[0]
    width, total = nt.shape
    cols = dt.shape[0]
    cl = cols // 3
    a_keep, a_got, c_keep, c_got, q_keep, q_send, a_mine, a_other, c_mine, c_other = refs[:10]
    m_scr, dw_scr = refs[10:]
    split_y(y_ref[0], a_keep, a_got, a_mine, a_other)
    top_split(z_ref, c_keep, c_got, c_mine, c_other)
    feats = q_keep.shape[0]
    for c in range(3):
        rows = slice(c * cl, (c + 1) * cl)
        m_scr[:, rows] = dot_nt(nt[...], dt[rows, :])
    ones = jnp.ones((8, total), BF)
    sums_row = dot_nt(ones, dt[...])[0:1]
    gcol = jnp.transpose(jnp.broadcast_to(g1[...], (LANES, width)))
    bcol = jnp.transpose(jnp.broadcast_to(b1[...], (LANES, width)))
    gg = jnp.zeros((width, LANES), F32)
    gb = jnp.zeros((width, LANES), F32)
    for j in range(cols // LANES):
        lanes = slice(j * LANES, (j + 1) * LANES)
        first = (j * LANES // cl) * width + r_ref[0] * cl + j * LANES % cl
        w = w_in[:, pl.ds(pl.multiple_of(first, LANES), LANES)].astype(F32)
        m = m_scr[:, lanes]
        gg = gg + w * m
        gb = gb + w * sums_row[:, lanes]
        dw_scr[:, lanes] = (m * gcol + bcol * sums_row[:, lanes]).astype(BF)
    gg = jnp.sum(jnp.transpose(gg), 0, keepdims=True)
    gb = jnp.sum(jnp.transpose(gb), 0, keepdims=True)
    vec = jnp.concatenate([gg, gb, jnp.zeros((SUB - 2, width), F32)], 0).astype(BF)
    per = width // cl
    last = q_keep.shape[1] - SUB
    for e in range(feats):
        for ref, side in ((q_keep, x), (q_send, 1 - x)):
            for s in range(6):
                j, b = divmod(s, 2)
                src = pl.multiple_of((e * 4 + b) * SUB + side * 2 * SUB, SUB)
                to = (s // per) * SUB
                ref[e, to : to + SUB, (s % per) * cl : (s % per + 1) * cl] = dw_scr[
                    pl.ds(src, SUB), j * cl : (j + 1) * cl
                ]
            used = 6 % per
            if used:
                ref[e, last - SUB : last, used * cl :] = jnp.zeros((SUB, width - used * cl), BF)
            ref[e, last:, :] = vec


def gather_kernel(hpd, r_ref, x_ref, *refs):
    same, other = refs[:hpd], refs[hpd : 2 * hpd]
    a_side, a_pair, c_sum, c_pair = refs[2 * hpd : 2 * hpd + 4]
    out, vec, down, up, fqkv, fout, sout, vectors = refs[2 * hpd + 4 :]
    piece = out.shape[0]
    rows, width = same[0].shape
    cl = width // hpd
    r, x = r_ref[0], x_ref[0]
    blocks = piece // SUB
    first = lax.rem(r * blocks, 2)
    from_same = r * blocks // 2 == x
    for s in range(hpd):
        owner = lax.rem(r - s + hpd, hpd)
        for j in range(3):
            lo = 2 * j // hpd * SUB
            to = pl.ds(pl.multiple_of(j * width + owner * cl, LANES), cl)
            for b in range(blocks):
                col = pl.multiple_of((2 * j % hpd + first + b) * cl, LANES)
                at = (slice(lo, lo + SUB), pl.ds(col, cl))
                picked = jnp.where(from_same, same[s][at].astype(F32), other[s][at].astype(F32))
                out[b * SUB : (b + 1) * SUB, to] = picked
    total = same[0][rows - SUB : rows, :].astype(F32)
    for s in range(1, hpd):
        total = total + same[s][rows - SUB : rows, :].astype(F32)
    vec[...] = total[:8]

    down[...] = jnp.where(x == 0, a_side[...].astype(F32), a_pair[...].astype(F32))

    def both(first, size):
        at = slice(first, first + size)
        return c_sum[at, :].astype(F32) + c_pair[at, :].astype(F32)

    for b in range(up.shape[1] // width):
        at = slice(b * piece, (b + 1) * piece)
        block = jnp.where(x == 0, a_pair[at, :].astype(F32), a_side[at, :].astype(F32))
        up[:, b * width : (b + 1) * width] = block
    base = 0
    for ref in (fqkv, fout, sout):
        for b in range(ref.shape[1] // width):
            ref[:, b * width : (b + 1) * width] = both(base, piece)
            base += piece
    vectors[...] = both(base, vectors.shape[0])


def norm_kernel(hpd, *refs):
    parts = refs[:-5]
    x, g1, q_keep, q_got, out = refs[-5:]
    part, count, _w = parts[0].shape
    cuts = len(parts) // hpd
    feats = cuts * part
    for k in range(feats):
        dh = parts[k // part][k % part].astype(F32)
        for s in range(1, hpd):
            dh = dh + parts[cuts * s + k // part][k % part].astype(F32)
        n, r = ln_parts(x[k, :count, :].astype(F32))
        out[k, :count, :] = ln_back(dh, n, r, g1[...]).astype(BF)
        out[k, count:, :] = add_all((q_keep[k], q_got[k]))


def final_kernel(dx1, both, out, q_sum, scr):
    feats = both.shape[0]
    count, _f, width = out.shape
    q_sum[...] = add_all([both[k, count:, :] for k in range(feats)])
    for f in range(feats):
        val = dx1[f * count : (f + 1) * count, :] + both[f, :count, :].astype(F32)
        place(scr, f, count, feats, val)
    out[...] = lift(scr).reshape(count, feats, width)


def rows_kernel(
    hpd,
    me_ref,
    o_recv,
    xt,
    cot_hbm,
    g2,
    b2,
    g3,
    b3,
    ub,
    db,
    wso_hbm,
    wfq_hbm,
    wfo_hbm,
    wup_hbm,
    wdn_hbm,
    *refs,
):
    outs_hbm, scratch = refs[:7], refs[7:-2]
    (wso, wfq, wfo, wup, wdn, cot), scratch = scratch[:6], scratch[6:]
    outs_vmem, scratch = scratch[:7], scratch[7:]
    out, dx1, do_send, a_keep, a_send, b_keep, b_send = outs_vmem
    (
        wide,
        ct,
        o1,
        x1,
        h2,
        qkv,
        o2,
        x2,
        h3,
        u,
        dz,
        dx2,
        do2,
        dqkv,
        pscr,
        tr,
        wblk,
        ubg,
        wdn_scr,
    ) = scratch
    in_sem, out_sem = refs[-2:]
    loads = [
        pltpu.make_async_copy(src, dst, in_sem.at[i])
        for i, (src, dst) in enumerate(
            (
                (cot_hbm, cot),
                (wso_hbm, wso),
                (wfq_hbm, wfq),
                (wfo_hbm, wfo),
                (wup_hbm, wup),
                (wdn_hbm, wdn),
            )
        )
    ]
    for load in loads:
        load.start()
    stores = [
        pltpu.make_async_copy(src, dst, out_sem.at[i])
        for i, (src, dst) in enumerate(zip(outs_vmem, outs_hbm))
    ]
    feats = xt.shape[0]
    count = xt.shape[1] - PAD
    width = xt.shape[2]
    rows = feats * count
    hidden = wup.shape[1]
    n = o_recv.shape[0]
    cl = o_recv.shape[2]
    half = rows // 2
    me = me_ref[0]
    lane = iota((1, LANES), 1)
    part = 16
    tiles = count // part
    size = feats * part

    loads[0].wait()
    lay(wide, cot[...].astype(F32).reshape(rows, width))
    for f in range(feats):
        ct[f * count : (f + 1) * count, :] = take(wide, f, count, feats).astype(BF)
        for c in range(hpd):
            o1[f * count : (f + 1) * count, c * cl : (c + 1) * cl] = o_recv[f * hpd + c]

    loads[1].wait()
    for b in range(2):
        at = slice(b * half, (b + 1) * half)
        x = xt[b * feats // 2 : (b + 1) * feats // 2, :count, :].astype(F32).reshape(half, width)
        v = x + dot(o1[at, :], wso[...])
        x1[at, :] = v
        nn, _r = ln_parts(v)
        h2[at, :] = (nn * g2[...] + b2[...]).astype(BF)

    loads[2].wait()
    qkv3 = qkv

    def qkv_step(c, _):
        cols = pl.ds(pl.multiple_of(c * TILE, TILE), TILE)
        scale = jnp.where(c < width // TILE, SCALING, 1.0)
        y = dot(h2[...], wfq[:, cols])
        qkv3[:, :, cols] = (y * scale).astype(BF).reshape(feats, count, TILE)
        return 0

    lax.fori_loop(0, 3 * width // TILE, qkv_step, 0)

    ri = lax.broadcasted_iota(jnp.int32, (2 * size, size), 0)
    ci = lax.broadcasted_iota(jnp.int32, (2 * size, size), 1)
    same = lax.rem(ri, part) == lax.rem(ci, part)
    low_lane = jnp.where(iota((1, LANES), 1) < HD, 1.0, 0.0).astype(BF)
    high_lane = jnp.where(iota((1, LANES), 1) < HD, 0.0, 1.0).astype(BF)

    def tile_of(ref, at, lo):
        return ref[:, at, lo : lo + LANES].reshape(size, LANES)

    def by_head(v):
        return jnp.concatenate([v * low_lane, v * high_lane], 0)

    def by_head_t(v):
        vt = jnp.transpose(v)
        zero = jnp.zeros((HD, size), BF)
        return jnp.concatenate(
            [jnp.concatenate([vt[:HD], zero], 0), jnp.concatenate([zero, vt[HD:]], 0)], 1
        )

    def side(v):
        return jnp.concatenate([v[:size], v[size:]], 1)

    def per_head(v, fn):
        return jnp.concatenate(
            [jnp.broadcast_to(fn(v[i * size : (i + 1) * size]), (size, size)) for i in (0, 1)], 0
        )

    def feat_fwd(t, _):
        at = pl.ds(pl.multiple_of(t * part, part), part)
        for p2 in range(H // 2):
            lo = p2 * LANES
            q = tile_of(qkv3, at, lo)
            k = tile_of(qkv3, at, width + lo)
            v = tile_of(qkv3, at, 2 * width + lo)
            s = jnp.where(same, dot_nt(by_head(k), q), NEGATIVE)
            e = jnp.exp(s - per_head(s, lambda w: jnp.max(w, 0, keepdims=True)))
            p = (e * per_head(e, lambda w: 1.0 / jnp.sum(w, 0, keepdims=True))).astype(BF)
            pscr[t, p2] = p
            ot = dot(by_head_t(v), p)
            o2[:, at, lo : lo + LANES] = jnp.transpose(ot).astype(BF).reshape(feats, part, LANES)
        return 0

    lax.fori_loop(0, tiles, feat_fwd, 0, unroll=True)

    loads[3].wait()
    for b in range(2):
        at = slice(b * half, (b + 1) * half)
        o = o2[b * feats // 2 : (b + 1) * feats // 2, :, :].reshape(half, width)
        v = x1[at, :] + dot(o, wfo[...])
        x2[at, :] = v
        nn, _r = ln_parts(v)
        h3[at, :] = (nn * g3[...] + b3[...]).astype(BF)

    loads[4].wait()
    loads[5].wait()

    def ffn(c, _):
        cols = pl.ds(pl.multiple_of(c * FT, FT), FT)
        total = jnp.zeros((8, FT), F32)
        for b in range(2):
            at = slice(b * half, (b + 1) * half)
            z = dot(h3[at, :], wup[:, cols]) + ub[0:1, cols]
            w = GELU_C * GELU_A * (z * z) + GELU_C
            cdf = 0.5 * jnp.tanh(z * w) + 0.5
            g = z * cdf
            u[at, cols] = g.astype(BF)
            slope = cdf + g * (1.0 - cdf) * (6.0 * w - 4.0 * GELU_C)
            d = dot_nt(ct[at, :], wdn[cols, :]) * slope
            dz[at, cols] = d.astype(BF)
            total = total + jnp.sum(d.reshape(half // 8, 8, FT), 0)
        ubg[:, cols] = total
        return 0

    lax.fori_loop(0, hidden // FT, ffn, 0)

    vectors = []
    gg = jnp.zeros((1, width), F32)
    gb = jnp.zeros((1, width), F32)
    gd = jnp.zeros((1, width), F32)
    for b in range(2):
        at = slice(b * half, (b + 1) * half)
        y = x2[at, :] + dot(u[at, :], wdn[...]) + db[...]
        for j in range(feats // 2):
            f = b * (feats // 2) + j
            place(wide, f, count, feats, y[j * count : (j + 1) * count])
        dh = dot_nt(dz[at, :], wup[...])
        nn, r = ln_parts(x2[at, :])
        c = ct[at, :].astype(F32)
        gg = gg + jnp.sum(dh * nn, 0, keepdims=True)
        gb = gb + jnp.sum(dh, 0, keepdims=True)
        gd = gd + jnp.sum(c, 0, keepdims=True)
        v = c + ln_back(dh, nn, r, g3[...])
        dx2[at, :] = v
        do2[b * feats // 2 : (b + 1) * feats // 2, :, :] = (
            dot_nt(v.astype(BF), wfo[...]).astype(BF).reshape(feats // 2, count, width)
        )
    out[...] = lift(wide).reshape(count, feats, width).astype(BF)
    stores[0].start()
    vectors = [gg, gb, gd]

    core = lax.rem(me, 2)

    def slot(pos):
        at, other = divmod(pos, 2)
        refs = (a_send, b_send) if other else (a_keep, b_keep)
        return refs, at, 2 * at + (1 - core if other else core)

    piece = width // n
    fpiece = hidden // n

    def spread(group, base):
        for pos in range(n):
            refs, at, d = slot(pos)
            src = pl.multiple_of(d * piece, piece)
            refs[group][at, base : base + piece, :] = wblk[pl.ds(src, piece), :]

    base = 0
    for b in range(hidden // width):
        tr[...] = flip(u[:, b * width : (b + 1) * width])
        wdn_scr[b * width : (b + 1) * width, :] = dot(tr[...], ct[...]).astype(BF)
    for pos in range(n):
        refs, at, d = slot(pos)
        src = pl.multiple_of(d * fpiece, fpiece)
        refs[0][at, base : base + fpiece, :] = wdn_scr[pl.ds(src, fpiece), :]
    base += fpiece
    tr[...] = flip(h3[...])
    for b in range(hidden // width):
        wblk[...] = dot(tr[...], dz[:, b * width : (b + 1) * width]).astype(BF)
        spread(0, base)
        base += piece
    stores[3].start()
    stores[4].start()

    def feat_bwd(t, _):
        at = pl.ds(pl.multiple_of(t * part, part), part)
        for p2 in range(H // 2):
            lo = p2 * LANES
            q = tile_of(qkv3, at, lo)
            k = tile_of(qkv3, at, width + lo)
            v = tile_of(qkv3, at, 2 * width + lo)
            g = tile_of(do2, at, lo)
            p = pscr[t, p2]
            pf = p.astype(F32)
            dp = dot_nt(by_head(v), g)
            ds = pf * (dp - per_head(pf * dp, lambda w: jnp.sum(w, 0, keepdims=True)))
            ds = ds.astype(BF)
            dv = dot(side(p), by_head(g))
            dk = dot(side(ds), by_head(q))
            dq = jnp.transpose(dot(by_head_t(k), ds)) * SCALING
            for j, d in enumerate((dq, dk, dv)):
                dqkv[:, at, j * width + lo : j * width + lo + LANES] = d.astype(BF).reshape(
                    feats, part, LANES
                )
        return 0

    lax.fori_loop(0, tiles, feat_bwd, 0, unroll=True)

    gg = jnp.zeros((1, width), F32)
    gb = jnp.zeros((1, width), F32)
    for b in range(2):
        at = slice(b * half, (b + 1) * half)
        d = dqkv[b * feats // 2 : (b + 1) * feats // 2, :, :].reshape(half, 3 * width)
        dh = dot_nt(d, wfq[...])
        nn, r = ln_parts(x1[at, :])
        gg = gg + jnp.sum(dh * nn, 0, keepdims=True)
        gb = gb + jnp.sum(dh, 0, keepdims=True)
        v = dx2[at, :] + ln_back(dh, nn, r, g2[...])
        dx1[at, :] = v
        g = dot_nt(v.astype(BF), wso[...]).astype(BF)
        for j in range(feats // 2):
            f = b * (feats // 2) + j
            for c in range(hpd):
                do_send[f * hpd + c] = g[j * count : (j + 1) * count, c * cl : (c + 1) * cl]
    stores[1].start()
    stores[2].start()
    vectors = [gg, gb] + vectors

    base = 0
    tr[...] = flip(h2[...])
    for b in range(3):
        d = dqkv[:, :, b * width : (b + 1) * width].reshape(rows, width)
        wblk[...] = dot(tr[...], d).astype(BF)
        spread(1, base)
        base += piece
    tr[...] = flip(o2[...].reshape(rows, width))
    wblk[...] = dot(tr[...], dx2[...].astype(BF)).astype(BF)
    spread(1, base)
    base += piece
    tr[...] = flip(o1[...])
    wblk[...] = dot(tr[...], dx1[...].astype(BF)).astype(BF)
    spread(1, base)
    base += piece
    ubs = jnp.sum(ubg[...], 0, keepdims=True)
    vectors = vectors + [ubs[:, b * width : (b + 1) * width] for b in range(hidden // width)]
    vec = jnp.concatenate(vectors + [jnp.zeros((16 - len(vectors), width), F32)], 0).astype(BF)
    for pos in range(n):
        refs, at, _d = slot(pos)
        refs[1][at, base : base + 16, :] = vec
    stores[5].start()
    stores[6].start()
    for store in stores:
        store.wait()


def solution(mesh):
    n = mesh.shape["samp"]
    groups = mesh.shape["grp"]
    gbits = groups.bit_length() - 1
    tie = lax.optimization_barrier
    swap_core = [(d, d ^ 1) for d in range(n)]
    swap_y = [(d, d ^ 2) for d in range(n)]
    same_core = [[2 * k + c for k in range(n // 2)] for c in (0, 1)]

    def swap_grp(v, bit=0):
        return lax.ppermute(v, "grp", [(d, d ^ (1 << bit)) for d in range(groups)])

    def rest_of_grp(v):
        for bit in range(1, gbits):
            v = (v.astype(F32) + swap_grp(v, bit).astype(F32)).astype(BF)
        return v

    def body(
        tokens,
        segments,
        cotangent,
        first_gain,
        first_shift,
        sample_qkv,
        sample_out,
        second_gain,
        second_shift,
        feature_qkv,
        feature_out,
        third_gain,
        third_shift,
        up_weight,
        up_bias,
        down_weight,
        down_bias,
    ):
        count, feats, width = tokens.shape[1:]
        hidden = up_weight.shape[1]
        rows = count * feats
        hpd = n // feats
        hl = H // hpd
        cl = hl * HD
        total = n * count
        heads8 = 8
        me = lax.axis_index("samp")
        r = lax.rem(me, hpd)
        x = lax.rem(lax.axis_index("grp"), 2)
        y, z = (me >> 1) & 1, me >> 2
        r1, me1, x1, y1, z1 = (v.reshape(1).astype(jnp.int32) for v in (r, me, x, y, z))
        peers = [[q + hpd * k for k in range(feats)] for q in range(hpd)]
        g1, b1, g2, b2, g3, b3, ub, db = (
            v.reshape(1, -1)
            for v in (
                first_gain,
                first_shift,
                second_gain,
                second_shift,
                third_gain,
                third_shift,
                up_bias,
                down_bias,
            )
        )

        def shift(s):
            return [(d, d // hpd * hpd + (d % hpd + s) % hpd) for d in range(n)]

        (xt,) = call(
            pack_kernel,
            [((feats, count + PAD, width), BF)],
            [pltpu.VMEM((width // LANES, rows, LANES), F32)],
            tokens[0],
            segments,
        )
        mine = lax.all_to_all(xt, "samp", 0, 0, tiled=True, axis_index_groups=peers)
        xparts = [mine] + [lax.ppermute(mine, "samp", shift(s)) for s in range(1, hpd)]

        o_send, xs, ot, lse, rank_row, rank_col, starts = call(
            functools.partial(fwd_kernel, hpd, hl),
            [
                ((n, count, cl), BF),
                ((total, width), BF),
                ((cl, total), BF),
                ((heads8, total), F32),
                ((8, total), F32),
                ((total, LANES), F32),
                ((8,), jnp.int32),
            ],
            [
                pltpu.VMEM((total, width), BF),
                pltpu.VMEM((total, LANES), F32),
                pltpu.VMEM((hl, LANES, total), BF),
                pltpu.VMEM((total, cl), BF),
                pltpu.VMEM((hl, HD + 16, total), BF),
                pltpu.VMEM((total, cl), BF),
                pltpu.VMEM((total, LANES), F32),
                pltpu.VMEM((8, total), F32),
                pltpu.VMEM((hl, HD + 16, TQ), F32),
                pltpu.VMEM((hl, 8, TQ), F32),
                pltpu.VMEM((hl, total, TQ), F32),
                pltpu.VMEM((cl, width), BF),
                pltpu.VMEM((cl, width), BF),
            ],
            r1,
            *xparts,
            g1,
            b1,
            sample_qkv,
            smem=(0,),
            smem_out=(6,),
            vmem=28,
        )
        o_recv = lax.all_to_all(o_send, "samp", 0, 0, tiled=True)

        piece = width // n
        fpiece = hidden // n
        apieces = fpiece + piece * (hidden // width)
        bpieces = piece * 5 + 16
        vm = pltpu.VMEM
        out, dx1, do_send, a_keep, a_send, b_keep, b_send = call(
            functools.partial(rows_kernel, hpd),
            [
                ((count, feats, width), BF),
                ((rows, width), F32),
                ((n, count, cl), BF),
                ((n // 2, apieces, width), BF),
                ((n // 2, apieces, width), BF),
                ((n // 2, bpieces, width), BF),
                ((n // 2, bpieces, width), BF),
            ],
            [
                vm((width, width), BF),
                vm((width, 3 * width), BF),
                vm((width, width), BF),
                vm((width, hidden), BF),
                vm((hidden, width), BF),
                vm((count, feats, width), BF),
                vm((count, feats, width), BF),
                vm((rows, width), F32),
                vm((n, count, cl), BF),
                vm((n // 2, apieces, width), BF),
                vm((n // 2, apieces, width), BF),
                vm((n // 2, bpieces, width), BF),
                vm((n // 2, bpieces, width), BF),
                vm((width // LANES, rows, LANES), F32),
                vm((rows, width), BF),
                vm((rows, width), BF),
                vm((rows, width), F32),
                vm((rows, width), BF),
                vm((feats, count, 3 * width), BF),
                vm((feats, count, width), BF),
                vm((rows, width), F32),
                vm((rows, width), BF),
                vm((rows, hidden), BF),
                vm((rows, hidden), BF),
                vm((rows, width), F32),
                vm((feats, count, width), BF),
                vm((feats, count, 3 * width), BF),
                vm((count // 16, H // 2, 32 * feats, 16 * feats), BF),
                vm((width, rows), BF),
                vm((width, width), BF),
                vm((8, hidden), F32),
                vm((hidden, width), BF),
                pltpu.SemaphoreType.DMA((6,)),
                pltpu.SemaphoreType.DMA((7,)),
            ],
            me1,
            o_recv,
            xt,
            cotangent[0],
            g2,
            b2,
            g3,
            b3,
            ub,
            db,
            sample_out,
            feature_qkv,
            feature_out,
            up_weight,
            down_weight,
            smem=(0,),
            hbm=(3, 10, 11, 12, 13, 14),
            hbm_out=tuple(range(7)),
            vmem=48,
        )
        a_got = lax.ppermute(a_send, "samp", swap_core)
        b_got = lax.ppermute(b_send, "samp", swap_core)
        do_recv = lax.all_to_all(do_send, "samp", 0, 0, tiled=True)

        qr = q_rows(cl, width)
        half = apieces // 2
        zs = n // 4

        def along_z(pieces, unit):
            return [pieces[0]] + [
                lax.ppermute(pieces[c], "samp", [(d, d ^ (unit * c)) for d in range(n)])
                for c in range(1, len(pieces))
            ]

        am, ao, cm, co = call(
            first_sums,
            [((n // 2, half, width), BF)] * 2 + [((n // 4, bpieces, width), BF)] * 2,
            [],
            x1,
            y1,
            a_keep,
            a_got,
            b_keep,
            b_got,
            smem=(0, 1),
            vmem=16,
        )
        ag, cg = swap_grp(ao), lax.ppermute(co, "samp", swap_y)
        xs_after, _ = tie((xs, am))
        k_all, v_all, kt_all, qtz, nt = call(
            functools.partial(prep_kernel, hl),
            [
                ((total, cl), BF),
                ((total, cl), BF),
                ((cl, total), BF),
                ((hl, LANES, total), BF),
                ((width, total), BF),
            ],
            [vm((cl, width), BF), vm((cl, width), BF)],
            r1,
            xs_after,
            g1,
            b1,
            sample_qkv,
            smem=(0,),
            vmem=16,
        )
        (dt,) = call(
            functools.partial(bwd_kernel, hpd, hl),
            [((3 * cl, total), BF)],
            [
                vm((total, cl), BF),
                vm((hl, LANES, total), BF),
                vm((8, total), F32),
                vm((total, LANES), F32),
                vm((8, total), F32),
                vm((cl, total), F32),
                vm((cl, total), F32),
                vm((cl, total), F32),
                vm((hl, KB, QB), BF),
                vm((hl, KB, QB), BF),
                pltpu.SMEM(((total // KB) * (total // QB),), jnp.int32),
            ],
            r1,
            starts,
            do_recv,
            k_all,
            v_all,
            kt_all,
            qtz,
            ot,
            lse,
            rank_row,
            smem=(0, 1),
            vmem=58,
        )
        am, ag, cm, cg, _ = tie((am, ag, cm, cg, dt))
        q_keep, q_send, am, ao, cm, co = call(
            dw_kernel,
            [((feats, qr, width), BF)] * 2
            + [((n // 4, half, width), BF)] * 2
            + [((zs // 2, bpieces, width), BF)] * 2,
            [vm((width, 3 * cl), F32), vm((width, 3 * cl), BF)],
            r1,
            x1,
            y1,
            z1,
            dt,
            nt,
            sample_qkv,
            g1,
            b1,
            am,
            ag,
            cm,
            cg,
            smem=(0, 1, 2, 3),
            vmem=16,
        )
        ag = lax.ppermute(ao, "samp", swap_y)
        cg = lax.ppermute(co, "samp", [(d, d ^ (n // 2)) for d in range(n)])
        dt, _ = tie((dt, q_send))
        dhs = call(
            functools.partial(dh_kernel, hpd),
            [((feats // CUTS, count, width), BF)] * (CUTS * hpd),
            [vm((width, total), BF)],
            r1,
            dt,
            sample_qkv,
            rank_col,
            smem=(0,),
            vmem=16,
        )
        parts = list(dhs[:CUTS])
        for s in range(1, hpd):
            parts += [lax.ppermute(v, "samp", shift(-s)) for v in dhs[CUTS * s : CUTS * s + CUTS]]
        pieces = call(
            middle_sums,
            [((half, width), BF)] * zs + [((bpieces, width), BF)] * (zs // 2),
            [],
            z1,
            am,
            ag,
            cm,
            cg,
            smem=(0,),
        )
        parts[0], _ = tie((parts[0], pieces[0]))
        a_pieces, c_pieces = along_z(pieces[:zs], 4), along_z(pieces[zs:], 4)
        (both,) = call(
            functools.partial(norm_kernel, hpd),
            [((feats, count + qr, width), BF)],
            [],
            *parts,
            mine,
            g1,
            q_keep,
            swap_grp(q_send),
            vmem=10,
        )
        both_send, *ends = tie((both, *a_pieces, *c_pieces))
        a_pieces, c_pieces = ends[:zs], ends[zs:]
        both = lax.all_to_all(both_send, "samp", 0, 0, tiled=True, axis_index_groups=peers)

        def last_steps(*pieces):
            (c_sum,) = call(sum_kernel, [((bpieces, width), BF)], [], *pieces[zs:])
            c_sum = rest_of_grp(c_sum)
            (a_side,) = call(sum_kernel, [((half, width), BF)], [], *pieces[:zs])
            a_side = rest_of_grp(a_side)
            return a_side, swap_grp(a_side), c_sum, swap_grp(c_sum)

        terms = (*a_pieces, *c_pieces)
        parts_summed = lax.cond(
            starts[0] == 0,
            last_steps,
            lambda *t: jax.tree.map(
                lambda v: jnp.zeros(v.shape, v.dtype), jax.eval_shape(last_steps, *t)
            ),
            *tie((*terms, both_send))[: len(terms)],
        )
        dx1, _ = tie((dx1, parts_summed[0]))
        grad_tokens, q_sum = call(
            final_kernel,
            [((count, feats, width), F32), ((qr, width), BF)],
            [vm((width // LANES, rows, LANES), F32)],
            dx1,
            both,
            vmem=12,
        )
        q_sum = rest_of_grp(q_sum)

        def from_peer(s, other):
            if not s and not other:
                return q_sum
            pairs = [
                (g * n + d, (g ^ other) * n + e) for g in range(groups) for d, e in shift(s)
            ]
            return lax.ppermute(q_sum, ("grp", "samp"), pairs)

        peers_same = [from_peer(s, 0) for s in range(hpd)]
        peers_other = [from_peer(s, 1) for s in range(hpd)]
        grad_sample_qkv, vec_sum, grad_down, grad_up, grad_fqkv, grad_fout, grad_sout, vu = call(
            functools.partial(gather_kernel, hpd),
            [
                ((piece, 3 * width), F32),
                ((8, width), F32),
                ((fpiece, width), F32),
                ((piece, hidden), F32),
                ((piece, 3 * width), F32),
                ((piece, width), F32),
                ((piece, width), F32),
                ((16, width), F32),
            ],
            [],
            r1,
            x1,
            *peers_same,
            *peers_other,
            *parts_summed,
            smem=(0, 1),
        )

        def own(v):
            return lax.dynamic_slice_in_dim(v, me * (v.shape[0] // n), v.shape[0] // n, 0)

        def own_rows(v):
            return lax.dynamic_slice_in_dim(v, me * piece, piece, 1)

        five = own_rows(vu[:5])
        two = own_rows(vec_sum[:2])
        vectors = [five[i] for i in range(5)]
        vectors.append(own(vu[5 : 5 + hidden // width].reshape(-1)))
        return (
            out[None],
            grad_tokens[None],
            two[0],
            two[1],
            grad_sample_qkv,
            grad_sout,
            vectors[0],
            vectors[1],
            grad_fqkv,
            grad_fout,
            vectors[2],
            vectors[3],
            grad_up,
            vectors[5],
            grad_down,
            vectors[4],
        )

    rep = P()
    data = P("grp", "samp", None, None)
    line = P("samp")
    flat = P("samp", None)
    in_specs = (data, P("grp", "samp"), data) + (rep,) * 14
    out_specs = (
        data,
        data,
        line,
        line,
        flat,
        flat,
        line,
        line,
        flat,
        flat,
        line,
        line,
        flat,
        line,
        flat,
        line,
    )
    return jax.shard_map(body, mesh=mesh, in_specs=in_specs, out_specs=out_specs, check_vma=False)
```

```python
import functools
import math

import jax
import jax.numpy as jnp
from jax import lax
from jax.experimental import pallas as pl
from jax.experimental.pallas import tpu as pltpu
from jax.sharding import PartitionSpec as P

H = 8
HD = 64
EPSILON = 1e-05
SCALING = 0.125
NEGATIVE = -1e30
BF = jnp.bfloat16
F32 = jnp.float32
TILE = 256
FT = 512
PB = 512
KB = 256
QB = 256
TQ = 256
TK = 256
LANES = 128
PAD = 8
GELU_C = math.sqrt(2.0 / math.pi)
GELU_A = 0.044715
MIB = 1024 * 1024
CLASSES = 5


def dot(a, b):
    return jnp.dot(a, b, preferred_element_type=F32)


def dot_nt(a, b):
    return lax.dot_general(a, b, (((1,), (1,)), ((), ())), preferred_element_type=F32)


def dot_tn(a, b):
    return lax.dot_general(a, b, (((0,), (0,)), ((), ())), preferred_element_type=F32)


def ln_parts(v):
    c = v - jnp.mean(v, -1, keepdims=True)
    r = lax.rsqrt(jnp.mean(c * c, -1, keepdims=True) + EPSILON)
    return c * r, r


def ln_back(dh, n, r, g):
    e = dh * g
    return r * (e - jnp.mean(e, -1, keepdims=True) - n * jnp.mean(e * n, -1, keepdims=True))


def flip(v):
    return jnp.transpose(v)


def head_columns(w, r, cl, which):
    first = which * (w.shape[1] // 3) + r * cl
    return w[:, pl.ds(pl.multiple_of(first, LANES), cl)]


def lay(scr, v):
    for a in range(scr.shape[0]):
        scr[a] = v[:, a * LANES : (a + 1) * LANES]


def lift(scr):
    return jnp.concatenate([scr[a] for a in range(scr.shape[0])], -1)


def take(scr, first, count, step):
    return jnp.concatenate(
        [scr[a, pl.ds(first, count, stride=step), :] for a in range(scr.shape[0])], -1
    )


def place(scr, first, count, step, v):
    for a in range(scr.shape[0]):
        scr[a, pl.ds(first, count, stride=step), :] = v[:, a * LANES : (a + 1) * LANES]


def iota(shape, dim):
    return lax.broadcasted_iota(jnp.int32, shape, dim).astype(F32)


def call(fn, outs, scratch, *args, smem=(), smem_out=(), hbm=(), hbm_out=(), vmem=16):
    def spec(space):
        return pl.BlockSpec(memory_space=space)

    def place_of(i, scalars, far):
        return spec(pltpu.SMEM if i in scalars else pl.ANY if i in far else pltpu.VMEM)

    in_specs = [place_of(i, smem, hbm) for i in range(len(args))]
    out_specs = [place_of(i, smem_out, hbm_out) for i in range(len(outs))]
    return pl.pallas_call(
        fn,
        out_shape=[jax.ShapeDtypeStruct(*o) for o in outs],
        in_specs=in_specs,
        out_specs=out_specs,
        scratch_shapes=scratch,
        compiler_params=pltpu.CompilerParams(vmem_limit_bytes=vmem * MIB),
        cost_estimate=pl.CostEstimate(flops=0, bytes_accessed=0, transcendentals=0),
    )(*args)


def pack_kernel(tok, seg, out, scr):
    count, feats, width = tok.shape
    lay(scr, tok[...].astype(F32).reshape(count * feats, width))
    row = seg[...].astype(F32)
    for f in range(feats):
        out[f, :count, :] = take(scr, f, count, feats).astype(BF)
        out[f, count:, :] = jnp.zeros((PAD, width), BF)
        out[f, count:, :count] = jnp.broadcast_to(row, (PAD, count)).astype(BF)


def codes(pos, starts):
    cls = jnp.zeros_like(pos)
    for st in starts:
        cls = cls + jnp.where(pos >= st, 1.0, 0.0)
    return jnp.where(cls >= CLASSES - 1, pos + CLASSES, cls)


def tile_range(start_ref, first, size, tile):
    last = first + size - 1
    lo = jnp.int32(0)
    hi = start_ref[1]
    for c in range(1, CLASSES - 1):
        st = start_ref[c]
        lo = jnp.where(first >= st, st, lo)
        hi = jnp.where(last >= st, start_ref[c + 1], hi)
    pad = start_ref[CLASSES - 1]
    lo = jnp.where(first >= pad, first, lo)
    hi = jnp.where(last >= pad, first + size, hi)
    return lo // tile, (hi + tile - 1) // tile


def permute_block(rank_row, first, rows, total):
    pos = iota((rows, LANES), 0) + first.astype(F32)
    parts = []
    for j in range(total // LANES):
        hit = rank_row[0:1, j * LANES : (j + 1) * LANES] == pos
        parts.append(jnp.where(hit, 1.0, 0.0).astype(BF))
    return jnp.concatenate(parts, -1)


def unpermute_block(rank_col, total):
    rows = rank_col.shape[0]
    parts = []
    for j in range(total // LANES):
        pos = iota((1, LANES), 1) + float(j * LANES)
        parts.append(jnp.where(rank_col == pos, 1.0, 0.0).astype(BF))
    return jnp.concatenate(parts, -1)


def fwd_kernel(hpd, hl, r_ref, *refs):
    xparts = refs[:hpd]
    (g1, b1, w_in) = refs[hpd : hpd + 3]
    (o_send, xs_out, ot_out, lse_out, rank_row, rank_col, start_ref) = refs[hpd + 3 : hpd + 10]
    (x_scr, seg_scr, qtz, k_scr, vt, o_scr, code_col, code_row, acc, top, s_scr) = refs[
        hpd + 10 : hpd + 21
    ]
    wqt, wvt = refs[hpd + 21 :]
    feats = xparts[0].shape[0]
    count = xparts[0].shape[1] - PAD
    total = x_scr.shape[0]
    cl = hl * HD
    r = r_ref[0]
    chunks = total // LANES
    wqt[...] = flip(head_columns(w_in, r, cl, 0)) * BF(SCALING)
    wvt[...] = flip(head_columns(w_in, r, cl, 2))

    for s in range(hpd):
        for k in range(feats):
            at = (s * feats + k) * count
            x_scr[at : at + count, :] = xparts[s][k, :count, :]
            row = xparts[s][k, count : count + PAD, :LANES].astype(F32)[0:1]
            col = jnp.transpose(jnp.broadcast_to(row, (LANES, LANES)))
            seg_scr[at : at + count, :] = col[:count, :]

    seg = seg_scr[...]
    cls = jnp.where(seg < 0.0, float(CLASSES - 1), seg)
    seg_scr[...] = cls * 8192.0 + iota((total, LANES), 0)
    key_rows = []
    for j in range(chunks):
        blk = seg_scr[j * LANES : (j + 1) * LANES, :]
        key_rows.append(jnp.transpose(blk)[0:8, :])

    def count_less(i, carry):
        blk = seg_scr[pl.ds(pl.multiple_of(i * 64, 64), 64), :]
        out = []
        for j in range(chunks):
            less = jnp.where(blk < key_rows[j][0:1], 1.0, 0.0)
            out.append(carry[j] + jnp.sum(less.reshape(8, 8, LANES), 0))
        return tuple(out)

    ranks = lax.fori_loop(
        0, total // 64, count_less, tuple(jnp.zeros((8, LANES), F32) for _ in range(chunks))
    )
    for j in range(chunks):
        row = jnp.sum(ranks[j], 0, keepdims=True)
        rank_row[:, j * LANES : (j + 1) * LANES] = jnp.broadcast_to(row, (8, LANES))
        rank_col[j * LANES : (j + 1) * LANES, :] = jnp.transpose(
            jnp.broadcast_to(row, (LANES, LANES))
        )
    starts = []
    keys = jnp.concatenate([k[0:1] for k in key_rows], 0)
    for c in range(1, CLASSES):
        st = jnp.sum(jnp.where(keys < c * 8192.0, 1.0, 0.0))
        starts.append(st)
        start_ref[c] = st.astype(jnp.int32)
    start_ref[0] = jnp.int32(0)
    for c in range(CLASSES, 8):
        start_ref[c] = jnp.int32(total)
    code_col[...] = codes(iota((total, LANES), 0), starts)
    code_row[...] = codes(iota((8, total), 1), starts)

    qtz[...] = jnp.zeros_like(qtz)
    ones = jnp.where(iota((16, total), 0) == 0.0, 1.0, 0.0).astype(BF)
    for h in range(hl):
        vt[h, HD:, :] = ones

    def project(b, _):
        at = pl.multiple_of(b * PB, PB)
        block = dot(permute_block(rank_row, at, PB, total), x_scr[...])
        xs_out[pl.ds(at, PB), :] = block.astype(BF)
        n, _r = ln_parts(block)
        h1 = (n * g1[...] + b1[...]).astype(BF)
        qt = dot_nt(wqt[...], h1).astype(BF)
        k_scr[pl.ds(at, PB), :] = dot(h1, head_columns(w_in, r, cl, 1)).astype(BF)
        vv = dot_nt(wvt[...], h1).astype(BF)
        for h in range(hl):
            sub = (h % 2) * HD
            qtz[h, sub : sub + HD, pl.ds(at, PB)] = qt[h * HD : (h + 1) * HD]
            vt[h, :HD, pl.ds(at, PB)] = vv[h * HD : (h + 1) * HD]
        return 0

    lax.fori_loop(0, total // PB, project, 0)

    def attend(b, _):
        at = pl.multiple_of(b * TQ, TQ)
        t0, t1 = tile_range(start_ref, at, TQ, TK)
        acc[...] = jnp.zeros_like(acc)
        top[...] = jnp.full_like(top, NEGATIVE)
        crow = code_row[0:1, pl.ds(at, TQ)]

        def score(t, _):
            kt = pl.multiple_of(t * TK, TK)
            ccol = code_col[pl.ds(kt, TK), :]
            ccol = jnp.concatenate([ccol] * (TQ // LANES), -1)
            seen = ccol == crow
            for h in range(hl):
                pair = (h // 2) * LANES
                s = dot(k_scr[pl.ds(kt, TK), pair : pair + LANES], qtz[h, :, pl.ds(at, TQ)])
                s = jnp.where(seen, s, NEGATIVE)
                s_scr[h, pl.ds(kt, TK), :] = s
                top[h] = jnp.maximum(top[h], jnp.max(s.reshape(TK // 8, 8, TQ), 0))
            return 0

        lax.fori_loop(t0, t1, score, 0)
        for h in range(hl):
            top[h] = jnp.broadcast_to(jnp.max(top[h], 0, keepdims=True), (8, TQ))

        def mix(t, _):
            kt = pl.multiple_of(t * TK, TK)
            for h in range(hl):
                p = jnp.exp(s_scr[h, pl.ds(kt, TK), :] - top[h, 0:1, :]).astype(BF)
                acc[h] += dot(vt[h, :, pl.ds(kt, TK)], p)
            return 0

        lax.fori_loop(t0, t1, mix, 0)
        outs = []
        for h in range(hl):
            total_h = acc[h, HD : HD + 1, :]
            outs.append(acc[h, :HD, :] / total_h)
            lse_out[h : h + 1, pl.ds(at, TQ)] = top[h, 0:1, :] + jnp.log(total_h)
        ot = jnp.concatenate(outs, 0)
        ot_out[:, pl.ds(at, TQ)] = ot.astype(BF)
        o_scr[pl.ds(at, TQ), :] = jnp.transpose(ot).astype(BF)
        return 0

    lax.fori_loop(0, total // TQ, attend, 0)

    group = feats // 2
    for blk in range(total // (group * count)):
        at = blk * group * count
        hot = unpermute_block(rank_col[at : at + group * count, :], total)
        o = dot(hot, o_scr[...]).astype(BF)
        for j in range(group):
            s, k = divmod(blk * group + j, feats)
            dest = k * hpd + lax.rem(r - s + hpd, hpd)
            o_send[dest] = o[j * count : (j + 1) * count]


def prep_kernel(
    hl,
    r_ref,
    xs,
    g1,
    b1,
    w_in,
    k_out,
    v_out,
    kt_out,
    qtz,
    nt,
    wqt,
    wkt,
):
    total = xs.shape[0]
    cl = hl * HD
    r = r_ref[0]
    wqt[...] = flip(head_columns(w_in, r, cl, 0)) * BF(SCALING)
    wkt[...] = flip(head_columns(w_in, r, cl, 1))
    qtz[...] = jnp.zeros_like(qtz)

    def project(b, _):
        at = pl.multiple_of(b * PB, PB)
        n, _r = ln_parts(xs[pl.ds(at, PB), :].astype(F32))
        h1 = (n * g1[...] + b1[...]).astype(BF)
        nt[:, pl.ds(at, PB)] = jnp.transpose(n.astype(BF))
        qt = dot_nt(wqt[...], h1).astype(BF)
        k_out[pl.ds(at, PB), :] = dot(h1, head_columns(w_in, r, cl, 1)).astype(BF)
        v_out[pl.ds(at, PB), :] = dot(h1, head_columns(w_in, r, cl, 2)).astype(BF)
        kt_out[:, pl.ds(at, PB)] = dot_nt(wkt[...], h1).astype(BF)
        for h in range(hl):
            sub = (h % 2) * HD
            qtz[h, sub : sub + HD, pl.ds(at, PB)] = qt[h * HD : (h + 1) * HD]
        return 0

    lax.fori_loop(0, total // PB, project, 0)


def plus(a, b):
    return (a.astype(F32) + b.astype(F32)).astype(BF)


def first_sums(x_ref, y_ref, a_keep, a_got, c_keep, c_got, a_mine, a_other, c_mine, c_other):
    half = a_mine.shape[1]
    mine = pl.multiple_of(x_ref[0] * half, half)
    other = pl.multiple_of((1 - x_ref[0]) * half, half)

    def step(i, _):
        for ref, first in ((a_mine, mine), (a_other, other)):
            ref[i] = plus(a_keep[i, pl.ds(first, half), :], a_got[i, pl.ds(first, half), :])
        return 0

    lax.fori_loop(0, a_mine.shape[0], step, 0)
    split_y(y_ref[0], c_keep, c_got, c_mine, c_other)


def split_y(y, keep, got, mine, other):
    def step(i, _):
        for ref, at in ((mine, 2 * i + y), (other, 2 * i + 1 - y)):
            ref[i] = plus(keep[at], got[at])
        return 0

    lax.fori_loop(0, mine.shape[0], step, 0)


def top_split(z_ref, keep, got, mine, other):
    chunks = mine.shape[0]
    top = z_ref[0] // chunks
    for j in range(chunks):
        mine[j] = plus(keep[top * chunks + j], got[top * chunks + j])
        other[j] = plus(keep[(1 - top) * chunks + j], got[(1 - top) * chunks + j])


def middle_sums(z_ref, a_keep, a_got, c_keep, c_got, *pieces):
    count = a_keep.shape[0]
    pick_z(z_ref, a_keep, a_got, *pieces[:count])
    for c, ref in enumerate(pieces[count:]):
        at = lax.bitwise_xor(lax.rem(z_ref[0], count // 2), c)
        ref[...] = plus(c_keep[at], c_got[at])


def add_all(terms):
    total = terms[0].astype(F32)
    for term in terms[1:]:
        total = total + term.astype(F32)
    return total.astype(BF)


def pick_y(y_ref, keep, got, mine, other):
    split_y(y_ref[0], keep, got, mine, other)


def pick_z(z_ref, keep, got, *pieces):
    for c, ref in enumerate(pieces):
        at = lax.bitwise_xor(z_ref[0], c)
        ref[...] = plus(keep[at], got[at])


def sum_kernel(*refs):
    refs[-1][...] = add_all([ref[...] for ref in refs[:-1]])


def bwd_kernel(
    hpd,
    hl,
    r_ref,
    start_ref,
    do_recv,
    k_in,
    v_in,
    kt_in,
    qtz,
    ot,
    lse,
    rank_row,
    dt_out,
    do_scr,
    dotz,
    dots,
    code_col,
    code_row,
    dq_acc,
    dk_acc,
    dv_acc,
    p_scr,
    ds_scr,
    pairs,
):
    feats = do_recv.shape[0] // hpd
    count = do_recv.shape[1]
    total = do_scr.shape[0]
    cl = hl * HD
    r = r_ref[0]

    for s in range(hpd):
        for k in range(feats):
            at = (s * feats + k) * count
            do_scr[at : at + count, :] = do_recv[k * hpd + lax.rem(r - s + hpd, hpd)]
    starts = [start_ref[c].astype(F32) for c in range(1, CLASSES)]
    code_col[...] = codes(iota((total, LANES), 0), starts)
    code_row[...] = codes(iota((8, total), 1), starts)
    dotz[...] = jnp.zeros_like(dotz)

    def arrange(b, _):
        at = pl.multiple_of(b * PB, PB)
        block = jnp.transpose(dot(permute_block(rank_row, at, PB, total), do_scr[...]))
        prod = block * ot[:, pl.ds(at, PB)].astype(F32)
        for h in range(hl):
            sub = (h % 2) * HD
            rows = slice(h * HD, (h + 1) * HD)
            dotz[h, sub : sub + HD, pl.ds(at, PB)] = block[rows].astype(BF)
            dots[h : h + 1, pl.ds(at, PB)] = jnp.sum(prod[rows], 0, keepdims=True)
        return 0

    lax.fori_loop(0, total // PB, arrange, 0)
    dq_acc[...] = jnp.zeros_like(dq_acc)
    dk_acc[...] = jnp.zeros_like(dk_acc)
    dv_acc[...] = jnp.zeros_like(dv_acc)

    def list_keys(b, filled):
        t0, t1 = tile_range(start_ref, b * KB, KB, QB)

        def put(t, i):
            pairs[i] = b * 4096 + t
            return i + 1

        return lax.fori_loop(t0, t1, put, filled)

    filled = lax.fori_loop(0, total // KB, list_keys, jnp.int32(0))

    def places(i):
        b, t = pairs[i] // 4096, lax.rem(pairs[i], 4096)
        return pl.ds(pl.multiple_of(b * KB, KB), KB), pl.ds(pl.multiple_of(t * QB, QB), QB)

    def scores(i):
        kt, at = places(i)
        ccol = code_col[kt, :]
        seen = jnp.concatenate([ccol] * (QB // LANES), -1) == code_row[0:1, at]
        for h in range(hl):
            cols = slice(h // 2 * LANES, (h // 2 + 1) * LANES)
            s = dot(k_in[kt, cols], qtz[h, :, at])
            p = jnp.where(seen, jnp.exp(s - lse[h : h + 1, at]), 0.0)
            dp = dot(v_in[kt, cols], dotz[h, :, at])
            p_scr[h] = p.astype(BF)
            ds_scr[h] = (p * (dp - dots[h : h + 1, at])).astype(BF)

    def collect(i):
        kt, at = places(i)
        for h in range(hl):
            rows = slice(h * HD, (h + 1) * HD)
            own = slice((h % 2) * HD, (h % 2 + 1) * HD)
            ds = ds_scr[h]
            dv_acc[rows, kt] += dot_nt(dotz[h, own, at], p_scr[h])
            dk_acc[rows, kt] += dot_nt(qtz[h, own, at], ds)
            dq_acc[rows, at] += dot(kt_in[rows, kt], ds)

    def step(i, _):
        scores(i)
        collect(i)
        return 0

    lax.fori_loop(0, filled, step, 0)
    dt_out[:cl, :] = (dq_acc[...] * SCALING).astype(BF)
    dt_out[cl : 2 * cl, :] = dk_acc[...].astype(BF)
    dt_out[2 * cl :, :] = dv_acc[...].astype(BF)


def dh_kernel(hpd, r_ref, dt, w_in, rank_col, *refs):
    dh_outs, dht = refs[:-1], refs[-1]
    part, count, width = dh_outs[0].shape
    cuts = len(dh_outs) // hpd
    feats = cuts * part
    total = dt.shape[1]
    cl = dt.shape[0] // 3
    w3 = jnp.concatenate([head_columns(w_in, r_ref[0], cl, j) for j in range(3)], 1)
    for b in range(total // PB):
        at = slice(b * PB, (b + 1) * PB)
        dht[:, at] = dot(w3, dt[:, at]).astype(BF)
    group = feats // 2
    for blk in range(total // (group * count)):
        at = blk * group * count
        hot = unpermute_block(rank_col[at : at + group * count, :], total)
        o = dot_nt(hot, dht[...]).astype(BF)
        for j in range(group):
            s, k = divmod(blk * group + j, feats)
            dh_outs[cuts * s + k // part][k % part] = o[j * count : (j + 1) * count]


SUB = 16
CUTS = 4


def q_rows(cl, width):
    return SUB * (-(-6 * cl // width)) + SUB


def dw_kernel(r_ref, x_ref, y_ref, z_ref, dt, nt, w_in, g1, b1, *refs):
    x = x_ref[0]
    width, total = nt.shape
    cols = dt.shape[0]
    cl = cols // 3
    a_keep, a_got, c_keep, c_got, q_keep, q_send, a_mine, a_other, c_mine, c_other = refs[:10]
    m_scr, dw_scr = refs[10:]
    split_y(y_ref[0], a_keep, a_got, a_mine, a_other)
    top_split(z_ref, c_keep, c_got, c_mine, c_other)
    feats = q_keep.shape[0]
    for c in range(3):
        rows = slice(c * cl, (c + 1) * cl)
        m_scr[:, rows] = dot_nt(nt[...], dt[rows, :])
    ones = jnp.ones((8, total), BF)
    sums_row = dot_nt(ones, dt[...])[0:1]
    gcol = jnp.transpose(jnp.broadcast_to(g1[...], (LANES, width)))
    bcol = jnp.transpose(jnp.broadcast_to(b1[...], (LANES, width)))
    gg = jnp.zeros((width, LANES), F32)
    gb = jnp.zeros((width, LANES), F32)
    for j in range(cols // LANES):
        lanes = slice(j * LANES, (j + 1) * LANES)
        first = (j * LANES // cl) * width + r_ref[0] * cl + j * LANES % cl
        w = w_in[:, pl.ds(pl.multiple_of(first, LANES), LANES)].astype(F32)
        m = m_scr[:, lanes]
        gg = gg + w * m
        gb = gb + w * sums_row[:, lanes]
        dw_scr[:, lanes] = (m * gcol + bcol * sums_row[:, lanes]).astype(BF)
    gg = jnp.sum(jnp.transpose(gg), 0, keepdims=True)
    gb = jnp.sum(jnp.transpose(gb), 0, keepdims=True)
    vec = jnp.concatenate([gg, gb, jnp.zeros((SUB - 2, width), F32)], 0).astype(BF)
    per = width // cl
    last = q_keep.shape[1] - SUB
    for e in range(feats):
        for ref, side in ((q_keep, x), (q_send, 1 - x)):
            for s in range(6):
                j, b = divmod(s, 2)
                src = pl.multiple_of((e * 4 + b) * SUB + side * 2 * SUB, SUB)
                to = (s // per) * SUB
                ref[e, to : to + SUB, (s % per) * cl : (s % per + 1) * cl] = dw_scr[
                    pl.ds(src, SUB), j * cl : (j + 1) * cl
                ]
            used = 6 % per
            if used:
                ref[e, last - SUB : last, used * cl :] = jnp.zeros((SUB, width - used * cl), BF)
            ref[e, last:, :] = vec


def gather_kernel(hpd, r_ref, x_ref, *refs):
    same, other = refs[:hpd], refs[hpd : 2 * hpd]
    a_side, a_pair, c_sum, c_pair = refs[2 * hpd : 2 * hpd + 4]
    out, vec, down, up, fqkv, fout, sout, vectors = refs[2 * hpd + 4 :]
    piece = out.shape[0]
    rows, width = same[0].shape
    cl = width // hpd
    r, x = r_ref[0], x_ref[0]
    blocks = piece // SUB
    first = lax.rem(r * blocks, 2)
    from_same = r * blocks // 2 == x
    for s in range(hpd):
        owner = lax.rem(r - s + hpd, hpd)
        for j in range(3):
            lo = 2 * j // hpd * SUB
            to = pl.ds(pl.multiple_of(j * width + owner * cl, LANES), cl)
            for b in range(blocks):
                col = pl.multiple_of((2 * j % hpd + first + b) * cl, LANES)
                at = (slice(lo, lo + SUB), pl.ds(col, cl))
                picked = jnp.where(from_same, same[s][at].astype(F32), other[s][at].astype(F32))
                out[b * SUB : (b + 1) * SUB, to] = picked
    total = same[0][rows - SUB : rows, :].astype(F32)
    for s in range(1, hpd):
        total = total + same[s][rows - SUB : rows, :].astype(F32)
    vec[...] = total[:8]

    down[...] = jnp.where(x == 0, a_side[...].astype(F32), a_pair[...].astype(F32))

    def both(first, size):
        at = slice(first, first + size)
        return c_sum[at, :].astype(F32) + c_pair[at, :].astype(F32)

    for b in range(up.shape[1] // width):
        at = slice(b * piece, (b + 1) * piece)
        block = jnp.where(x == 0, a_pair[at, :].astype(F32), a_side[at, :].astype(F32))
        up[:, b * width : (b + 1) * width] = block
    base = 0
    for ref in (fqkv, fout, sout):
        for b in range(ref.shape[1] // width):
            ref[:, b * width : (b + 1) * width] = both(base, piece)
            base += piece
    vectors[...] = both(base, vectors.shape[0])


def norm_kernel(hpd, *refs):
    parts = refs[:-5]
    x, g1, q_keep, q_got, out = refs[-5:]
    part, count, _w = parts[0].shape
    cuts = len(parts) // hpd
    feats = cuts * part
    for k in range(feats):
        dh = parts[k // part][k % part].astype(F32)
        for s in range(1, hpd):
            dh = dh + parts[cuts * s + k // part][k % part].astype(F32)
        n, r = ln_parts(x[k, :count, :].astype(F32))
        out[k, :count, :] = ln_back(dh, n, r, g1[...]).astype(BF)
        out[k, count:, :] = add_all((q_keep[k], q_got[k]))


def final_kernel(dx1, both, out, q_sum, scr):
    feats = both.shape[0]
    count, _f, width = out.shape
    q_sum[...] = add_all([both[k, count:, :] for k in range(feats)])
    for f in range(feats):
        val = dx1[f * count : (f + 1) * count, :] + both[f, :count, :].astype(F32)
        place(scr, f, count, feats, val)
    out[...] = lift(scr).reshape(count, feats, width)


def rows_kernel(
    hpd,
    me_ref,
    o_recv,
    xt,
    cot_hbm,
    g2,
    b2,
    g3,
    b3,
    ub,
    db,
    wso_hbm,
    wfq_hbm,
    wfo_hbm,
    wup_hbm,
    wdn_hbm,
    *refs,
):
    outs_hbm, scratch = refs[:7], refs[7:-2]
    (wso, wfq, wfo, wup, wdn, cot), scratch = scratch[:6], scratch[6:]
    outs_vmem, scratch = scratch[:7], scratch[7:]
    out, dx1, do_send, a_keep, a_send, b_keep, b_send = outs_vmem
    (
        wide,
        ct,
        o1,
        x1,
        h2,
        qkv,
        o2,
        x2,
        h3,
        u,
        dz,
        dx2,
        do2,
        dqkv,
        pscr,
        tr,
        wblk,
        ubg,
        wdn_scr,
    ) = scratch
    in_sem, out_sem = refs[-2:]
    loads = [
        pltpu.make_async_copy(src, dst, in_sem.at[i])
        for i, (src, dst) in enumerate(
            (
                (cot_hbm, cot),
                (wso_hbm, wso),
                (wfq_hbm, wfq),
                (wfo_hbm, wfo),
                (wup_hbm, wup),
                (wdn_hbm, wdn),
            )
        )
    ]
    for load in loads:
        load.start()
    stores = [
        pltpu.make_async_copy(src, dst, out_sem.at[i])
        for i, (src, dst) in enumerate(zip(outs_vmem, outs_hbm))
    ]
    feats = xt.shape[0]
    count = xt.shape[1] - PAD
    width = xt.shape[2]
    rows = feats * count
    hidden = wup.shape[1]
    n = o_recv.shape[0]
    cl = o_recv.shape[2]
    half = rows // 2
    me = me_ref[0]
    lane = iota((1, LANES), 1)
    part = 16
    tiles = count // part
    size = feats * part

    loads[0].wait()
    lay(wide, cot[...].astype(F32).reshape(rows, width))
    for f in range(feats):
        ct[f * count : (f + 1) * count, :] = take(wide, f, count, feats).astype(BF)
        for c in range(hpd):
            o1[f * count : (f + 1) * count, c * cl : (c + 1) * cl] = o_recv[f * hpd + c]

    loads[1].wait()
    for b in range(2):
        at = slice(b * half, (b + 1) * half)
        x = xt[b * feats // 2 : (b + 1) * feats // 2, :count, :].astype(F32).reshape(half, width)
        v = x + dot(o1[at, :], wso[...])
        x1[at, :] = v
        nn, _r = ln_parts(v)
        h2[at, :] = (nn * g2[...] + b2[...]).astype(BF)

    loads[2].wait()
    qkv3 = qkv

    def qkv_step(c, _):
        cols = pl.ds(pl.multiple_of(c * TILE, TILE), TILE)
        scale = jnp.where(c < width // TILE, SCALING, 1.0)
        y = dot(h2[...], wfq[:, cols])
        qkv3[:, :, cols] = (y * scale).astype(BF).reshape(feats, count, TILE)
        return 0

    lax.fori_loop(0, 3 * width // TILE, qkv_step, 0)

    ri = lax.broadcasted_iota(jnp.int32, (2 * size, size), 0)
    ci = lax.broadcasted_iota(jnp.int32, (2 * size, size), 1)
    same = lax.rem(ri, part) == lax.rem(ci, part)
    low_lane = jnp.where(iota((1, LANES), 1) < HD, 1.0, 0.0).astype(BF)
    high_lane = jnp.where(iota((1, LANES), 1) < HD, 0.0, 1.0).astype(BF)

    def tile_of(ref, at, lo):
        return ref[:, at, lo : lo + LANES].reshape(size, LANES)

    def by_head(v):
        return jnp.concatenate([v * low_lane, v * high_lane], 0)

    def by_head_t(v):
        vt = jnp.transpose(v)
        zero = jnp.zeros((HD, size), BF)
        return jnp.concatenate(
            [jnp.concatenate([vt[:HD], zero], 0), jnp.concatenate([zero, vt[HD:]], 0)], 1
        )

    def side(v):
        return jnp.concatenate([v[:size], v[size:]], 1)

    def per_head(v, fn):
        return jnp.concatenate(
            [jnp.broadcast_to(fn(v[i * size : (i + 1) * size]), (size, size)) for i in (0, 1)], 0
        )

    def feat_fwd(t, _):
        at = pl.ds(pl.multiple_of(t * part, part), part)
        for p2 in range(H // 2):
            lo = p2 * LANES
            q = tile_of(qkv3, at, lo)
            k = tile_of(qkv3, at, width + lo)
            v = tile_of(qkv3, at, 2 * width + lo)
            s = jnp.where(same, dot_nt(by_head(k), q), NEGATIVE)
            e = jnp.exp(s - per_head(s, lambda w: jnp.max(w, 0, keepdims=True)))
            p = (e * per_head(e, lambda w: 1.0 / jnp.sum(w, 0, keepdims=True))).astype(BF)
            pscr[t, p2] = p
            ot = dot(by_head_t(v), p)
            o2[:, at, lo : lo + LANES] = jnp.transpose(ot).astype(BF).reshape(feats, part, LANES)
        return 0

    lax.fori_loop(0, tiles, feat_fwd, 0, unroll=True)

    loads[3].wait()
    for b in range(2):
        at = slice(b * half, (b + 1) * half)
        o = o2[b * feats // 2 : (b + 1) * feats // 2, :, :].reshape(half, width)
        v = x1[at, :] + dot(o, wfo[...])
        x2[at, :] = v
        nn, _r = ln_parts(v)
        h3[at, :] = (nn * g3[...] + b3[...]).astype(BF)

    loads[4].wait()
    loads[5].wait()

    def ffn(c, _):
        cols = pl.ds(pl.multiple_of(c * FT, FT), FT)
        total = jnp.zeros((8, FT), F32)
        for b in range(2):
            at = slice(b * half, (b + 1) * half)
            z = dot(h3[at, :], wup[:, cols]) + ub[0:1, cols]
            w = GELU_C * GELU_A * (z * z) + GELU_C
            cdf = 0.5 * jnp.tanh(z * w) + 0.5
            g = z * cdf
            u[at, cols] = g.astype(BF)
            slope = cdf + g * (1.0 - cdf) * (6.0 * w - 4.0 * GELU_C)
            d = dot_nt(ct[at, :], wdn[cols, :]) * slope
            dz[at, cols] = d.astype(BF)
            total = total + jnp.sum(d.reshape(half // 8, 8, FT), 0)
        ubg[:, cols] = total
        return 0

    lax.fori_loop(0, hidden // FT, ffn, 0)

    vectors = []
    gg = jnp.zeros((1, width), F32)
    gb = jnp.zeros((1, width), F32)
    gd = jnp.zeros((1, width), F32)
    for b in range(2):
        at = slice(b * half, (b + 1) * half)
        y = x2[at, :] + dot(u[at, :], wdn[...]) + db[...]
        for j in range(feats // 2):
            f = b * (feats // 2) + j
            place(wide, f, count, feats, y[j * count : (j + 1) * count])
        dh = dot_nt(dz[at, :], wup[...])
        nn, r = ln_parts(x2[at, :])
        c = ct[at, :].astype(F32)
        gg = gg + jnp.sum(dh * nn, 0, keepdims=True)
        gb = gb + jnp.sum(dh, 0, keepdims=True)
        gd = gd + jnp.sum(c, 0, keepdims=True)
        v = c + ln_back(dh, nn, r, g3[...])
        dx2[at, :] = v
        do2[b * feats // 2 : (b + 1) * feats // 2, :, :] = (
            dot_nt(v.astype(BF), wfo[...]).astype(BF).reshape(feats // 2, count, width)
        )
    out[...] = lift(wide).reshape(count, feats, width).astype(BF)
    stores[0].start()
    vectors = [gg, gb, gd]

    core = lax.rem(me, 2)

    def slot(pos):
        at, other = divmod(pos, 2)
        refs = (a_send, b_send) if other else (a_keep, b_keep)
        return refs, at, 2 * at + (1 - core if other else core)

    piece = width // n
    fpiece = hidden // n

    def spread(group, base):
        for pos in range(n):
            refs, at, d = slot(pos)
            src = pl.multiple_of(d * piece, piece)
            refs[group][at, base : base + piece, :] = wblk[pl.ds(src, piece), :]

    base = 0
    for b in range(hidden // width):
        tr[...] = flip(u[:, b * width : (b + 1) * width])
        wdn_scr[b * width : (b + 1) * width, :] = dot(tr[...], ct[...]).astype(BF)
    for pos in range(n):
        refs, at, d = slot(pos)
        src = pl.multiple_of(d * fpiece, fpiece)
        refs[0][at, base : base + fpiece, :] = wdn_scr[pl.ds(src, fpiece), :]
    base += fpiece
    tr[...] = flip(h3[...])
    for b in range(hidden // width):
        wblk[...] = dot(tr[...], dz[:, b * width : (b + 1) * width]).astype(BF)
        spread(0, base)
        base += piece
    stores[3].start()
    stores[4].start()

    def feat_bwd(t, _):
        at = pl.ds(pl.multiple_of(t * part, part), part)
        for p2 in range(H // 2):
            lo = p2 * LANES
            q = tile_of(qkv3, at, lo)
            k = tile_of(qkv3, at, width + lo)
            v = tile_of(qkv3, at, 2 * width + lo)
            g = tile_of(do2, at, lo)
            p = pscr[t, p2]
            pf = p.astype(F32)
            dp = dot_nt(by_head(v), g)
            ds = pf * (dp - per_head(pf * dp, lambda w: jnp.sum(w, 0, keepdims=True)))
            ds = ds.astype(BF)
            dv = dot(side(p), by_head(g))
            dk = dot(side(ds), by_head(q))
            dq = jnp.transpose(dot(by_head_t(k), ds)) * SCALING
            for j, d in enumerate((dq, dk, dv)):
                dqkv[:, at, j * width + lo : j * width + lo + LANES] = d.astype(BF).reshape(
                    feats, part, LANES
                )
        return 0

    lax.fori_loop(0, tiles, feat_bwd, 0, unroll=True)

    gg = jnp.zeros((1, width), F32)
    gb = jnp.zeros((1, width), F32)
    for b in range(2):
        at = slice(b * half, (b + 1) * half)
        d = dqkv[b * feats // 2 : (b + 1) * feats // 2, :, :].reshape(half, 3 * width)
        dh = dot_nt(d, wfq[...])
        nn, r = ln_parts(x1[at, :])
        gg = gg + jnp.sum(dh * nn, 0, keepdims=True)
        gb = gb + jnp.sum(dh, 0, keepdims=True)
        v = dx2[at, :] + ln_back(dh, nn, r, g2[...])
        dx1[at, :] = v
        g = dot_nt(v.astype(BF), wso[...]).astype(BF)
        for j in range(feats // 2):
            f = b * (feats // 2) + j
            for c in range(hpd):
                do_send[f * hpd + c] = g[j * count : (j + 1) * count, c * cl : (c + 1) * cl]
    stores[1].start()
    stores[2].start()
    vectors = [gg, gb] + vectors

    base = 0
    tr[...] = flip(h2[...])
    for b in range(3):
        d = dqkv[:, :, b * width : (b + 1) * width].reshape(rows, width)
        wblk[...] = dot(tr[...], d).astype(BF)
        spread(1, base)
        base += piece
    tr[...] = flip(o2[...].reshape(rows, width))
    wblk[...] = dot(tr[...], dx2[...].astype(BF)).astype(BF)
    spread(1, base)
    base += piece
    tr[...] = flip(o1[...])
    wblk[...] = dot(tr[...], dx1[...].astype(BF)).astype(BF)
    spread(1, base)
    base += piece
    ubs = jnp.sum(ubg[...], 0, keepdims=True)
    vectors = vectors + [ubs[:, b * width : (b + 1) * width] for b in range(hidden // width)]
    vec = jnp.concatenate(vectors + [jnp.zeros((16 - len(vectors), width), F32)], 0).astype(BF)
    for pos in range(n):
        refs, at, _d = slot(pos)
        refs[1][at, base : base + 16, :] = vec
    stores[5].start()
    stores[6].start()
    for store in stores:
        store.wait()


def solution(mesh):
    n = mesh.shape["samp"]
    groups = mesh.shape["grp"]
    gbits = groups.bit_length() - 1
    tie = lax.optimization_barrier
    swap_core = [(d, d ^ 1) for d in range(n)]
    swap_y = [(d, d ^ 2) for d in range(n)]
    same_core = [[2 * k + c for k in range(n // 2)] for c in (0, 1)]

    def swap_grp(v, bit=0):
        return lax.ppermute(v, "grp", [(d, d ^ (1 << bit)) for d in range(groups)])

    def rest_of_grp(v):
        for bit in range(1, gbits):
            v = (v.astype(F32) + swap_grp(v, bit).astype(F32)).astype(BF)
        return v

    def body(
        tokens,
        segments,
        cotangent,
        first_gain,
        first_shift,
        sample_qkv,
        sample_out,
        second_gain,
        second_shift,
        feature_qkv,
        feature_out,
        third_gain,
        third_shift,
        up_weight,
        up_bias,
        down_weight,
        down_bias,
    ):
        count, feats, width = tokens.shape[1:]
        hidden = up_weight.shape[1]
        rows = count * feats
        hpd = n // feats
        hl = H // hpd
        cl = hl * HD
        total = n * count
        heads8 = 8
        me = lax.axis_index("samp")
        r = lax.rem(me, hpd)
        x = lax.rem(lax.axis_index("grp"), 2)
        y, z = (me >> 1) & 1, me >> 2
        r1, me1, x1, y1, z1 = (v.reshape(1).astype(jnp.int32) for v in (r, me, x, y, z))
        peers = [[q + hpd * k for k in range(feats)] for q in range(hpd)]
        g1, b1, g2, b2, g3, b3, ub, db = (
            v.reshape(1, -1)
            for v in (
                first_gain,
                first_shift,
                second_gain,
                second_shift,
                third_gain,
                third_shift,
                up_bias,
                down_bias,
            )
        )

        def shift(s):
            return [(d, d // hpd * hpd + (d % hpd + s) % hpd) for d in range(n)]

        (xt,) = call(
            pack_kernel,
            [((feats, count + PAD, width), BF)],
            [pltpu.VMEM((width // LANES, rows, LANES), F32)],
            tokens[0],
            segments,
        )
        mine = lax.all_to_all(xt, "samp", 0, 0, tiled=True, axis_index_groups=peers)
        xparts = [mine] + [lax.ppermute(mine, "samp", shift(s)) for s in range(1, hpd)]

        o_send, xs, ot, lse, rank_row, rank_col, starts = call(
            functools.partial(fwd_kernel, hpd, hl),
            [
                ((n, count, cl), BF),
                ((total, width), BF),
                ((cl, total), BF),
                ((heads8, total), F32),
                ((8, total), F32),
                ((total, LANES), F32),
                ((8,), jnp.int32),
            ],
            [
                pltpu.VMEM((total, width), BF),
                pltpu.VMEM((total, LANES), F32),
                pltpu.VMEM((hl, LANES, total), BF),
                pltpu.VMEM((total, cl), BF),
                pltpu.VMEM((hl, HD + 16, total), BF),
                pltpu.VMEM((total, cl), BF),
                pltpu.VMEM((total, LANES), F32),
                pltpu.VMEM((8, total), F32),
                pltpu.VMEM((hl, HD + 16, TQ), F32),
                pltpu.VMEM((hl, 8, TQ), F32),
                pltpu.VMEM((hl, total, TQ), F32),
                pltpu.VMEM((cl, width), BF),
                pltpu.VMEM((cl, width), BF),
            ],
            r1,
            *xparts,
            g1,
            b1,
            sample_qkv,
            smem=(0,),
            smem_out=(6,),
            vmem=28,
        )
        o_recv = lax.all_to_all(o_send, "samp", 0, 0, tiled=True)

        piece = width // n
        fpiece = hidden // n
        apieces = fpiece + piece * (hidden // width)
        bpieces = piece * 5 + 16
        vm = pltpu.VMEM
        out, dx1, do_send, a_keep, a_send, b_keep, b_send = call(
            functools.partial(rows_kernel, hpd),
            [
                ((count, feats, width), BF),
                ((rows, width), F32),
                ((n, count, cl), BF),
                ((n // 2, apieces, width), BF),
                ((n // 2, apieces, width), BF),
                ((n // 2, bpieces, width), BF),
                ((n // 2, bpieces, width), BF),
            ],
            [
                vm((width, width), BF),
                vm((width, 3 * width), BF),
                vm((width, width), BF),
                vm((width, hidden), BF),
                vm((hidden, width), BF),
                vm((count, feats, width), BF),
                vm((count, feats, width), BF),
                vm((rows, width), F32),
                vm((n, count, cl), BF),
                vm((n // 2, apieces, width), BF),
                vm((n // 2, apieces, width), BF),
                vm((n // 2, bpieces, width), BF),
                vm((n // 2, bpieces, width), BF),
                vm((width // LANES, rows, LANES), F32),
                vm((rows, width), BF),
                vm((rows, width), BF),
                vm((rows, width), F32),
                vm((rows, width), BF),
                vm((feats, count, 3 * width), BF),
                vm((feats, count, width), BF),
                vm((rows, width), F32),
                vm((rows, width), BF),
                vm((rows, hidden), BF),
                vm((rows, hidden), BF),
                vm((rows, width), F32),
                vm((feats, count, width), BF),
                vm((feats, count, 3 * width), BF),
                vm((count // 16, H // 2, 32 * feats, 16 * feats), BF),
                vm((width, rows), BF),
                vm((width, width), BF),
                vm((8, hidden), F32),
                vm((hidden, width), BF),
                pltpu.SemaphoreType.DMA((6,)),
                pltpu.SemaphoreType.DMA((7,)),
            ],
            me1,
            o_recv,
            xt,
            cotangent[0],
            g2,
            b2,
            g3,
            b3,
            ub,
            db,
            sample_out,
            feature_qkv,
            feature_out,
            up_weight,
            down_weight,
            smem=(0,),
            hbm=(3, 10, 11, 12, 13, 14),
            hbm_out=tuple(range(7)),
            vmem=48,
        )
        a_got = lax.ppermute(a_send, "samp", swap_core)
        b_got = lax.ppermute(b_send, "samp", swap_core)
        do_recv = lax.all_to_all(do_send, "samp", 0, 0, tiled=True)

        qr = q_rows(cl, width)
        half = apieces // 2
        zs = n // 4

        def along_z(pieces, unit):
            return [pieces[0]] + [
                lax.ppermute(pieces[c], "samp", [(d, d ^ (unit * c)) for d in range(n)])
                for c in range(1, len(pieces))
            ]

        am, ao, cm, co = call(
            first_sums,
            [((n // 2, half, width), BF)] * 2 + [((n // 4, bpieces, width), BF)] * 2,
            [],
            x1,
            y1,
            a_keep,
            a_got,
            b_keep,
            b_got,
            smem=(0, 1),
            vmem=16,
        )
        ag, cg = swap_grp(ao), lax.ppermute(co, "samp", swap_y)
        xs_after, _ = tie((xs, am))
        k_all, v_all, kt_all, qtz, nt = call(
            functools.partial(prep_kernel, hl),
            [
                ((total, cl), BF),
                ((total, cl), BF),
                ((cl, total), BF),
                ((hl, LANES, total), BF),
                ((width, total), BF),
            ],
            [vm((cl, width), BF), vm((cl, width), BF)],
            r1,
            xs_after,
            g1,
            b1,
            sample_qkv,
            smem=(0,),
            vmem=16,
        )
        (dt,) = call(
            functools.partial(bwd_kernel, hpd, hl),
            [((3 * cl, total), BF)],
            [
                vm((total, cl), BF),
                vm((hl, LANES, total), BF),
                vm((8, total), F32),
                vm((total, LANES), F32),
                vm((8, total), F32),
                vm((cl, total), F32),
                vm((cl, total), F32),
                vm((cl, total), F32),
                vm((hl, KB, QB), BF),
                vm((hl, KB, QB), BF),
                pltpu.SMEM(((total // KB) * (total // QB),), jnp.int32),
            ],
            r1,
            starts,
            do_recv,
            k_all,
            v_all,
            kt_all,
            qtz,
            ot,
            lse,
            rank_row,
            smem=(0, 1),
            vmem=58,
        )
        am, ag, cm, cg, _ = tie((am, ag, cm, cg, dt))
        q_keep, q_send, am, ao, cm, co = call(
            dw_kernel,
            [((feats, qr, width), BF)] * 2
            + [((n // 4, half, width), BF)] * 2
            + [((zs // 2, bpieces, width), BF)] * 2,
            [vm((width, 3 * cl), F32), vm((width, 3 * cl), BF)],
            r1,
            x1,
            y1,
            z1,
            dt,
            nt,
            sample_qkv,
            g1,
            b1,
            am,
            ag,
            cm,
            cg,
            smem=(0, 1, 2, 3),
            vmem=16,
        )
        ag = lax.ppermute(ao, "samp", swap_y)
        cg = lax.ppermute(co, "samp", [(d, d ^ (n // 2)) for d in range(n)])
        dt, _ = tie((dt, q_send))
        dhs = call(
            functools.partial(dh_kernel, hpd),
            [((feats // CUTS, count, width), BF)] * (CUTS * hpd),
            [vm((width, total), BF)],
            r1,
            dt,
            sample_qkv,
            rank_col,
            smem=(0,),
            vmem=16,
        )
        parts = list(dhs[:CUTS])
        for s in range(1, hpd):
            parts += [lax.ppermute(v, "samp", shift(-s)) for v in dhs[CUTS * s : CUTS * s + CUTS]]
        pieces = call(
            middle_sums,
            [((half, width), BF)] * zs + [((bpieces, width), BF)] * (zs // 2),
            [],
            z1,
            am,
            ag,
            cm,
            cg,
            smem=(0,),
        )
        parts[0], _ = tie((parts[0], pieces[0]))
        a_pieces, c_pieces = along_z(pieces[:zs], 4), along_z(pieces[zs:], 4)
        (both,) = call(
            functools.partial(norm_kernel, hpd),
            [((feats, count + qr, width), BF)],
            [],
            *parts,
            mine,
            g1,
            q_keep,
            swap_grp(q_send),
            vmem=10,
        )
        both_send, *ends = tie((both, *a_pieces, *c_pieces))
        a_pieces, c_pieces = ends[:zs], ends[zs:]
        both = lax.all_to_all(both_send, "samp", 0, 0, tiled=True, axis_index_groups=peers)

        def last_steps(*pieces):
            (c_sum,) = call(sum_kernel, [((bpieces, width), BF)], [], *pieces[zs:])
            c_sum = rest_of_grp(c_sum)
            (a_side,) = call(sum_kernel, [((half, width), BF)], [], *pieces[:zs])
            a_side = rest_of_grp(a_side)
            return a_side, swap_grp(a_side), c_sum, swap_grp(c_sum)

        terms = (*a_pieces, *c_pieces)
        parts_summed = last_steps(*tie((*terms, both_send))[: len(terms)])
        grad_tokens, q_sum = call(
            final_kernel,
            [((count, feats, width), F32), ((qr, width), BF)],
            [vm((width // LANES, rows, LANES), F32)],
            dx1,
            both,
            vmem=12,
        )
        q_sum = rest_of_grp(q_sum)

        def from_peer(s, other):
            if not s and not other:
                return q_sum
            pairs = [
                (g * n + d, (g ^ other) * n + e) for g in range(groups) for d, e in shift(s)
            ]
            return lax.ppermute(q_sum, ("grp", "samp"), pairs)

        peers_same = [from_peer(s, 0) for s in range(hpd)]
        peers_other = [from_peer(s, 1) for s in range(hpd)]
        grad_sample_qkv, vec_sum, grad_down, grad_up, grad_fqkv, grad_fout, grad_sout, vu = call(
            functools.partial(gather_kernel, hpd),
            [
                ((piece, 3 * width), F32),
                ((8, width), F32),
                ((fpiece, width), F32),
                ((piece, hidden), F32),
                ((piece, 3 * width), F32),
                ((piece, width), F32),
                ((piece, width), F32),
                ((16, width), F32),
            ],
            [],
            r1,
            x1,
            *peers_same,
            *peers_other,
            *parts_summed,
            smem=(0, 1),
        )

        def own(v):
            return lax.dynamic_slice_in_dim(v, me * (v.shape[0] // n), v.shape[0] // n, 0)

        def own_rows(v):
            return lax.dynamic_slice_in_dim(v, me * piece, piece, 1)

        five = own_rows(vu[:5])
        two = own_rows(vec_sum[:2])
        vectors = [five[i] for i in range(5)]
        vectors.append(own(vu[5 : 5 + hidden // width].reshape(-1)))
        return (
            out[None],
            grad_tokens[None],
            two[0],
            two[1],
            grad_sample_qkv,
            grad_sout,
            vectors[0],
            vectors[1],
            grad_fqkv,
            grad_fout,
            vectors[2],
            vectors[3],
            grad_up,
            vectors[5],
            grad_down,
            vectors[4],
        )

    rep = P()
    data = P("grp", "samp", None, None)
    line = P("samp")
    flat = P("samp", None)
    in_specs = (data, P("grp", "samp"), data) + (rep,) * 14
    out_specs = (
        data,
        data,
        line,
        line,
        flat,
        flat,
        line,
        line,
        flat,
        flat,
        line,
        line,
        flat,
        line,
        flat,
        line,
    )
    return jax.shard_map(body, mesh=mesh, in_specs=in_specs, out_specs=out_specs, check_vma=False)
```

```python
import functools
import math

import jax
import jax.numpy as jnp
from jax import lax
from jax.experimental import pallas as pl
from jax.experimental.pallas import tpu as pltpu
from jax.sharding import PartitionSpec as P

H = 8
HD = 64
EPSILON = 1e-05
SCALING = 0.125
NEGATIVE = -1e30
BF = jnp.bfloat16
F32 = jnp.float32
TILE = 256
FT = 512
PB = 512
KB = 256
QB = 256
TQ = 256
TK = 256
LANES = 128
PAD = 8
GELU_C = math.sqrt(2.0 / math.pi)
GELU_A = 0.044715
MIB = 1024 * 1024
CLASSES = 5


def dot(a, b):
    return jnp.dot(a, b, preferred_element_type=F32)


def dot_nt(a, b):
    return lax.dot_general(a, b, (((1,), (1,)), ((), ())), preferred_element_type=F32)


def dot_tn(a, b):
    return lax.dot_general(a, b, (((0,), (0,)), ((), ())), preferred_element_type=F32)


def ln_parts(v):
    c = v - jnp.mean(v, -1, keepdims=True)
    r = lax.rsqrt(jnp.mean(c * c, -1, keepdims=True) + EPSILON)
    return c * r, r


def ln_back(dh, n, r, g):
    e = dh * g
    return r * (e - jnp.mean(e, -1, keepdims=True) - n * jnp.mean(e * n, -1, keepdims=True))


def flip(v):
    return jnp.transpose(v)


def head_columns(w, r, cl, which):
    first = which * (w.shape[1] // 3) + r * cl
    return w[:, pl.ds(pl.multiple_of(first, LANES), cl)]


def lay(scr, v):
    for a in range(scr.shape[0]):
        scr[a] = v[:, a * LANES : (a + 1) * LANES]


def lift(scr):
    return jnp.concatenate([scr[a] for a in range(scr.shape[0])], -1)


def take(scr, first, count, step):
    return jnp.concatenate(
        [scr[a, pl.ds(first, count, stride=step), :] for a in range(scr.shape[0])], -1
    )


def place(scr, first, count, step, v):
    for a in range(scr.shape[0]):
        scr[a, pl.ds(first, count, stride=step), :] = v[:, a * LANES : (a + 1) * LANES]


def iota(shape, dim):
    return lax.broadcasted_iota(jnp.int32, shape, dim).astype(F32)


def call(fn, outs, scratch, *args, smem=(), smem_out=(), hbm=(), hbm_out=(), vmem=16):
    def spec(space):
        return pl.BlockSpec(memory_space=space)

    def place_of(i, scalars, far):
        return spec(pltpu.SMEM if i in scalars else pl.ANY if i in far else pltpu.VMEM)

    in_specs = [place_of(i, smem, hbm) for i in range(len(args))]
    out_specs = [place_of(i, smem_out, hbm_out) for i in range(len(outs))]
    return pl.pallas_call(
        fn,
        out_shape=[jax.ShapeDtypeStruct(*o) for o in outs],
        in_specs=in_specs,
        out_specs=out_specs,
        scratch_shapes=scratch,
        compiler_params=pltpu.CompilerParams(vmem_limit_bytes=vmem * MIB),
        cost_estimate=pl.CostEstimate(flops=0, bytes_accessed=0, transcendentals=0),
    )(*args)


def pack_kernel(tok, seg, out, scr):
    count, feats, width = tok.shape
    lay(scr, tok[...].astype(F32).reshape(count * feats, width))
    row = seg[...].astype(F32)
    for f in range(feats):
        out[f, :count, :] = take(scr, f, count, feats).astype(BF)
        out[f, count:, :] = jnp.zeros((PAD, width), BF)
        out[f, count:, :count] = jnp.broadcast_to(row, (PAD, count)).astype(BF)


def codes(pos, starts):
    cls = jnp.zeros_like(pos)
    for st in starts:
        cls = cls + jnp.where(pos >= st, 1.0, 0.0)
    return jnp.where(cls >= CLASSES - 1, pos + CLASSES, cls)


def tile_range(start_ref, first, size, tile):
    last = first + size - 1
    lo = jnp.int32(0)
    hi = start_ref[1]
    for c in range(1, CLASSES - 1):
        st = start_ref[c]
        lo = jnp.where(first >= st, st, lo)
        hi = jnp.where(last >= st, start_ref[c + 1], hi)
    pad = start_ref[CLASSES - 1]
    lo = jnp.where(first >= pad, first, lo)
    hi = jnp.where(last >= pad, first + size, hi)
    return lo // tile, (hi + tile - 1) // tile


def permute_block(rank_row, first, rows, total):
    pos = iota((rows, LANES), 0) + first.astype(F32)
    parts = []
    for j in range(total // LANES):
        hit = rank_row[0:1, j * LANES : (j + 1) * LANES] == pos
        parts.append(jnp.where(hit, 1.0, 0.0).astype(BF))
    return jnp.concatenate(parts, -1)


def unpermute_block(rank_col, total):
    rows = rank_col.shape[0]
    parts = []
    for j in range(total // LANES):
        pos = iota((1, LANES), 1) + float(j * LANES)
        parts.append(jnp.where(rank_col == pos, 1.0, 0.0).astype(BF))
    return jnp.concatenate(parts, -1)


def fwd_kernel(hpd, hl, r_ref, *refs):
    xparts = refs[:hpd]
    (g1, b1, w_in) = refs[hpd : hpd + 3]
    (o_send, xs_out, ot_out, lse_out, rank_row, rank_col, start_ref) = refs[hpd + 3 : hpd + 10]
    (x_scr, seg_scr, qtz, k_scr, vt, o_scr, code_col, code_row, acc, top, s_scr) = refs[
        hpd + 10 : hpd + 21
    ]
    wqt, wvt = refs[hpd + 21 :]
    feats = xparts[0].shape[0]
    count = xparts[0].shape[1] - PAD
    total = x_scr.shape[0]
    cl = hl * HD
    r = r_ref[0]
    chunks = total // LANES
    wqt[...] = flip(head_columns(w_in, r, cl, 0)) * BF(SCALING)
    wvt[...] = flip(head_columns(w_in, r, cl, 2))

    for s in range(hpd):
        for k in range(feats):
            at = (s * feats + k) * count
            x_scr[at : at + count, :] = xparts[s][k, :count, :]
            row = xparts[s][k, count : count + PAD, :LANES].astype(F32)[0:1]
            col = jnp.transpose(jnp.broadcast_to(row, (LANES, LANES)))
            seg_scr[at : at + count, :] = col[:count, :]

    seg = seg_scr[...]
    cls = jnp.where(seg < 0.0, float(CLASSES - 1), seg)
    seg_scr[...] = cls * 8192.0 + iota((total, LANES), 0)
    key_rows = []
    for j in range(chunks):
        blk = seg_scr[j * LANES : (j + 1) * LANES, :]
        key_rows.append(jnp.transpose(blk)[0:8, :])

    def count_less(i, carry):
        blk = seg_scr[pl.ds(pl.multiple_of(i * 64, 64), 64), :]
        out = []
        for j in range(chunks):
            less = jnp.where(blk < key_rows[j][0:1], 1.0, 0.0)
            out.append(carry[j] + jnp.sum(less.reshape(8, 8, LANES), 0))
        return tuple(out)

    ranks = lax.fori_loop(
        0, total // 64, count_less, tuple(jnp.zeros((8, LANES), F32) for _ in range(chunks))
    )
    for j in range(chunks):
        row = jnp.sum(ranks[j], 0, keepdims=True)
        rank_row[:, j * LANES : (j + 1) * LANES] = jnp.broadcast_to(row, (8, LANES))
        rank_col[j * LANES : (j + 1) * LANES, :] = jnp.transpose(
            jnp.broadcast_to(row, (LANES, LANES))
        )
    starts = []
    keys = jnp.concatenate([k[0:1] for k in key_rows], 0)
    for c in range(1, CLASSES):
        st = jnp.sum(jnp.where(keys < c * 8192.0, 1.0, 0.0))
        starts.append(st)
        start_ref[c] = st.astype(jnp.int32)
    start_ref[0] = jnp.int32(0)
    for c in range(CLASSES, 8):
        start_ref[c] = jnp.int32(total)
    code_col[...] = codes(iota((total, LANES), 0), starts)
    code_row[...] = codes(iota((8, total), 1), starts)

    qtz[...] = jnp.zeros_like(qtz)
    ones = jnp.where(iota((16, total), 0) == 0.0, 1.0, 0.0).astype(BF)
    for h in range(hl):
        vt[h, HD:, :] = ones

    def project(b, _):
        at = pl.multiple_of(b * PB, PB)
        block = dot(permute_block(rank_row, at, PB, total), x_scr[...])
        xs_out[pl.ds(at, PB), :] = block.astype(BF)
        n, _r = ln_parts(block)
        h1 = (n * g1[...] + b1[...]).astype(BF)
        qt = dot_nt(wqt[...], h1).astype(BF)
        k_scr[pl.ds(at, PB), :] = dot(h1, head_columns(w_in, r, cl, 1)).astype(BF)
        vv = dot_nt(wvt[...], h1).astype(BF)
        for h in range(hl):
            sub = (h % 2) * HD
            qtz[h, sub : sub + HD, pl.ds(at, PB)] = qt[h * HD : (h + 1) * HD]
            vt[h, :HD, pl.ds(at, PB)] = vv[h * HD : (h + 1) * HD]
        return 0

    lax.fori_loop(0, total // PB, project, 0)

    def attend(b, _):
        at = pl.multiple_of(b * TQ, TQ)
        t0, t1 = tile_range(start_ref, at, TQ, TK)
        acc[...] = jnp.zeros_like(acc)
        top[...] = jnp.full_like(top, NEGATIVE)
        crow = code_row[0:1, pl.ds(at, TQ)]

        def score(t, _):
            kt = pl.multiple_of(t * TK, TK)
            ccol = code_col[pl.ds(kt, TK), :]
            ccol = jnp.concatenate([ccol] * (TQ // LANES), -1)
            seen = ccol == crow
            for h in range(hl):
                pair = (h // 2) * LANES
                s = dot(k_scr[pl.ds(kt, TK), pair : pair + LANES], qtz[h, :, pl.ds(at, TQ)])
                s = jnp.where(seen, s, NEGATIVE)
                s_scr[h, pl.ds(kt, TK), :] = s
                top[h] = jnp.maximum(top[h], jnp.max(s.reshape(TK // 8, 8, TQ), 0))
            return 0

        lax.fori_loop(t0, t1, score, 0)
        for h in range(hl):
            top[h] = jnp.broadcast_to(jnp.max(top[h], 0, keepdims=True), (8, TQ))

        def mix(t, _):
            kt = pl.multiple_of(t * TK, TK)
            for h in range(hl):
                p = jnp.exp(s_scr[h, pl.ds(kt, TK), :] - top[h, 0:1, :]).astype(BF)
                acc[h] += dot(vt[h, :, pl.ds(kt, TK)], p)
            return 0

        lax.fori_loop(t0, t1, mix, 0)
        outs = []
        for h in range(hl):
            total_h = acc[h, HD : HD + 1, :]
            outs.append(acc[h, :HD, :] / total_h)
            lse_out[h : h + 1, pl.ds(at, TQ)] = top[h, 0:1, :] + jnp.log(total_h)
        ot = jnp.concatenate(outs, 0)
        ot_out[:, pl.ds(at, TQ)] = ot.astype(BF)
        o_scr[pl.ds(at, TQ), :] = jnp.transpose(ot).astype(BF)
        return 0

    lax.fori_loop(0, total // TQ, attend, 0)

    group = feats // 2
    for blk in range(total // (group * count)):
        at = blk * group * count
        hot = unpermute_block(rank_col[at : at + group * count, :], total)
        o = dot(hot, o_scr[...]).astype(BF)
        for j in range(group):
            s, k = divmod(blk * group + j, feats)
            dest = k * hpd + lax.rem(r - s + hpd, hpd)
            o_send[dest] = o[j * count : (j + 1) * count]


def prep_kernel(
    hl,
    r_ref,
    xs,
    g1,
    b1,
    w_in,
    k_out,
    v_out,
    kt_out,
    qtz,
    nt,
    wqt,
    wkt,
):
    total = xs.shape[0]
    cl = hl * HD
    r = r_ref[0]
    wqt[...] = flip(head_columns(w_in, r, cl, 0)) * BF(SCALING)
    wkt[...] = flip(head_columns(w_in, r, cl, 1))
    qtz[...] = jnp.zeros_like(qtz)

    def project(b, _):
        at = pl.multiple_of(b * PB, PB)
        n, _r = ln_parts(xs[pl.ds(at, PB), :].astype(F32))
        h1 = (n * g1[...] + b1[...]).astype(BF)
        nt[:, pl.ds(at, PB)] = jnp.transpose(n.astype(BF))
        qt = dot_nt(wqt[...], h1).astype(BF)
        k_out[pl.ds(at, PB), :] = dot(h1, head_columns(w_in, r, cl, 1)).astype(BF)
        v_out[pl.ds(at, PB), :] = dot(h1, head_columns(w_in, r, cl, 2)).astype(BF)
        kt_out[:, pl.ds(at, PB)] = dot_nt(wkt[...], h1).astype(BF)
        for h in range(hl):
            sub = (h % 2) * HD
            qtz[h, sub : sub + HD, pl.ds(at, PB)] = qt[h * HD : (h + 1) * HD]
        return 0

    lax.fori_loop(0, total // PB, project, 0)


def plus(a, b):
    return (a.astype(F32) + b.astype(F32)).astype(BF)


def first_sums(x_ref, y_ref, a_keep, a_got, c_keep, c_got, a_mine, a_other, c_mine, c_other):
    half = a_mine.shape[1]
    mine = pl.multiple_of(x_ref[0] * half, half)
    other = pl.multiple_of((1 - x_ref[0]) * half, half)

    def step(i, _):
        for ref, first in ((a_mine, mine), (a_other, other)):
            ref[i] = plus(a_keep[i, pl.ds(first, half), :], a_got[i, pl.ds(first, half), :])
        return 0

    lax.fori_loop(0, a_mine.shape[0], step, 0)
    split_y(y_ref[0], c_keep, c_got, c_mine, c_other)


def split_y(y, keep, got, mine, other):
    def step(i, _):
        for ref, at in ((mine, 2 * i + y), (other, 2 * i + 1 - y)):
            ref[i] = plus(keep[at], got[at])
        return 0

    lax.fori_loop(0, mine.shape[0], step, 0)


def top_split(z_ref, keep, got, mine, other):
    chunks = mine.shape[0]
    top = z_ref[0] // chunks
    for j in range(chunks):
        mine[j] = plus(keep[top * chunks + j], got[top * chunks + j])
        other[j] = plus(keep[(1 - top) * chunks + j], got[(1 - top) * chunks + j])


def middle_sums(z_ref, a_keep, a_got, c_keep, c_got, *pieces):
    count = a_keep.shape[0]
    pick_z(z_ref, a_keep, a_got, *pieces[:count])
    for c, ref in enumerate(pieces[count:]):
        at = lax.bitwise_xor(lax.rem(z_ref[0], count // 2), c)
        ref[...] = plus(c_keep[at], c_got[at])


def add_all(terms):
    total = terms[0].astype(F32)
    for term in terms[1:]:
        total = total + term.astype(F32)
    return total.astype(BF)


def pick_y(y_ref, keep, got, mine, other):
    split_y(y_ref[0], keep, got, mine, other)


def pick_z(z_ref, keep, got, *pieces):
    for c, ref in enumerate(pieces):
        at = lax.bitwise_xor(z_ref[0], c)
        ref[...] = plus(keep[at], got[at])


def sum_kernel(*refs):
    refs[-1][...] = add_all([ref[...] for ref in refs[:-1]])


def bwd_kernel(
    hpd,
    hl,
    r_ref,
    start_ref,
    do_recv,
    k_in,
    v_in,
    kt_in,
    qtz,
    ot,
    lse,
    rank_row,
    dt_out,
    do_scr,
    dotz,
    dots,
    code_col,
    code_row,
    dq_acc,
    dk_acc,
    dv_acc,
    p_scr,
    ds_scr,
    pairs,
):
    feats = do_recv.shape[0] // hpd
    count = do_recv.shape[1]
    total = do_scr.shape[0]
    cl = hl * HD
    r = r_ref[0]

    for s in range(hpd):
        for k in range(feats):
            at = (s * feats + k) * count
            do_scr[at : at + count, :] = do_recv[k * hpd + lax.rem(r - s + hpd, hpd)]
    starts = [start_ref[c].astype(F32) for c in range(1, CLASSES)]
    code_col[...] = codes(iota((total, LANES), 0), starts)
    code_row[...] = codes(iota((8, total), 1), starts)
    dotz[...] = jnp.zeros_like(dotz)

    def arrange(b, _):
        at = pl.multiple_of(b * PB, PB)
        block = jnp.transpose(dot(permute_block(rank_row, at, PB, total), do_scr[...]))
        prod = block * ot[:, pl.ds(at, PB)].astype(F32)
        for h in range(hl):
            sub = (h % 2) * HD
            rows = slice(h * HD, (h + 1) * HD)
            dotz[h, sub : sub + HD, pl.ds(at, PB)] = block[rows].astype(BF)
            dots[h : h + 1, pl.ds(at, PB)] = jnp.sum(prod[rows], 0, keepdims=True)
        return 0

    lax.fori_loop(0, total // PB, arrange, 0)
    dq_acc[...] = jnp.zeros_like(dq_acc)
    dk_acc[...] = jnp.zeros_like(dk_acc)
    dv_acc[...] = jnp.zeros_like(dv_acc)

    def list_keys(b, filled):
        t0, t1 = tile_range(start_ref, b * KB, KB, QB)

        def put(t, i):
            pairs[i] = b * 4096 + t
            return i + 1

        return lax.fori_loop(t0, t1, put, filled)

    filled = lax.fori_loop(0, total // KB, list_keys, jnp.int32(0))

    def places(i):
        b, t = pairs[i] // 4096, lax.rem(pairs[i], 4096)
        return pl.ds(pl.multiple_of(b * KB, KB), KB), pl.ds(pl.multiple_of(t * QB, QB), QB)

    def scores(i):
        kt, at = places(i)
        ccol = code_col[kt, :]
        seen = jnp.concatenate([ccol] * (QB // LANES), -1) == code_row[0:1, at]
        for h in range(hl):
            cols = slice(h // 2 * LANES, (h // 2 + 1) * LANES)
            s = dot(k_in[kt, cols], qtz[h, :, at])
            p = jnp.where(seen, jnp.exp(s - lse[h : h + 1, at]), 0.0)
            dp = dot(v_in[kt, cols], dotz[h, :, at])
            p_scr[h] = p.astype(BF)
            ds_scr[h] = (p * (dp - dots[h : h + 1, at])).astype(BF)

    def collect(i):
        kt, at = places(i)
        for h in range(hl):
            rows = slice(h * HD, (h + 1) * HD)
            own = slice((h % 2) * HD, (h % 2 + 1) * HD)
            ds = ds_scr[h]
            dv_acc[rows, kt] += dot_nt(dotz[h, own, at], p_scr[h])
            dk_acc[rows, kt] += dot_nt(qtz[h, own, at], ds)
            dq_acc[rows, at] += dot(kt_in[rows, kt], ds)

    def step(i, _):
        scores(i)
        collect(i)
        return 0

    lax.fori_loop(0, filled, step, 0)
    dt_out[:cl, :] = (dq_acc[...] * SCALING).astype(BF)
    dt_out[cl : 2 * cl, :] = dk_acc[...].astype(BF)
    dt_out[2 * cl :, :] = dv_acc[...].astype(BF)


def dh_kernel(hpd, r_ref, dt, w_in, rank_col, *refs):
    dh_outs, dht = refs[:-1], refs[-1]
    part, count, width = dh_outs[0].shape
    cuts = len(dh_outs) // hpd
    feats = cuts * part
    total = dt.shape[1]
    cl = dt.shape[0] // 3
    w3 = jnp.concatenate([head_columns(w_in, r_ref[0], cl, j) for j in range(3)], 1)
    for b in range(total // PB):
        at = slice(b * PB, (b + 1) * PB)
        dht[:, at] = dot(w3, dt[:, at]).astype(BF)
    group = feats // 2
    for blk in range(total // (group * count)):
        at = blk * group * count
        hot = unpermute_block(rank_col[at : at + group * count, :], total)
        o = dot_nt(hot, dht[...]).astype(BF)
        for j in range(group):
            s, k = divmod(blk * group + j, feats)
            dh_outs[cuts * s + k // part][k % part] = o[j * count : (j + 1) * count]


SUB = 16
CUTS = 4


def q_rows(cl, width):
    return SUB * (-(-6 * cl // width)) + SUB


def dw_kernel(r_ref, x_ref, y_ref, z_ref, dt, nt, w_in, g1, b1, *refs):
    x = x_ref[0]
    width, total = nt.shape
    cols = dt.shape[0]
    cl = cols // 3
    a_keep, a_got, c_keep, c_got, q_keep, q_send, a_mine, a_other, c_mine, c_other = refs[:10]
    m_scr, dw_scr = refs[10:]
    split_y(y_ref[0], a_keep, a_got, a_mine, a_other)
    top_split(z_ref, c_keep, c_got, c_mine, c_other)
    feats = q_keep.shape[0]
    for c in range(3):
        rows = slice(c * cl, (c + 1) * cl)
        m_scr[:, rows] = dot_nt(nt[...], dt[rows, :])
    ones = jnp.ones((8, total), BF)
    sums_row = dot_nt(ones, dt[...])[0:1]
    gcol = jnp.transpose(jnp.broadcast_to(g1[...], (LANES, width)))
    bcol = jnp.transpose(jnp.broadcast_to(b1[...], (LANES, width)))
    gg = jnp.zeros((width, LANES), F32)
    gb = jnp.zeros((width, LANES), F32)
    for j in range(cols // LANES):
        lanes = slice(j * LANES, (j + 1) * LANES)
        first = (j * LANES // cl) * width + r_ref[0] * cl + j * LANES % cl
        w = w_in[:, pl.ds(pl.multiple_of(first, LANES), LANES)].astype(F32)
        m = m_scr[:, lanes]
        gg = gg + w * m
        gb = gb + w * sums_row[:, lanes]
        dw_scr[:, lanes] = (m * gcol + bcol * sums_row[:, lanes]).astype(BF)
    gg = jnp.sum(jnp.transpose(gg), 0, keepdims=True)
    gb = jnp.sum(jnp.transpose(gb), 0, keepdims=True)
    vec = jnp.concatenate([gg, gb, jnp.zeros((SUB - 2, width), F32)], 0).astype(BF)
    per = width // cl
    last = q_keep.shape[1] - SUB
    for e in range(feats):
        for ref, side in ((q_keep, x), (q_send, 1 - x)):
            for s in range(6):
                j, b = divmod(s, 2)
                src = pl.multiple_of((e * 4 + b) * SUB + side * 2 * SUB, SUB)
                to = (s // per) * SUB
                ref[e, to : to + SUB, (s % per) * cl : (s % per + 1) * cl] = dw_scr[
                    pl.ds(src, SUB), j * cl : (j + 1) * cl
                ]
            used = 6 % per
            if used:
                ref[e, last - SUB : last, used * cl :] = jnp.zeros((SUB, width - used * cl), BF)
            ref[e, last:, :] = vec


def gather_kernel(hpd, r_ref, x_ref, *refs):
    same, other = refs[:hpd], refs[hpd : 2 * hpd]
    a_side, a_pair, c_sum, c_pair = refs[2 * hpd : 2 * hpd + 4]
    out, vec, down, up, fqkv, fout, sout, vectors = refs[2 * hpd + 4 :]
    piece = out.shape[0]
    rows, width = same[0].shape
    cl = width // hpd
    r, x = r_ref[0], x_ref[0]
    blocks = piece // SUB
    first = lax.rem(r * blocks, 2)
    from_same = r * blocks // 2 == x
    for s in range(hpd):
        owner = lax.rem(r - s + hpd, hpd)
        for j in range(3):
            lo = 2 * j // hpd * SUB
            to = pl.ds(pl.multiple_of(j * width + owner * cl, LANES), cl)
            for b in range(blocks):
                col = pl.multiple_of((2 * j % hpd + first + b) * cl, LANES)
                at = (slice(lo, lo + SUB), pl.ds(col, cl))
                picked = jnp.where(from_same, same[s][at].astype(F32), other[s][at].astype(F32))
                out[b * SUB : (b + 1) * SUB, to] = picked
    total = same[0][rows - SUB : rows, :].astype(F32)
    for s in range(1, hpd):
        total = total + same[s][rows - SUB : rows, :].astype(F32)
    vec[...] = total[:8]

    down[...] = jnp.where(x == 0, a_side[...].astype(F32), a_pair[...].astype(F32))

    def both(first, size):
        at = slice(first, first + size)
        return c_sum[at, :].astype(F32) + c_pair[at, :].astype(F32)

    for b in range(up.shape[1] // width):
        at = slice(b * piece, (b + 1) * piece)
        block = jnp.where(x == 0, a_pair[at, :].astype(F32), a_side[at, :].astype(F32))
        up[:, b * width : (b + 1) * width] = block
    base = 0
    for ref in (fqkv, fout, sout):
        for b in range(ref.shape[1] // width):
            ref[:, b * width : (b + 1) * width] = both(base, piece)
            base += piece
    vectors[...] = both(base, vectors.shape[0])


def norm_kernel(hpd, *refs):
    parts = refs[:-5]
    x, g1, q_keep, q_got, out = refs[-5:]
    part, count, _w = parts[0].shape
    cuts = len(parts) // hpd
    feats = cuts * part
    for k in range(feats):
        dh = parts[k // part][k % part].astype(F32)
        for s in range(1, hpd):
            dh = dh + parts[cuts * s + k // part][k % part].astype(F32)
        n, r = ln_parts(x[k, :count, :].astype(F32))
        out[k, :count, :] = ln_back(dh, n, r, g1[...]).astype(BF)
        out[k, count:, :] = add_all((q_keep[k], q_got[k]))


def final_kernel(dx1, both, out, q_sum, scr):
    feats = both.shape[0]
    count, _f, width = out.shape
    q_sum[...] = add_all([both[k, count:, :] for k in range(feats)])
    for f in range(feats):
        val = dx1[f * count : (f + 1) * count, :] + both[f, :count, :].astype(F32)
        place(scr, f, count, feats, val)
    out[...] = lift(scr).reshape(count, feats, width)


def rows_kernel(
    hpd,
    me_ref,
    o_recv,
    xt,
    cot_hbm,
    g2,
    b2,
    g3,
    b3,
    ub,
    db,
    wso_hbm,
    wfq_hbm,
    wfo_hbm,
    wup_hbm,
    wdn_hbm,
    *refs,
):
    outs_hbm, scratch = refs[:7], refs[7:-2]
    (wso, wfq, wfo, wup, wdn, cot), scratch = scratch[:6], scratch[6:]
    outs_vmem, scratch = scratch[:7], scratch[7:]
    out, dx1, do_send, a_keep, a_send, b_keep, b_send = outs_vmem
    (
        wide,
        ct,
        o1,
        x1,
        h2,
        qkv,
        o2,
        x2,
        h3,
        u,
        dz,
        dx2,
        do2,
        dqkv,
        pscr,
        tr,
        wblk,
        ubg,
        wdn_scr,
    ) = scratch
    in_sem, out_sem = refs[-2:]
    loads = [
        pltpu.make_async_copy(src, dst, in_sem.at[i])
        for i, (src, dst) in enumerate(
            (
                (cot_hbm, cot),
                (wso_hbm, wso),
                (wfq_hbm, wfq),
                (wfo_hbm, wfo),
                (wup_hbm, wup),
                (wdn_hbm, wdn),
            )
        )
    ]
    for load in loads:
        load.start()
    stores = [
        pltpu.make_async_copy(src, dst, out_sem.at[i])
        for i, (src, dst) in enumerate(zip(outs_vmem, outs_hbm))
    ]
    feats = xt.shape[0]
    count = xt.shape[1] - PAD
    width = xt.shape[2]
    rows = feats * count
    hidden = wup.shape[1]
    n = o_recv.shape[0]
    cl = o_recv.shape[2]
    half = rows // 2
    me = me_ref[0]
    lane = iota((1, LANES), 1)
    part = 16
    tiles = count // part
    size = feats * part

    loads[0].wait()
    lay(wide, cot[...].astype(F32).reshape(rows, width))
    for f in range(feats):
        ct[f * count : (f + 1) * count, :] = take(wide, f, count, feats).astype(BF)
        for c in range(hpd):
            o1[f * count : (f + 1) * count, c * cl : (c + 1) * cl] = o_recv[f * hpd + c]

    loads[1].wait()
    for b in range(2):
        at = slice(b * half, (b + 1) * half)
        x = xt[b * feats // 2 : (b + 1) * feats // 2, :count, :].astype(F32).reshape(half, width)
        v = x + dot(o1[at, :], wso[...])
        x1[at, :] = v
        nn, _r = ln_parts(v)
        h2[at, :] = (nn * g2[...] + b2[...]).astype(BF)

    loads[2].wait()
    qkv3 = qkv

    def qkv_step(c, _):
        cols = pl.ds(pl.multiple_of(c * TILE, TILE), TILE)
        scale = jnp.where(c < width // TILE, SCALING, 1.0)
        y = dot(h2[...], wfq[:, cols])
        qkv3[:, :, cols] = (y * scale).astype(BF).reshape(feats, count, TILE)
        return 0

    lax.fori_loop(0, 3 * width // TILE, qkv_step, 0)

    ri = lax.broadcasted_iota(jnp.int32, (2 * size, size), 0)
    ci = lax.broadcasted_iota(jnp.int32, (2 * size, size), 1)
    same = lax.rem(ri, part) == lax.rem(ci, part)
    low_lane = jnp.where(iota((1, LANES), 1) < HD, 1.0, 0.0).astype(BF)
    high_lane = jnp.where(iota((1, LANES), 1) < HD, 0.0, 1.0).astype(BF)

    def tile_of(ref, at, lo):
        return ref[:, at, lo : lo + LANES].reshape(size, LANES)

    def by_head(v):
        return jnp.concatenate([v * low_lane, v * high_lane], 0)

    def by_head_t(v):
        vt = jnp.transpose(v)
        zero = jnp.zeros((HD, size), BF)
        return jnp.concatenate(
            [jnp.concatenate([vt[:HD], zero], 0), jnp.concatenate([zero, vt[HD:]], 0)], 1
        )

    def side(v):
        return jnp.concatenate([v[:size], v[size:]], 1)

    def per_head(v, fn):
        return jnp.concatenate(
            [jnp.broadcast_to(fn(v[i * size : (i + 1) * size]), (size, size)) for i in (0, 1)], 0
        )

    def feat_fwd(t, _):
        at = pl.ds(pl.multiple_of(t * part, part), part)
        for p2 in range(H // 2):
            lo = p2 * LANES
            q = tile_of(qkv3, at, lo)
            k = tile_of(qkv3, at, width + lo)
            v = tile_of(qkv3, at, 2 * width + lo)
            s = jnp.where(same, dot_nt(by_head(k), q), NEGATIVE)
            e = jnp.exp(s - per_head(s, lambda w: jnp.max(w, 0, keepdims=True)))
            p = (e * per_head(e, lambda w: 1.0 / jnp.sum(w, 0, keepdims=True))).astype(BF)
            pscr[t, p2] = p
            ot = dot(by_head_t(v), p)
            o2[:, at, lo : lo + LANES] = jnp.transpose(ot).astype(BF).reshape(feats, part, LANES)
        return 0

    lax.fori_loop(0, tiles, feat_fwd, 0, unroll=2)

    loads[3].wait()
    for b in range(2):
        at = slice(b * half, (b + 1) * half)
        o = o2[b * feats // 2 : (b + 1) * feats // 2, :, :].reshape(half, width)
        v = x1[at, :] + dot(o, wfo[...])
        x2[at, :] = v
        nn, _r = ln_parts(v)
        h3[at, :] = (nn * g3[...] + b3[...]).astype(BF)

    loads[4].wait()
    loads[5].wait()

    def ffn(c, _):
        cols = pl.ds(pl.multiple_of(c * FT, FT), FT)
        total = jnp.zeros((8, FT), F32)
        for b in range(2):
            at = slice(b * half, (b + 1) * half)
            z = dot(h3[at, :], wup[:, cols]) + ub[0:1, cols]
            w = GELU_C * GELU_A * (z * z) + GELU_C
            cdf = 0.5 * jnp.tanh(z * w) + 0.5
            g = z * cdf
            u[at, cols] = g.astype(BF)
            slope = cdf + g * (1.0 - cdf) * (6.0 * w - 4.0 * GELU_C)
            d = dot_nt(ct[at, :], wdn[cols, :]) * slope
            dz[at, cols] = d.astype(BF)
            total = total + jnp.sum(d.reshape(half // 8, 8, FT), 0)
        ubg[:, cols] = total
        return 0

    lax.fori_loop(0, hidden // FT, ffn, 0)

    vectors = []
    gg = jnp.zeros((1, width), F32)
    gb = jnp.zeros((1, width), F32)
    gd = jnp.zeros((1, width), F32)
    for b in range(2):
        at = slice(b * half, (b + 1) * half)
        y = x2[at, :] + dot(u[at, :], wdn[...]) + db[...]
        for j in range(feats // 2):
            f = b * (feats // 2) + j
            place(wide, f, count, feats, y[j * count : (j + 1) * count])
        dh = dot_nt(dz[at, :], wup[...])
        nn, r = ln_parts(x2[at, :])
        c = ct[at, :].astype(F32)
        gg = gg + jnp.sum(dh * nn, 0, keepdims=True)
        gb = gb + jnp.sum(dh, 0, keepdims=True)
        gd = gd + jnp.sum(c, 0, keepdims=True)
        v = c + ln_back(dh, nn, r, g3[...])
        dx2[at, :] = v
        do2[b * feats // 2 : (b + 1) * feats // 2, :, :] = (
            dot_nt(v.astype(BF), wfo[...]).astype(BF).reshape(feats // 2, count, width)
        )
    out[...] = lift(wide).reshape(count, feats, width).astype(BF)
    stores[0].start()
    vectors = [gg, gb, gd]

    core = lax.rem(me, 2)

    def slot(pos):
        at, other = divmod(pos, 2)
        refs = (a_send, b_send) if other else (a_keep, b_keep)
        return refs, at, 2 * at + (1 - core if other else core)

    piece = width // n
    fpiece = hidden // n

    def spread(group, base):
        for pos in range(n):
            refs, at, d = slot(pos)
            src = pl.multiple_of(d * piece, piece)
            refs[group][at, base : base + piece, :] = wblk[pl.ds(src, piece), :]

    base = 0
    for b in range(hidden // width):
        tr[...] = flip(u[:, b * width : (b + 1) * width])
        wdn_scr[b * width : (b + 1) * width, :] = dot(tr[...], ct[...]).astype(BF)
    for pos in range(n):
        refs, at, d = slot(pos)
        src = pl.multiple_of(d * fpiece, fpiece)
        refs[0][at, base : base + fpiece, :] = wdn_scr[pl.ds(src, fpiece), :]
    base += fpiece
    tr[...] = flip(h3[...])
    for b in range(hidden // width):
        wblk[...] = dot(tr[...], dz[:, b * width : (b + 1) * width]).astype(BF)
        spread(0, base)
        base += piece
    stores[3].start()
    stores[4].start()

    def feat_bwd(t, _):
        at = pl.ds(pl.multiple_of(t * part, part), part)
        for p2 in range(H // 2):
            lo = p2 * LANES
            q = tile_of(qkv3, at, lo)
            k = tile_of(qkv3, at, width + lo)
            v = tile_of(qkv3, at, 2 * width + lo)
            g = tile_of(do2, at, lo)
            p = pscr[t, p2]
            pf = p.astype(F32)
            dp = dot_nt(by_head(v), g)
            ds = pf * (dp - per_head(pf * dp, lambda w: jnp.sum(w, 0, keepdims=True)))
            ds = ds.astype(BF)
            dv = dot(side(p), by_head(g))
            dk = dot(side(ds), by_head(q))
            dq = jnp.transpose(dot(by_head_t(k), ds)) * SCALING
            for j, d in enumerate((dq, dk, dv)):
                dqkv[:, at, j * width + lo : j * width + lo + LANES] = d.astype(BF).reshape(
                    feats, part, LANES
                )
        return 0

    lax.fori_loop(0, tiles, feat_bwd, 0, unroll=2)

    gg = jnp.zeros((1, width), F32)
    gb = jnp.zeros((1, width), F32)
    for b in range(2):
        at = slice(b * half, (b + 1) * half)
        d = dqkv[b * feats // 2 : (b + 1) * feats // 2, :, :].reshape(half, 3 * width)
        dh = dot_nt(d, wfq[...])
        nn, r = ln_parts(x1[at, :])
        gg = gg + jnp.sum(dh * nn, 0, keepdims=True)
        gb = gb + jnp.sum(dh, 0, keepdims=True)
        v = dx2[at, :] + ln_back(dh, nn, r, g2[...])
        dx1[at, :] = v
        g = dot_nt(v.astype(BF), wso[...]).astype(BF)
        for j in range(feats // 2):
            f = b * (feats // 2) + j
            for c in range(hpd):
                do_send[f * hpd + c] = g[j * count : (j + 1) * count, c * cl : (c + 1) * cl]
    stores[1].start()
    stores[2].start()
    vectors = [gg, gb] + vectors

    base = 0
    tr[...] = flip(h2[...])
    for b in range(3):
        d = dqkv[:, :, b * width : (b + 1) * width].reshape(rows, width)
        wblk[...] = dot(tr[...], d).astype(BF)
        spread(1, base)
        base += piece
    tr[...] = flip(o2[...].reshape(rows, width))
    wblk[...] = dot(tr[...], dx2[...].astype(BF)).astype(BF)
    spread(1, base)
    base += piece
    tr[...] = flip(o1[...])
    wblk[...] = dot(tr[...], dx1[...].astype(BF)).astype(BF)
    spread(1, base)
    base += piece
    ubs = jnp.sum(ubg[...], 0, keepdims=True)
    vectors = vectors + [ubs[:, b * width : (b + 1) * width] for b in range(hidden // width)]
    vec = jnp.concatenate(vectors + [jnp.zeros((16 - len(vectors), width), F32)], 0).astype(BF)
    for pos in range(n):
        refs, at, _d = slot(pos)
        refs[1][at, base : base + 16, :] = vec
    stores[5].start()
    stores[6].start()
    for store in stores:
        store.wait()


def solution(mesh):
    n = mesh.shape["samp"]
    groups = mesh.shape["grp"]
    gbits = groups.bit_length() - 1
    tie = lax.optimization_barrier
    swap_core = [(d, d ^ 1) for d in range(n)]
    swap_y = [(d, d ^ 2) for d in range(n)]
    same_core = [[2 * k + c for k in range(n // 2)] for c in (0, 1)]

    def swap_grp(v, bit=0):
        return lax.ppermute(v, "grp", [(d, d ^ (1 << bit)) for d in range(groups)])

    def rest_of_grp(v):
        for bit in range(1, gbits):
            v = (v.astype(F32) + swap_grp(v, bit).astype(F32)).astype(BF)
        return v

    def body(
        tokens,
        segments,
        cotangent,
        first_gain,
        first_shift,
        sample_qkv,
        sample_out,
        second_gain,
        second_shift,
        feature_qkv,
        feature_out,
        third_gain,
        third_shift,
        up_weight,
        up_bias,
        down_weight,
        down_bias,
    ):
        count, feats, width = tokens.shape[1:]
        hidden = up_weight.shape[1]
        rows = count * feats
        hpd = n // feats
        hl = H // hpd
        cl = hl * HD
        total = n * count
        heads8 = 8
        me = lax.axis_index("samp")
        r = lax.rem(me, hpd)
        x = lax.rem(lax.axis_index("grp"), 2)
        y, z = (me >> 1) & 1, me >> 2
        r1, me1, x1, y1, z1 = (v.reshape(1).astype(jnp.int32) for v in (r, me, x, y, z))
        peers = [[q + hpd * k for k in range(feats)] for q in range(hpd)]
        g1, b1, g2, b2, g3, b3, ub, db = (
            v.reshape(1, -1)
            for v in (
                first_gain,
                first_shift,
                second_gain,
                second_shift,
                third_gain,
                third_shift,
                up_bias,
                down_bias,
            )
        )

        def shift(s):
            return [(d, d // hpd * hpd + (d % hpd + s) % hpd) for d in range(n)]

        (xt,) = call(
            pack_kernel,
            [((feats, count + PAD, width), BF)],
            [pltpu.VMEM((width // LANES, rows, LANES), F32)],
            tokens[0],
            segments,
        )
        mine = lax.all_to_all(xt, "samp", 0, 0, tiled=True, axis_index_groups=peers)
        xparts = [mine] + [lax.ppermute(mine, "samp", shift(s)) for s in range(1, hpd)]

        o_send, xs, ot, lse, rank_row, rank_col, starts = call(
            functools.partial(fwd_kernel, hpd, hl),
            [
                ((n, count, cl), BF),
                ((total, width), BF),
                ((cl, total), BF),
                ((heads8, total), F32),
                ((8, total), F32),
                ((total, LANES), F32),
                ((8,), jnp.int32),
            ],
            [
                pltpu.VMEM((total, width), BF),
                pltpu.VMEM((total, LANES), F32),
                pltpu.VMEM((hl, LANES, total), BF),
                pltpu.VMEM((total, cl), BF),
                pltpu.VMEM((hl, HD + 16, total), BF),
                pltpu.VMEM((total, cl), BF),
                pltpu.VMEM((total, LANES), F32),
                pltpu.VMEM((8, total), F32),
                pltpu.VMEM((hl, HD + 16, TQ), F32),
                pltpu.VMEM((hl, 8, TQ), F32),
                pltpu.VMEM((hl, total, TQ), F32),
                pltpu.VMEM((cl, width), BF),
                pltpu.VMEM((cl, width), BF),
            ],
            r1,
            *xparts,
            g1,
            b1,
            sample_qkv,
            smem=(0,),
            smem_out=(6,),
            vmem=28,
        )
        o_recv = lax.all_to_all(o_send, "samp", 0, 0, tiled=True)

        piece = width // n
        fpiece = hidden // n
        apieces = fpiece + piece * (hidden // width)
        bpieces = piece * 5 + 16
        vm = pltpu.VMEM
        out, dx1, do_send, a_keep, a_send, b_keep, b_send = call(
            functools.partial(rows_kernel, hpd),
            [
                ((count, feats, width), BF),
                ((rows, width), F32),
                ((n, count, cl), BF),
                ((n // 2, apieces, width), BF),
                ((n // 2, apieces, width), BF),
                ((n // 2, bpieces, width), BF),
                ((n // 2, bpieces, width), BF),
            ],
            [
                vm((width, width), BF),
                vm((width, 3 * width), BF),
                vm((width, width), BF),
                vm((width, hidden), BF),
                vm((hidden, width), BF),
                vm((count, feats, width), BF),
                vm((count, feats, width), BF),
                vm((rows, width), F32),
                vm((n, count, cl), BF),
                vm((n // 2, apieces, width), BF),
                vm((n // 2, apieces, width), BF),
                vm((n // 2, bpieces, width), BF),
                vm((n // 2, bpieces, width), BF),
                vm((width // LANES, rows, LANES), F32),
                vm((rows, width), BF),
                vm((rows, width), BF),
                vm((rows, width), F32),
                vm((rows, width), BF),
                vm((feats, count, 3 * width), BF),
                vm((feats, count, width), BF),
                vm((rows, width), F32),
                vm((rows, width), BF),
                vm((rows, hidden), BF),
                vm((rows, hidden), BF),
                vm((rows, width), F32),
                vm((feats, count, width), BF),
                vm((feats, count, 3 * width), BF),
                vm((count // 16, H // 2, 32 * feats, 16 * feats), BF),
                vm((width, rows), BF),
                vm((width, width), BF),
                vm((8, hidden), F32),
                vm((hidden, width), BF),
                pltpu.SemaphoreType.DMA((6,)),
                pltpu.SemaphoreType.DMA((7,)),
            ],
            me1,
            o_recv,
            xt,
            cotangent[0],
            g2,
            b2,
            g3,
            b3,
            ub,
            db,
            sample_out,
            feature_qkv,
            feature_out,
            up_weight,
            down_weight,
            smem=(0,),
            hbm=(3, 10, 11, 12, 13, 14),
            hbm_out=tuple(range(7)),
            vmem=48,
        )
        a_got = lax.ppermute(a_send, "samp", swap_core)
        b_got = lax.ppermute(b_send, "samp", swap_core)
        do_recv = lax.all_to_all(do_send, "samp", 0, 0, tiled=True)

        qr = q_rows(cl, width)
        half = apieces // 2
        zs = n // 4

        def along_z(pieces, unit):
            return [pieces[0]] + [
                lax.ppermute(pieces[c], "samp", [(d, d ^ (unit * c)) for d in range(n)])
                for c in range(1, len(pieces))
            ]

        am, ao, cm, co = call(
            first_sums,
            [((n // 2, half, width), BF)] * 2 + [((n // 4, bpieces, width), BF)] * 2,
            [],
            x1,
            y1,
            a_keep,
            a_got,
            b_keep,
            b_got,
            smem=(0, 1),
            vmem=16,
        )
        ag, cg = swap_grp(ao), lax.ppermute(co, "samp", swap_y)
        xs_after, _ = tie((xs, am))
        k_all, v_all, kt_all, qtz, nt = call(
            functools.partial(prep_kernel, hl),
            [
                ((total, cl), BF),
                ((total, cl), BF),
                ((cl, total), BF),
                ((hl, LANES, total), BF),
                ((width, total), BF),
            ],
            [vm((cl, width), BF), vm((cl, width), BF)],
            r1,
            xs_after,
            g1,
            b1,
            sample_qkv,
            smem=(0,),
            vmem=16,
        )
        (dt,) = call(
            functools.partial(bwd_kernel, hpd, hl),
            [((3 * cl, total), BF)],
            [
                vm((total, cl), BF),
                vm((hl, LANES, total), BF),
                vm((8, total), F32),
                vm((total, LANES), F32),
                vm((8, total), F32),
                vm((cl, total), F32),
                vm((cl, total), F32),
                vm((cl, total), F32),
                vm((hl, KB, QB), BF),
                vm((hl, KB, QB), BF),
                pltpu.SMEM(((total // KB) * (total // QB),), jnp.int32),
            ],
            r1,
            starts,
            do_recv,
            k_all,
            v_all,
            kt_all,
            qtz,
            ot,
            lse,
            rank_row,
            smem=(0, 1),
            vmem=58,
        )
        am, ag, cm, cg, _ = tie((am, ag, cm, cg, dt))
        q_keep, q_send, am, ao, cm, co = call(
            dw_kernel,
            [((feats, qr, width), BF)] * 2
            + [((n // 4, half, width), BF)] * 2
            + [((zs // 2, bpieces, width), BF)] * 2,
            [vm((width, 3 * cl), F32), vm((width, 3 * cl), BF)],
            r1,
            x1,
            y1,
            z1,
            dt,
            nt,
            sample_qkv,
            g1,
            b1,
            am,
            ag,
            cm,
            cg,
            smem=(0, 1, 2, 3),
            vmem=16,
        )
        ag = lax.ppermute(ao, "samp", swap_y)
        cg = lax.ppermute(co, "samp", [(d, d ^ (n // 2)) for d in range(n)])
        dt, _ = tie((dt, q_send))
        dhs = call(
            functools.partial(dh_kernel, hpd),
            [((feats // CUTS, count, width), BF)] * (CUTS * hpd),
            [vm((width, total), BF)],
            r1,
            dt,
            sample_qkv,
            rank_col,
            smem=(0,),
            vmem=16,
        )
        parts = list(dhs[:CUTS])
        for s in range(1, hpd):
            parts += [lax.ppermute(v, "samp", shift(-s)) for v in dhs[CUTS * s : CUTS * s + CUTS]]
        pieces = call(
            middle_sums,
            [((half, width), BF)] * zs + [((bpieces, width), BF)] * (zs // 2),
            [],
            z1,
            am,
            ag,
            cm,
            cg,
            smem=(0,),
        )
        parts[0], _ = tie((parts[0], pieces[0]))
        a_pieces, c_pieces = along_z(pieces[:zs], 4), along_z(pieces[zs:], 4)
        (both,) = call(
            functools.partial(norm_kernel, hpd),
            [((feats, count + qr, width), BF)],
            [],
            *parts,
            mine,
            g1,
            q_keep,
            swap_grp(q_send),
            vmem=10,
        )
        both_send, *ends = tie((both, *a_pieces, *c_pieces))
        a_pieces, c_pieces = ends[:zs], ends[zs:]
        both = lax.all_to_all(both_send, "samp", 0, 0, tiled=True, axis_index_groups=peers)

        def last_steps(*pieces):
            (c_sum,) = call(sum_kernel, [((bpieces, width), BF)], [], *pieces[zs:])
            c_sum = rest_of_grp(c_sum)
            (a_side,) = call(sum_kernel, [((half, width), BF)], [], *pieces[:zs])
            a_side = rest_of_grp(a_side)
            return a_side, swap_grp(a_side), c_sum, swap_grp(c_sum)

        terms = (*a_pieces, *c_pieces)
        parts_summed = last_steps(*tie((*terms, both_send))[: len(terms)])
        grad_tokens, q_sum = call(
            final_kernel,
            [((count, feats, width), F32), ((qr, width), BF)],
            [vm((width // LANES, rows, LANES), F32)],
            dx1,
            both,
            vmem=12,
        )
        q_sum = rest_of_grp(q_sum)

        def from_peer(s, other):
            if not s and not other:
                return q_sum
            pairs = [
                (g * n + d, (g ^ other) * n + e) for g in range(groups) for d, e in shift(s)
            ]
            return lax.ppermute(q_sum, ("grp", "samp"), pairs)

        peers_same = [from_peer(s, 0) for s in range(hpd)]
        peers_other = [from_peer(s, 1) for s in range(hpd)]
        grad_sample_qkv, vec_sum, grad_down, grad_up, grad_fqkv, grad_fout, grad_sout, vu = call(
            functools.partial(gather_kernel, hpd),
            [
                ((piece, 3 * width), F32),
                ((8, width), F32),
                ((fpiece, width), F32),
                ((piece, hidden), F32),
                ((piece, 3 * width), F32),
                ((piece, width), F32),
                ((piece, width), F32),
                ((16, width), F32),
            ],
            [],
            r1,
            x1,
            *peers_same,
            *peers_other,
            *parts_summed,
            smem=(0, 1),
        )

        def own(v):
            return lax.dynamic_slice_in_dim(v, me * (v.shape[0] // n), v.shape[0] // n, 0)

        def own_rows(v):
            return lax.dynamic_slice_in_dim(v, me * piece, piece, 1)

        five = own_rows(vu[:5])
        two = own_rows(vec_sum[:2])
        vectors = [five[i] for i in range(5)]
        vectors.append(own(vu[5 : 5 + hidden // width].reshape(-1)))
        return (
            out[None],
            grad_tokens[None],
            two[0],
            two[1],
            grad_sample_qkv,
            grad_sout,
            vectors[0],
            vectors[1],
            grad_fqkv,
            grad_fout,
            vectors[2],
            vectors[3],
            grad_up,
            vectors[5],
            grad_down,
            vectors[4],
        )

    rep = P()
    data = P("grp", "samp", None, None)
    line = P("samp")
    flat = P("samp", None)
    in_specs = (data, P("grp", "samp"), data) + (rep,) * 14
    out_specs = (
        data,
        data,
        line,
        line,
        flat,
        flat,
        line,
        line,
        flat,
        flat,
        line,
        line,
        flat,
        line,
        flat,
        line,
    )
    return jax.shard_map(body, mesh=mesh, in_specs=in_specs, out_specs=out_specs, check_vma=False)
```

```python
import functools
import math

import jax
import jax.numpy as jnp
from jax import lax
from jax.experimental import pallas as pl
from jax.experimental.pallas import tpu as pltpu
from jax.sharding import PartitionSpec as P

H = 8
HD = 64
EPSILON = 1e-05
SCALING = 0.125
NEGATIVE = -1e30
BF = jnp.bfloat16
F32 = jnp.float32
TILE = 256
FT = 512
PB = 512
KB = 256
QB = 256
TQ = 256
TK = 256
LANES = 128
PAD = 8
GELU_C = math.sqrt(2.0 / math.pi)
GELU_A = 0.044715
MIB = 1024 * 1024
CLASSES = 5


def dot(a, b):
    return jnp.dot(a, b, preferred_element_type=F32)


def dot_nt(a, b):
    return lax.dot_general(a, b, (((1,), (1,)), ((), ())), preferred_element_type=F32)


def dot_tn(a, b):
    return lax.dot_general(a, b, (((0,), (0,)), ((), ())), preferred_element_type=F32)


def ln_parts(v):
    c = v - jnp.mean(v, -1, keepdims=True)
    r = lax.rsqrt(jnp.mean(c * c, -1, keepdims=True) + EPSILON)
    return c * r, r


def ln_back(dh, n, r, g):
    e = dh * g
    return r * (e - jnp.mean(e, -1, keepdims=True) - n * jnp.mean(e * n, -1, keepdims=True))


def flip(v):
    return jnp.transpose(v)


def head_columns(w, r, cl, which):
    first = which * (w.shape[1] // 3) + r * cl
    return w[:, pl.ds(pl.multiple_of(first, LANES), cl)]


def lay(scr, v):
    for a in range(scr.shape[0]):
        scr[a] = v[:, a * LANES : (a + 1) * LANES]


def lift(scr):
    return jnp.concatenate([scr[a] for a in range(scr.shape[0])], -1)


def take(scr, first, count, step):
    return jnp.concatenate(
        [scr[a, pl.ds(first, count, stride=step), :] for a in range(scr.shape[0])], -1
    )


def place(scr, first, count, step, v):
    for a in range(scr.shape[0]):
        scr[a, pl.ds(first, count, stride=step), :] = v[:, a * LANES : (a + 1) * LANES]


def iota(shape, dim):
    return lax.broadcasted_iota(jnp.int32, shape, dim).astype(F32)


def call(fn, outs, scratch, *args, smem=(), smem_out=(), hbm=(), hbm_out=(), vmem=16):
    def spec(space):
        return pl.BlockSpec(memory_space=space)

    def place_of(i, scalars, far):
        return spec(pltpu.SMEM if i in scalars else pl.ANY if i in far else pltpu.VMEM)

    in_specs = [place_of(i, smem, hbm) for i in range(len(args))]
    out_specs = [place_of(i, smem_out, hbm_out) for i in range(len(outs))]
    return pl.pallas_call(
        fn,
        out_shape=[jax.ShapeDtypeStruct(*o) for o in outs],
        in_specs=in_specs,
        out_specs=out_specs,
        scratch_shapes=scratch,
        compiler_params=pltpu.CompilerParams(vmem_limit_bytes=vmem * MIB),
        cost_estimate=pl.CostEstimate(flops=0, bytes_accessed=0, transcendentals=0),
    )(*args)


def pack_kernel(tok, seg, out, scr):
    count, feats, width = tok.shape
    lay(scr, tok[...].astype(F32).reshape(count * feats, width))
    row = seg[...].astype(F32)
    for f in range(feats):
        out[f, :count, :] = take(scr, f, count, feats).astype(BF)
        out[f, count:, :] = jnp.zeros((PAD, width), BF)
        out[f, count:, :count] = jnp.broadcast_to(row, (PAD, count)).astype(BF)


def codes(pos, starts):
    cls = jnp.zeros_like(pos)
    for st in starts:
        cls = cls + jnp.where(pos >= st, 1.0, 0.0)
    return jnp.where(cls >= CLASSES - 1, pos + CLASSES, cls)


def tile_range(start_ref, first, size, tile):
    last = first + size - 1
    lo = jnp.int32(0)
    hi = start_ref[1]
    for c in range(1, CLASSES - 1):
        st = start_ref[c]
        lo = jnp.where(first >= st, st, lo)
        hi = jnp.where(last >= st, start_ref[c + 1], hi)
    pad = start_ref[CLASSES - 1]
    lo = jnp.where(first >= pad, first, lo)
    hi = jnp.where(last >= pad, first + size, hi)
    return lo // tile, (hi + tile - 1) // tile


def permute_block(rank_row, first, rows, total):
    pos = iota((rows, LANES), 0) + first.astype(F32)
    parts = []
    for j in range(total // LANES):
        hit = rank_row[0:1, j * LANES : (j + 1) * LANES] == pos
        parts.append(jnp.where(hit, 1.0, 0.0).astype(BF))
    return jnp.concatenate(parts, -1)


def unpermute_block(rank_col, total):
    rows = rank_col.shape[0]
    parts = []
    for j in range(total // LANES):
        pos = iota((1, LANES), 1) + float(j * LANES)
        parts.append(jnp.where(rank_col == pos, 1.0, 0.0).astype(BF))
    return jnp.concatenate(parts, -1)


def fwd_kernel(hpd, hl, r_ref, *refs):
    xparts = refs[:hpd]
    (g1, b1, w_in) = refs[hpd : hpd + 3]
    (o_send, xs_out, ot_out, lse_out, rank_row, rank_col, start_ref) = refs[hpd + 3 : hpd + 10]
    (x_scr, seg_scr, qtz, k_scr, vt, o_scr, code_col, code_row, acc, top, s_scr) = refs[
        hpd + 10 : hpd + 21
    ]
    wqt, wvt = refs[hpd + 21 :]
    feats = xparts[0].shape[0]
    count = xparts[0].shape[1] - PAD
    total = x_scr.shape[0]
    cl = hl * HD
    r = r_ref[0]
    chunks = total // LANES
    wqt[...] = flip(head_columns(w_in, r, cl, 0)) * BF(SCALING)
    wvt[...] = flip(head_columns(w_in, r, cl, 2))

    for s in range(hpd):
        for k in range(feats):
            at = (s * feats + k) * count
            x_scr[at : at + count, :] = xparts[s][k, :count, :]
            row = xparts[s][k, count : count + PAD, :LANES].astype(F32)[0:1]
            col = jnp.transpose(jnp.broadcast_to(row, (LANES, LANES)))
            seg_scr[at : at + count, :] = col[:count, :]

    seg = seg_scr[...]
    cls = jnp.where(seg < 0.0, float(CLASSES - 1), seg)
    seg_scr[...] = cls * 8192.0 + iota((total, LANES), 0)
    key_rows = []
    for j in range(chunks):
        blk = seg_scr[j * LANES : (j + 1) * LANES, :]
        key_rows.append(jnp.transpose(blk)[0:8, :])

    def count_less(i, carry):
        blk = seg_scr[pl.ds(pl.multiple_of(i * 64, 64), 64), :]
        out = []
        for j in range(chunks):
            less = jnp.where(blk < key_rows[j][0:1], 1.0, 0.0)
            out.append(carry[j] + jnp.sum(less.reshape(8, 8, LANES), 0))
        return tuple(out)

    ranks = lax.fori_loop(
        0, total // 64, count_less, tuple(jnp.zeros((8, LANES), F32) for _ in range(chunks))
    )
    for j in range(chunks):
        row = jnp.sum(ranks[j], 0, keepdims=True)
        rank_row[:, j * LANES : (j + 1) * LANES] = jnp.broadcast_to(row, (8, LANES))
        rank_col[j * LANES : (j + 1) * LANES, :] = jnp.transpose(
            jnp.broadcast_to(row, (LANES, LANES))
        )
    starts = []
    keys = jnp.concatenate([k[0:1] for k in key_rows], 0)
    for c in range(1, CLASSES):
        st = jnp.sum(jnp.where(keys < c * 8192.0, 1.0, 0.0))
        starts.append(st)
        start_ref[c] = st.astype(jnp.int32)
    start_ref[0] = jnp.int32(0)
    for c in range(CLASSES, 8):
        start_ref[c] = jnp.int32(total)
    code_col[...] = codes(iota((total, LANES), 0), starts)
    code_row[...] = codes(iota((8, total), 1), starts)

    qtz[...] = jnp.zeros_like(qtz)
    ones = jnp.where(iota((16, total), 0) == 0.0, 1.0, 0.0).astype(BF)
    for h in range(hl):
        vt[h, HD:, :] = ones

    def project(b, _):
        at = pl.multiple_of(b * PB, PB)
        block = dot(permute_block(rank_row, at, PB, total), x_scr[...])
        xs_out[pl.ds(at, PB), :] = block.astype(BF)
        n, _r = ln_parts(block)
        h1 = (n * g1[...] + b1[...]).astype(BF)
        qt = dot_nt(wqt[...], h1).astype(BF)
        k_scr[pl.ds(at, PB), :] = dot(h1, head_columns(w_in, r, cl, 1)).astype(BF)
        vv = dot_nt(wvt[...], h1).astype(BF)
        for h in range(hl):
            sub = (h % 2) * HD
            qtz[h, sub : sub + HD, pl.ds(at, PB)] = qt[h * HD : (h + 1) * HD]
            vt[h, :HD, pl.ds(at, PB)] = vv[h * HD : (h + 1) * HD]
        return 0

    lax.fori_loop(0, total // PB, project, 0)

    def attend(b, _):
        at = pl.multiple_of(b * TQ, TQ)
        t0, t1 = tile_range(start_ref, at, TQ, TK)
        acc[...] = jnp.zeros_like(acc)
        top[...] = jnp.full_like(top, NEGATIVE)
        crow = code_row[0:1, pl.ds(at, TQ)]

        def score(t, _):
            kt = pl.multiple_of(t * TK, TK)
            ccol = code_col[pl.ds(kt, TK), :]
            ccol = jnp.concatenate([ccol] * (TQ // LANES), -1)
            seen = ccol == crow
            for h in range(hl):
                pair = (h // 2) * LANES
                s = dot(k_scr[pl.ds(kt, TK), pair : pair + LANES], qtz[h, :, pl.ds(at, TQ)])
                s = jnp.where(seen, s, NEGATIVE)
                s_scr[h, pl.ds(kt, TK), :] = s
                top[h] = jnp.maximum(top[h], jnp.max(s.reshape(TK // 8, 8, TQ), 0))
            return 0

        lax.fori_loop(t0, t1, score, 0)
        for h in range(hl):
            top[h] = jnp.broadcast_to(jnp.max(top[h], 0, keepdims=True), (8, TQ))

        def mix(t, _):
            kt = pl.multiple_of(t * TK, TK)
            for h in range(hl):
                p = jnp.exp(s_scr[h, pl.ds(kt, TK), :] - top[h, 0:1, :]).astype(BF)
                acc[h] += dot(vt[h, :, pl.ds(kt, TK)], p)
            return 0

        lax.fori_loop(t0, t1, mix, 0)
        outs = []
        for h in range(hl):
            total_h = acc[h, HD : HD + 1, :]
            outs.append(acc[h, :HD, :] / total_h)
            lse_out[h : h + 1, pl.ds(at, TQ)] = top[h, 0:1, :] + jnp.log(total_h)
        ot = jnp.concatenate(outs, 0)
        ot_out[:, pl.ds(at, TQ)] = ot.astype(BF)
        o_scr[pl.ds(at, TQ), :] = jnp.transpose(ot).astype(BF)
        return 0

    lax.fori_loop(0, total // TQ, attend, 0)

    group = feats // 2
    for blk in range(total // (group * count)):
        at = blk * group * count
        hot = unpermute_block(rank_col[at : at + group * count, :], total)
        o = dot(hot, o_scr[...]).astype(BF)
        for j in range(group):
            s, k = divmod(blk * group + j, feats)
            dest = k * hpd + lax.rem(r - s + hpd, hpd)
            o_send[dest] = o[j * count : (j + 1) * count]


def prep_kernel(
    hl,
    r_ref,
    xs,
    g1,
    b1,
    w_in,
    k_out,
    v_out,
    kt_out,
    qtz,
    nt,
    wqt,
    wkt,
):
    total = xs.shape[0]
    cl = hl * HD
    r = r_ref[0]
    wqt[...] = flip(head_columns(w_in, r, cl, 0)) * BF(SCALING)
    wkt[...] = flip(head_columns(w_in, r, cl, 1))
    qtz[...] = jnp.zeros_like(qtz)

    def project(b, _):
        at = pl.multiple_of(b * PB, PB)
        n, _r = ln_parts(xs[pl.ds(at, PB), :].astype(F32))
        h1 = (n * g1[...] + b1[...]).astype(BF)
        nt[:, pl.ds(at, PB)] = jnp.transpose(n.astype(BF))
        qt = dot_nt(wqt[...], h1).astype(BF)
        k_out[pl.ds(at, PB), :] = dot(h1, head_columns(w_in, r, cl, 1)).astype(BF)
        v_out[pl.ds(at, PB), :] = dot(h1, head_columns(w_in, r, cl, 2)).astype(BF)
        kt_out[:, pl.ds(at, PB)] = dot_nt(wkt[...], h1).astype(BF)
        for h in range(hl):
            sub = (h % 2) * HD
            qtz[h, sub : sub + HD, pl.ds(at, PB)] = qt[h * HD : (h + 1) * HD]
        return 0

    lax.fori_loop(0, total // PB, project, 0)


def plus(a, b):
    return (a.astype(F32) + b.astype(F32)).astype(BF)


def first_sums(x_ref, y_ref, a_keep, a_got, c_keep, c_got, a_mine, a_other, c_mine, c_other):
    half = a_mine.shape[1]
    mine = pl.multiple_of(x_ref[0] * half, half)
    other = pl.multiple_of((1 - x_ref[0]) * half, half)

    def step(i, _):
        for ref, first in ((a_mine, mine), (a_other, other)):
            ref[i] = plus(a_keep[i, pl.ds(first, half), :], a_got[i, pl.ds(first, half), :])
        return 0

    lax.fori_loop(0, a_mine.shape[0], step, 0)
    split_y(y_ref[0], c_keep, c_got, c_mine, c_other)


def split_y(y, keep, got, mine, other):
    def step(i, _):
        for ref, at in ((mine, 2 * i + y), (other, 2 * i + 1 - y)):
            ref[i] = plus(keep[at], got[at])
        return 0

    lax.fori_loop(0, mine.shape[0], step, 0)


def top_split(z_ref, keep, got, mine, other):
    chunks = mine.shape[0]
    top = z_ref[0] // chunks
    for j in range(chunks):
        mine[j] = plus(keep[top * chunks + j], got[top * chunks + j])
        other[j] = plus(keep[(1 - top) * chunks + j], got[(1 - top) * chunks + j])


def middle_sums(z_ref, a_keep, a_got, c_keep, c_got, *pieces):
    count = a_keep.shape[0]
    pick_z(z_ref, a_keep, a_got, *pieces[:count])
    for c, ref in enumerate(pieces[count:]):
        at = lax.bitwise_xor(lax.rem(z_ref[0], count // 2), c)
        ref[...] = plus(c_keep[at], c_got[at])


def add_all(terms):
    total = terms[0].astype(F32)
    for term in terms[1:]:
        total = total + term.astype(F32)
    return total.astype(BF)


def pick_y(y_ref, keep, got, mine, other):
    split_y(y_ref[0], keep, got, mine, other)


def pick_z(z_ref, keep, got, *pieces):
    for c, ref in enumerate(pieces):
        at = lax.bitwise_xor(z_ref[0], c)
        ref[...] = plus(keep[at], got[at])


def sum_kernel(*refs):
    refs[-1][...] = add_all([ref[...] for ref in refs[:-1]])


def bwd_kernel(
    hpd,
    hl,
    r_ref,
    start_ref,
    do_recv,
    k_hbm,
    v_hbm,
    kt_hbm,
    qtz_hbm,
    ot,
    lse,
    rank_row,
    dt_out,
    do_scr,
    dotz,
    dots,
    code_col,
    code_row,
    dq_acc,
    dk_acc,
    dv_acc,
    p_scr,
    ds_scr,
    pairs,
    k_in,
    v_in,
    kt_in,
    qtz,
    sems,
):
    loads = [
        pltpu.make_async_copy(src, dst, sems.at[i])
        for i, (src, dst) in enumerate(
            ((k_hbm, k_in), (v_hbm, v_in), (kt_hbm, kt_in), (qtz_hbm, qtz))
        )
    ]
    for load in loads:
        load.start()
    feats = do_recv.shape[0] // hpd
    count = do_recv.shape[1]
    total = do_scr.shape[0]
    cl = hl * HD
    r = r_ref[0]

    for s in range(hpd):
        for k in range(feats):
            at = (s * feats + k) * count
            do_scr[at : at + count, :] = do_recv[k * hpd + lax.rem(r - s + hpd, hpd)]
    starts = [start_ref[c].astype(F32) for c in range(1, CLASSES)]
    code_col[...] = codes(iota((total, LANES), 0), starts)
    code_row[...] = codes(iota((8, total), 1), starts)
    dotz[...] = jnp.zeros_like(dotz)

    def arrange(b, _):
        at = pl.multiple_of(b * PB, PB)
        block = jnp.transpose(dot(permute_block(rank_row, at, PB, total), do_scr[...]))
        prod = block * ot[:, pl.ds(at, PB)].astype(F32)
        for h in range(hl):
            sub = (h % 2) * HD
            rows = slice(h * HD, (h + 1) * HD)
            dotz[h, sub : sub + HD, pl.ds(at, PB)] = block[rows].astype(BF)
            dots[h : h + 1, pl.ds(at, PB)] = jnp.sum(prod[rows], 0, keepdims=True)
        return 0

    lax.fori_loop(0, total // PB, arrange, 0)
    dq_acc[...] = jnp.zeros_like(dq_acc)
    dk_acc[...] = jnp.zeros_like(dk_acc)
    dv_acc[...] = jnp.zeros_like(dv_acc)

    def list_keys(b, filled):
        t0, t1 = tile_range(start_ref, b * KB, KB, QB)

        def put(t, i):
            pairs[i] = b * 4096 + t
            return i + 1

        return lax.fori_loop(t0, t1, put, filled)

    filled = lax.fori_loop(0, total // KB, list_keys, jnp.int32(0))
    for load in loads:
        load.wait()

    def places(i):
        b, t = pairs[i] // 4096, lax.rem(pairs[i], 4096)
        return pl.ds(pl.multiple_of(b * KB, KB), KB), pl.ds(pl.multiple_of(t * QB, QB), QB)

    def scores(i):
        kt, at = places(i)
        ccol = code_col[kt, :]
        seen = jnp.concatenate([ccol] * (QB // LANES), -1) == code_row[0:1, at]
        for h in range(hl):
            cols = slice(h // 2 * LANES, (h // 2 + 1) * LANES)
            s = dot(k_in[kt, cols], qtz[h, :, at])
            p = jnp.where(seen, jnp.exp(s - lse[h : h + 1, at]), 0.0)
            dp = dot(v_in[kt, cols], dotz[h, :, at])
            p_scr[h] = p.astype(BF)
            ds_scr[h] = (p * (dp - dots[h : h + 1, at])).astype(BF)

    def collect(i):
        kt, at = places(i)
        for h in range(hl):
            rows = slice(h * HD, (h + 1) * HD)
            own = slice((h % 2) * HD, (h % 2 + 1) * HD)
            ds = ds_scr[h]
            dv_acc[rows, kt] += dot_nt(dotz[h, own, at], p_scr[h])
            dk_acc[rows, kt] += dot_nt(qtz[h, own, at], ds)
            dq_acc[rows, at] += dot(kt_in[rows, kt], ds)

    def step(i, _):
        scores(i)
        collect(i)
        return 0

    lax.fori_loop(0, filled, step, 0)
    dt_out[:cl, :] = (dq_acc[...] * SCALING).astype(BF)
    dt_out[cl : 2 * cl, :] = dk_acc[...].astype(BF)
    dt_out[2 * cl :, :] = dv_acc[...].astype(BF)


def dh_kernel(hpd, r_ref, dt, w_in, rank_col, *refs):
    dh_outs, dht = refs[:-1], refs[-1]
    part, count, width = dh_outs[0].shape
    cuts = len(dh_outs) // hpd
    feats = cuts * part
    total = dt.shape[1]
    cl = dt.shape[0] // 3
    w3 = jnp.concatenate([head_columns(w_in, r_ref[0], cl, j) for j in range(3)], 1)
    for b in range(total // PB):
        at = slice(b * PB, (b + 1) * PB)
        dht[:, at] = dot(w3, dt[:, at]).astype(BF)
    group = feats // 2
    for blk in range(total // (group * count)):
        at = blk * group * count
        hot = unpermute_block(rank_col[at : at + group * count, :], total)
        o = dot_nt(hot, dht[...]).astype(BF)
        for j in range(group):
            s, k = divmod(blk * group + j, feats)
            dh_outs[cuts * s + k // part][k % part] = o[j * count : (j + 1) * count]


SUB = 16
CUTS = 4


def q_rows(cl, width):
    return SUB * (-(-6 * cl // width)) + SUB


def dw_kernel(r_ref, x_ref, y_ref, z_ref, dt, nt, w_in, g1, b1, *refs):
    x = x_ref[0]
    width, total = nt.shape
    cols = dt.shape[0]
    cl = cols // 3
    a_keep, a_got, c_keep, c_got, q_keep, q_send, a_mine, a_other, c_mine, c_other = refs[:10]
    m_scr, dw_scr = refs[10:]
    split_y(y_ref[0], a_keep, a_got, a_mine, a_other)
    top_split(z_ref, c_keep, c_got, c_mine, c_other)
    feats = q_keep.shape[0]
    for c in range(3):
        rows = slice(c * cl, (c + 1) * cl)
        m_scr[:, rows] = dot_nt(nt[...], dt[rows, :])
    ones = jnp.ones((8, total), BF)
    sums_row = dot_nt(ones, dt[...])[0:1]
    gcol = jnp.transpose(jnp.broadcast_to(g1[...], (LANES, width)))
    bcol = jnp.transpose(jnp.broadcast_to(b1[...], (LANES, width)))
    gg = jnp.zeros((width, LANES), F32)
    gb = jnp.zeros((width, LANES), F32)
    for j in range(cols // LANES):
        lanes = slice(j * LANES, (j + 1) * LANES)
        first = (j * LANES // cl) * width + r_ref[0] * cl + j * LANES % cl
        w = w_in[:, pl.ds(pl.multiple_of(first, LANES), LANES)].astype(F32)
        m = m_scr[:, lanes]
        gg = gg + w * m
        gb = gb + w * sums_row[:, lanes]
        dw_scr[:, lanes] = (m * gcol + bcol * sums_row[:, lanes]).astype(BF)
    gg = jnp.sum(jnp.transpose(gg), 0, keepdims=True)
    gb = jnp.sum(jnp.transpose(gb), 0, keepdims=True)
    vec = jnp.concatenate([gg, gb, jnp.zeros((SUB - 2, width), F32)], 0).astype(BF)
    per = width // cl
    last = q_keep.shape[1] - SUB
    for e in range(feats):
        for ref, side in ((q_keep, x), (q_send, 1 - x)):
            for s in range(6):
                j, b = divmod(s, 2)
                src = pl.multiple_of((e * 4 + b) * SUB + side * 2 * SUB, SUB)
                to = (s // per) * SUB
                ref[e, to : to + SUB, (s % per) * cl : (s % per + 1) * cl] = dw_scr[
                    pl.ds(src, SUB), j * cl : (j + 1) * cl
                ]
            used = 6 % per
            if used:
                ref[e, last - SUB : last, used * cl :] = jnp.zeros((SUB, width - used * cl), BF)
            ref[e, last:, :] = vec


def gather_kernel(hpd, r_ref, x_ref, *refs):
    same, other = refs[:hpd], refs[hpd : 2 * hpd]
    a_side, a_pair, c_sum, c_pair = refs[2 * hpd : 2 * hpd + 4]
    out, vec, down, up, fqkv, fout, sout, vectors = refs[2 * hpd + 4 :]
    piece = out.shape[0]
    rows, width = same[0].shape
    cl = width // hpd
    r, x = r_ref[0], x_ref[0]
    blocks = piece // SUB
    first = lax.rem(r * blocks, 2)
    from_same = r * blocks // 2 == x
    for s in range(hpd):
        owner = lax.rem(r - s + hpd, hpd)
        for j in range(3):
            lo = 2 * j // hpd * SUB
            to = pl.ds(pl.multiple_of(j * width + owner * cl, LANES), cl)
            for b in range(blocks):
                col = pl.multiple_of((2 * j % hpd + first + b) * cl, LANES)
                at = (slice(lo, lo + SUB), pl.ds(col, cl))
                picked = jnp.where(from_same, same[s][at].astype(F32), other[s][at].astype(F32))
                out[b * SUB : (b + 1) * SUB, to] = picked
    total = same[0][rows - SUB : rows, :].astype(F32)
    for s in range(1, hpd):
        total = total + same[s][rows - SUB : rows, :].astype(F32)
    vec[...] = total[:8]

    down[...] = jnp.where(x == 0, a_side[...].astype(F32), a_pair[...].astype(F32))

    def both(first, size):
        at = slice(first, first + size)
        return c_sum[at, :].astype(F32) + c_pair[at, :].astype(F32)

    for b in range(up.shape[1] // width):
        at = slice(b * piece, (b + 1) * piece)
        block = jnp.where(x == 0, a_pair[at, :].astype(F32), a_side[at, :].astype(F32))
        up[:, b * width : (b + 1) * width] = block
    base = 0
    for ref in (fqkv, fout, sout):
        for b in range(ref.shape[1] // width):
            ref[:, b * width : (b + 1) * width] = both(base, piece)
            base += piece
    vectors[...] = both(base, vectors.shape[0])


def norm_kernel(hpd, *refs):
    parts = refs[:-5]
    x, g1, q_keep, q_got, out = refs[-5:]
    part, count, _w = parts[0].shape
    cuts = len(parts) // hpd
    feats = cuts * part
    for k in range(feats):
        dh = parts[k // part][k % part].astype(F32)
        for s in range(1, hpd):
            dh = dh + parts[cuts * s + k // part][k % part].astype(F32)
        n, r = ln_parts(x[k, :count, :].astype(F32))
        out[k, :count, :] = ln_back(dh, n, r, g1[...]).astype(BF)
        out[k, count:, :] = add_all((q_keep[k], q_got[k]))


def final_kernel(dx1, both, out, q_sum, scr):
    feats = both.shape[0]
    count, _f, width = out.shape
    q_sum[...] = add_all([both[k, count:, :] for k in range(feats)])
    for f in range(feats):
        val = dx1[f * count : (f + 1) * count, :] + both[f, :count, :].astype(F32)
        place(scr, f, count, feats, val)
    out[...] = lift(scr).reshape(count, feats, width)


def rows_kernel(
    hpd,
    me_ref,
    o_recv,
    xt,
    cot_hbm,
    g2,
    b2,
    g3,
    b3,
    ub,
    db,
    wso_hbm,
    wfq_hbm,
    wfo_hbm,
    wup_hbm,
    wdn_hbm,
    *refs,
):
    outs_hbm, scratch = refs[:7], refs[7:-2]
    (wso, wfq, wfo, wup, wdn, cot), scratch = scratch[:6], scratch[6:]
    outs_vmem, scratch = scratch[:7], scratch[7:]
    out, dx1, do_send, a_keep, a_send, b_keep, b_send = outs_vmem
    (
        wide,
        ct,
        o1,
        x1,
        h2,
        qkv,
        o2,
        x2,
        h3,
        u,
        dz,
        dx2,
        do2,
        dqkv,
        pscr,
        tr,
        wblk,
        ubg,
        wdn_scr,
    ) = scratch
    in_sem, out_sem = refs[-2:]
    loads = [
        pltpu.make_async_copy(src, dst, in_sem.at[i])
        for i, (src, dst) in enumerate(
            (
                (cot_hbm, cot),
                (wso_hbm, wso),
                (wfq_hbm, wfq),
                (wfo_hbm, wfo),
                (wup_hbm, wup),
                (wdn_hbm, wdn),
            )
        )
    ]
    for load in loads:
        load.start()
    stores = [
        pltpu.make_async_copy(src, dst, out_sem.at[i])
        for i, (src, dst) in enumerate(zip(outs_vmem, outs_hbm))
    ]
    feats = xt.shape[0]
    count = xt.shape[1] - PAD
    width = xt.shape[2]
    rows = feats * count
    hidden = wup.shape[1]
    n = o_recv.shape[0]
    cl = o_recv.shape[2]
    half = rows // 2
    me = me_ref[0]
    lane = iota((1, LANES), 1)
    part = 16
    tiles = count // part
    size = feats * part

    loads[0].wait()
    lay(wide, cot[...].astype(F32).reshape(rows, width))
    for f in range(feats):
        ct[f * count : (f + 1) * count, :] = take(wide, f, count, feats).astype(BF)
        for c in range(hpd):
            o1[f * count : (f + 1) * count, c * cl : (c + 1) * cl] = o_recv[f * hpd + c]

    loads[1].wait()
    for b in range(2):
        at = slice(b * half, (b + 1) * half)
        x = xt[b * feats // 2 : (b + 1) * feats // 2, :count, :].astype(F32).reshape(half, width)
        v = x + dot(o1[at, :], wso[...])
        x1[at, :] = v
        nn, _r = ln_parts(v)
        h2[at, :] = (nn * g2[...] + b2[...]).astype(BF)

    loads[2].wait()
    qkv3 = qkv

    def qkv_step(c, _):
        cols = pl.ds(pl.multiple_of(c * TILE, TILE), TILE)
        scale = jnp.where(c < width // TILE, SCALING, 1.0)
        y = dot(h2[...], wfq[:, cols])
        qkv3[:, :, cols] = (y * scale).astype(BF).reshape(feats, count, TILE)
        return 0

    lax.fori_loop(0, 3 * width // TILE, qkv_step, 0)

    ri = lax.broadcasted_iota(jnp.int32, (2 * size, size), 0)
    ci = lax.broadcasted_iota(jnp.int32, (2 * size, size), 1)
    same = lax.rem(ri, part) == lax.rem(ci, part)
    low_lane = jnp.where(iota((1, LANES), 1) < HD, 1.0, 0.0).astype(BF)
    high_lane = jnp.where(iota((1, LANES), 1) < HD, 0.0, 1.0).astype(BF)

    def tile_of(ref, at, lo):
        return ref[:, at, lo : lo + LANES].reshape(size, LANES)

    def by_head(v):
        return jnp.concatenate([v * low_lane, v * high_lane], 0)

    def by_head_t(v):
        vt = jnp.transpose(v)
        zero = jnp.zeros((HD, size), BF)
        return jnp.concatenate(
            [jnp.concatenate([vt[:HD], zero], 0), jnp.concatenate([zero, vt[HD:]], 0)], 1
        )

    def side(v):
        return jnp.concatenate([v[:size], v[size:]], 1)

    def per_head(v, fn):
        return jnp.concatenate(
            [jnp.broadcast_to(fn(v[i * size : (i + 1) * size]), (size, size)) for i in (0, 1)], 0
        )

    def feat_fwd(t, _):
        at = pl.ds(pl.multiple_of(t * part, part), part)
        for p2 in range(H // 2):
            lo = p2 * LANES
            q = tile_of(qkv3, at, lo)
            k = tile_of(qkv3, at, width + lo)
            v = tile_of(qkv3, at, 2 * width + lo)
            s = jnp.where(same, dot_nt(by_head(k), q), NEGATIVE)
            e = jnp.exp(s - per_head(s, lambda w: jnp.max(w, 0, keepdims=True)))
            p = (e * per_head(e, lambda w: 1.0 / jnp.sum(w, 0, keepdims=True))).astype(BF)
            pscr[t, p2] = p
            ot = dot(by_head_t(v), p)
            o2[:, at, lo : lo + LANES] = jnp.transpose(ot).astype(BF).reshape(feats, part, LANES)
        return 0

    lax.fori_loop(0, tiles, feat_fwd, 0, unroll=3)

    loads[3].wait()
    for b in range(2):
        at = slice(b * half, (b + 1) * half)
        o = o2[b * feats // 2 : (b + 1) * feats // 2, :, :].reshape(half, width)
        v = x1[at, :] + dot(o, wfo[...])
        x2[at, :] = v
        nn, _r = ln_parts(v)
        h3[at, :] = (nn * g3[...] + b3[...]).astype(BF)

    loads[4].wait()
    loads[5].wait()

    def ffn(c, _):
        cols = pl.ds(pl.multiple_of(c * FT, FT), FT)
        total = jnp.zeros((8, FT), F32)
        for b in range(2):
            at = slice(b * half, (b + 1) * half)
            z = dot(h3[at, :], wup[:, cols]) + ub[0:1, cols]
            w = GELU_C * GELU_A * (z * z) + GELU_C
            cdf = 0.5 * jnp.tanh(z * w) + 0.5
            g = z * cdf
            u[at, cols] = g.astype(BF)
            slope = cdf + g * (1.0 - cdf) * (6.0 * w - 4.0 * GELU_C)
            d = dot_nt(ct[at, :], wdn[cols, :]) * slope
            dz[at, cols] = d.astype(BF)
            total = total + jnp.sum(d.reshape(half // 8, 8, FT), 0)
        ubg[:, cols] = total
        return 0

    lax.fori_loop(0, hidden // FT, ffn, 0)

    vectors = []
    gg = jnp.zeros((1, width), F32)
    gb = jnp.zeros((1, width), F32)
    gd = jnp.zeros((1, width), F32)
    for b in range(2):
        at = slice(b * half, (b + 1) * half)
        y = x2[at, :] + dot(u[at, :], wdn[...]) + db[...]
        for j in range(feats // 2):
            f = b * (feats // 2) + j
            place(wide, f, count, feats, y[j * count : (j + 1) * count])
        dh = dot_nt(dz[at, :], wup[...])
        nn, r = ln_parts(x2[at, :])
        c = ct[at, :].astype(F32)
        gg = gg + jnp.sum(dh * nn, 0, keepdims=True)
        gb = gb + jnp.sum(dh, 0, keepdims=True)
        gd = gd + jnp.sum(c, 0, keepdims=True)
        v = c + ln_back(dh, nn, r, g3[...])
        dx2[at, :] = v
        do2[b * feats // 2 : (b + 1) * feats // 2, :, :] = (
            dot_nt(v.astype(BF), wfo[...]).astype(BF).reshape(feats // 2, count, width)
        )
    out[...] = lift(wide).reshape(count, feats, width).astype(BF)
    stores[0].start()
    vectors = [gg, gb, gd]

    core = lax.rem(me, 2)

    def slot(pos):
        at, other = divmod(pos, 2)
        refs = (a_send, b_send) if other else (a_keep, b_keep)
        return refs, at, 2 * at + (1 - core if other else core)

    piece = width // n
    fpiece = hidden // n

    def spread(group, base):
        for pos in range(n):
            refs, at, d = slot(pos)
            src = pl.multiple_of(d * piece, piece)
            refs[group][at, base : base + piece, :] = wblk[pl.ds(src, piece), :]

    base = 0
    for b in range(hidden // width):
        tr[...] = flip(u[:, b * width : (b + 1) * width])
        wdn_scr[b * width : (b + 1) * width, :] = dot(tr[...], ct[...]).astype(BF)
    for pos in range(n):
        refs, at, d = slot(pos)
        src = pl.multiple_of(d * fpiece, fpiece)
        refs[0][at, base : base + fpiece, :] = wdn_scr[pl.ds(src, fpiece), :]
    base += fpiece
    tr[...] = flip(h3[...])
    for b in range(hidden // width):
        wblk[...] = dot(tr[...], dz[:, b * width : (b + 1) * width]).astype(BF)
        spread(0, base)
        base += piece
    stores[3].start()
    stores[4].start()

    def feat_bwd(t, _):
        at = pl.ds(pl.multiple_of(t * part, part), part)
        for p2 in range(H // 2):
            lo = p2 * LANES
            q = tile_of(qkv3, at, lo)
            k = tile_of(qkv3, at, width + lo)
            v = tile_of(qkv3, at, 2 * width + lo)
            g = tile_of(do2, at, lo)
            p = pscr[t, p2]
            pf = p.astype(F32)
            dp = dot_nt(by_head(v), g)
            ds = pf * (dp - per_head(pf * dp, lambda w: jnp.sum(w, 0, keepdims=True)))
            ds = ds.astype(BF)
            dv = dot(side(p), by_head(g))
            dk = dot(side(ds), by_head(q))
            dq = jnp.transpose(dot(by_head_t(k), ds)) * SCALING
            for j, d in enumerate((dq, dk, dv)):
                dqkv[:, at, j * width + lo : j * width + lo + LANES] = d.astype(BF).reshape(
                    feats, part, LANES
                )
        return 0

    lax.fori_loop(0, tiles, feat_bwd, 0, unroll=3)

    gg = jnp.zeros((1, width), F32)
    gb = jnp.zeros((1, width), F32)
    for b in range(2):
        at = slice(b * half, (b + 1) * half)
        d = dqkv[b * feats // 2 : (b + 1) * feats // 2, :, :].reshape(half, 3 * width)
        dh = dot_nt(d, wfq[...])
        nn, r = ln_parts(x1[at, :])
        gg = gg + jnp.sum(dh * nn, 0, keepdims=True)
        gb = gb + jnp.sum(dh, 0, keepdims=True)
        v = dx2[at, :] + ln_back(dh, nn, r, g2[...])
        dx1[at, :] = v
        g = dot_nt(v.astype(BF), wso[...]).astype(BF)
        for j in range(feats // 2):
            f = b * (feats // 2) + j
            for c in range(hpd):
                do_send[f * hpd + c] = g[j * count : (j + 1) * count, c * cl : (c + 1) * cl]
    stores[1].start()
    stores[2].start()
    vectors = [gg, gb] + vectors

    base = 0
    tr[...] = flip(h2[...])
    for b in range(3):
        d = dqkv[:, :, b * width : (b + 1) * width].reshape(rows, width)
        wblk[...] = dot(tr[...], d).astype(BF)
        spread(1, base)
        base += piece
    tr[...] = flip(o2[...].reshape(rows, width))
    wblk[...] = dot(tr[...], dx2[...].astype(BF)).astype(BF)
    spread(1, base)
    base += piece
    tr[...] = flip(o1[...])
    wblk[...] = dot(tr[...], dx1[...].astype(BF)).astype(BF)
    spread(1, base)
    base += piece
    ubs = jnp.sum(ubg[...], 0, keepdims=True)
    vectors = vectors + [ubs[:, b * width : (b + 1) * width] for b in range(hidden // width)]
    vec = jnp.concatenate(vectors + [jnp.zeros((16 - len(vectors), width), F32)], 0).astype(BF)
    for pos in range(n):
        refs, at, _d = slot(pos)
        refs[1][at, base : base + 16, :] = vec
    stores[5].start()
    stores[6].start()
    for store in stores:
        store.wait()


def solution(mesh):
    n = mesh.shape["samp"]
    groups = mesh.shape["grp"]
    gbits = groups.bit_length() - 1
    tie = lax.optimization_barrier
    swap_core = [(d, d ^ 1) for d in range(n)]
    swap_y = [(d, d ^ 2) for d in range(n)]
    same_core = [[2 * k + c for k in range(n // 2)] for c in (0, 1)]

    def swap_grp(v, bit=0):
        return lax.ppermute(v, "grp", [(d, d ^ (1 << bit)) for d in range(groups)])

    def rest_of_grp(v):
        for bit in range(1, gbits):
            v = (v.astype(F32) + swap_grp(v, bit).astype(F32)).astype(BF)
        return v

    def body(
        tokens,
        segments,
        cotangent,
        first_gain,
        first_shift,
        sample_qkv,
        sample_out,
        second_gain,
        second_shift,
        feature_qkv,
        feature_out,
        third_gain,
        third_shift,
        up_weight,
        up_bias,
        down_weight,
        down_bias,
    ):
        count, feats, width = tokens.shape[1:]
        hidden = up_weight.shape[1]
        rows = count * feats
        hpd = n // feats
        hl = H // hpd
        cl = hl * HD
        total = n * count
        heads8 = 8
        me = lax.axis_index("samp")
        r = lax.rem(me, hpd)
        x = lax.rem(lax.axis_index("grp"), 2)
        y, z = (me >> 1) & 1, me >> 2
        r1, me1, x1, y1, z1 = (v.reshape(1).astype(jnp.int32) for v in (r, me, x, y, z))
        peers = [[q + hpd * k for k in range(feats)] for q in range(hpd)]
        g1, b1, g2, b2, g3, b3, ub, db = (
            v.reshape(1, -1)
            for v in (
                first_gain,
                first_shift,
                second_gain,
                second_shift,
                third_gain,
                third_shift,
                up_bias,
                down_bias,
            )
        )

        def shift(s):
            return [(d, d // hpd * hpd + (d % hpd + s) % hpd) for d in range(n)]

        (xt,) = call(
            pack_kernel,
            [((feats, count + PAD, width), BF)],
            [pltpu.VMEM((width // LANES, rows, LANES), F32)],
            tokens[0],
            segments,
        )
        mine = lax.all_to_all(xt, "samp", 0, 0, tiled=True, axis_index_groups=peers)
        xparts = [mine] + [lax.ppermute(mine, "samp", shift(s)) for s in range(1, hpd)]

        o_send, xs, ot, lse, rank_row, rank_col, starts = call(
            functools.partial(fwd_kernel, hpd, hl),
            [
                ((n, count, cl), BF),
                ((total, width), BF),
                ((cl, total), BF),
                ((heads8, total), F32),
                ((8, total), F32),
                ((total, LANES), F32),
                ((8,), jnp.int32),
            ],
            [
                pltpu.VMEM((total, width), BF),
                pltpu.VMEM((total, LANES), F32),
                pltpu.VMEM((hl, LANES, total), BF),
                pltpu.VMEM((total, cl), BF),
                pltpu.VMEM((hl, HD + 16, total), BF),
                pltpu.VMEM((total, cl), BF),
                pltpu.VMEM((total, LANES), F32),
                pltpu.VMEM((8, total), F32),
                pltpu.VMEM((hl, HD + 16, TQ), F32),
                pltpu.VMEM((hl, 8, TQ), F32),
                pltpu.VMEM((hl, total, TQ), F32),
                pltpu.VMEM((cl, width), BF),
                pltpu.VMEM((cl, width), BF),
            ],
            r1,
            *xparts,
            g1,
            b1,
            sample_qkv,
            smem=(0,),
            smem_out=(6,),
            vmem=28,
        )
        o_recv = lax.all_to_all(o_send, "samp", 0, 0, tiled=True)

        piece = width // n
        fpiece = hidden // n
        apieces = fpiece + piece * (hidden // width)
        bpieces = piece * 5 + 16
        vm = pltpu.VMEM
        out, dx1, do_send, a_keep, a_send, b_keep, b_send = call(
            functools.partial(rows_kernel, hpd),
            [
                ((count, feats, width), BF),
                ((rows, width), F32),
                ((n, count, cl), BF),
                ((n // 2, apieces, width), BF),
                ((n // 2, apieces, width), BF),
                ((n // 2, bpieces, width), BF),
                ((n // 2, bpieces, width), BF),
            ],
            [
                vm((width, width), BF),
                vm((width, 3 * width), BF),
                vm((width, width), BF),
                vm((width, hidden), BF),
                vm((hidden, width), BF),
                vm((count, feats, width), BF),
                vm((count, feats, width), BF),
                vm((rows, width), F32),
                vm((n, count, cl), BF),
                vm((n // 2, apieces, width), BF),
                vm((n // 2, apieces, width), BF),
                vm((n // 2, bpieces, width), BF),
                vm((n // 2, bpieces, width), BF),
                vm((width // LANES, rows, LANES), F32),
                vm((rows, width), BF),
                vm((rows, width), BF),
                vm((rows, width), F32),
                vm((rows, width), BF),
                vm((feats, count, 3 * width), BF),
                vm((feats, count, width), BF),
                vm((rows, width), F32),
                vm((rows, width), BF),
                vm((rows, hidden), BF),
                vm((rows, hidden), BF),
                vm((rows, width), F32),
                vm((feats, count, width), BF),
                vm((feats, count, 3 * width), BF),
                vm((count // 16, H // 2, 32 * feats, 16 * feats), BF),
                vm((width, rows), BF),
                vm((width, width), BF),
                vm((8, hidden), F32),
                vm((hidden, width), BF),
                pltpu.SemaphoreType.DMA((6,)),
                pltpu.SemaphoreType.DMA((7,)),
            ],
            me1,
            o_recv,
            xt,
            cotangent[0],
            g2,
            b2,
            g3,
            b3,
            ub,
            db,
            sample_out,
            feature_qkv,
            feature_out,
            up_weight,
            down_weight,
            smem=(0,),
            hbm=(3, 10, 11, 12, 13, 14),
            hbm_out=tuple(range(7)),
            vmem=48,
        )
        a_got = lax.ppermute(a_send, "samp", swap_core)
        b_got = lax.ppermute(b_send, "samp", swap_core)
        do_recv = lax.all_to_all(do_send, "samp", 0, 0, tiled=True)

        qr = q_rows(cl, width)
        half = apieces // 2
        zs = n // 4

        def along_z(pieces, unit):
            return [pieces[0]] + [
                lax.ppermute(pieces[c], "samp", [(d, d ^ (unit * c)) for d in range(n)])
                for c in range(1, len(pieces))
            ]

        am, ao, cm, co = call(
            first_sums,
            [((n // 2, half, width), BF)] * 2 + [((n // 4, bpieces, width), BF)] * 2,
            [],
            x1,
            y1,
            a_keep,
            a_got,
            b_keep,
            b_got,
            smem=(0, 1),
            vmem=16,
        )
        ag, cg = swap_grp(ao), lax.ppermute(co, "samp", swap_y)
        xs_after, _ = tie((xs, am))
        k_all, v_all, kt_all, qtz, nt = call(
            functools.partial(prep_kernel, hl),
            [
                ((total, cl), BF),
                ((total, cl), BF),
                ((cl, total), BF),
                ((hl, LANES, total), BF),
                ((width, total), BF),
            ],
            [vm((cl, width), BF), vm((cl, width), BF)],
            r1,
            xs_after,
            g1,
            b1,
            sample_qkv,
            smem=(0,),
            vmem=58,
        )
        (dt,) = call(
            functools.partial(bwd_kernel, hpd, hl),
            [((3 * cl, total), BF)],
            [
                vm((total, cl), BF),
                vm((hl, LANES, total), BF),
                vm((8, total), F32),
                vm((total, LANES), F32),
                vm((8, total), F32),
                vm((cl, total), F32),
                vm((cl, total), F32),
                vm((cl, total), F32),
                vm((hl, KB, QB), BF),
                vm((hl, KB, QB), BF),
                pltpu.SMEM(((total // KB) * (total // QB),), jnp.int32),
                vm((total, cl), BF),
                vm((total, cl), BF),
                vm((cl, total), BF),
                vm((hl, LANES, total), BF),
                pltpu.SemaphoreType.DMA((4,)),
            ],
            r1,
            starts,
            do_recv,
            k_all,
            v_all,
            kt_all,
            qtz,
            ot,
            lse,
            rank_row,
            smem=(0, 1),
            hbm=(3, 4, 5, 6),
            vmem=58,
        )
        am, ag, cm, cg, _ = tie((am, ag, cm, cg, dt))
        q_keep, q_send, am, ao, cm, co = call(
            dw_kernel,
            [((feats, qr, width), BF)] * 2
            + [((n // 4, half, width), BF)] * 2
            + [((zs // 2, bpieces, width), BF)] * 2,
            [vm((width, 3 * cl), F32), vm((width, 3 * cl), BF)],
            r1,
            x1,
            y1,
            z1,
            dt,
            nt,
            sample_qkv,
            g1,
            b1,
            am,
            ag,
            cm,
            cg,
            smem=(0, 1, 2, 3),
            vmem=16,
        )
        ag = lax.ppermute(ao, "samp", swap_y)
        cg = lax.ppermute(co, "samp", [(d, d ^ (n // 2)) for d in range(n)])
        dt, _ = tie((dt, q_send))
        dhs = call(
            functools.partial(dh_kernel, hpd),
            [((feats // CUTS, count, width), BF)] * (CUTS * hpd),
            [vm((width, total), BF)],
            r1,
            dt,
            sample_qkv,
            rank_col,
            smem=(0,),
            vmem=16,
        )
        parts = list(dhs[:CUTS])
        for s in range(1, hpd):
            parts += [lax.ppermute(v, "samp", shift(-s)) for v in dhs[CUTS * s : CUTS * s + CUTS]]
        pieces = call(
            middle_sums,
            [((half, width), BF)] * zs + [((bpieces, width), BF)] * (zs // 2),
            [],
            z1,
            am,
            ag,
            cm,
            cg,
            smem=(0,),
        )
        parts[0], _ = tie((parts[0], pieces[0]))
        a_pieces, c_pieces = along_z(pieces[:zs], 4), along_z(pieces[zs:], 4)
        (both,) = call(
            functools.partial(norm_kernel, hpd),
            [((feats, count + qr, width), BF)],
            [],
            *parts,
            mine,
            g1,
            q_keep,
            swap_grp(q_send),
            vmem=10,
        )
        both_send, *ends = tie((both, *a_pieces, *c_pieces))
        a_pieces, c_pieces = ends[:zs], ends[zs:]
        both = lax.all_to_all(both_send, "samp", 0, 0, tiled=True, axis_index_groups=peers)

        def last_steps(*pieces):
            (c_sum,) = call(sum_kernel, [((bpieces, width), BF)], [], *pieces[zs:])
            c_sum = rest_of_grp(c_sum)
            (a_side,) = call(sum_kernel, [((half, width), BF)], [], *pieces[:zs])
            a_side = rest_of_grp(a_side)
            return a_side, swap_grp(a_side), c_sum, swap_grp(c_sum)

        terms = (*a_pieces, *c_pieces)
        parts_summed = last_steps(*tie((*terms, both_send))[: len(terms)])
        grad_tokens, q_sum = call(
            final_kernel,
            [((count, feats, width), F32), ((qr, width), BF)],
            [vm((width // LANES, rows, LANES), F32)],
            dx1,
            both,
            vmem=12,
        )
        q_sum = rest_of_grp(q_sum)

        def from_peer(s, other):
            if not s and not other:
                return q_sum
            pairs = [
                (g * n + d, (g ^ other) * n + e) for g in range(groups) for d, e in shift(s)
            ]
            return lax.ppermute(q_sum, ("grp", "samp"), pairs)

        peers_same = [from_peer(s, 0) for s in range(hpd)]
        peers_other = [from_peer(s, 1) for s in range(hpd)]
        grad_sample_qkv, vec_sum, grad_down, grad_up, grad_fqkv, grad_fout, grad_sout, vu = call(
            functools.partial(gather_kernel, hpd),
            [
                ((piece, 3 * width), F32),
                ((8, width), F32),
                ((fpiece, width), F32),
                ((piece, hidden), F32),
                ((piece, 3 * width), F32),
                ((piece, width), F32),
                ((piece, width), F32),
                ((16, width), F32),
            ],
            [],
            r1,
            x1,
            *peers_same,
            *peers_other,
            *parts_summed,
            smem=(0, 1),
        )

        def own(v):
            return lax.dynamic_slice_in_dim(v, me * (v.shape[0] // n), v.shape[0] // n, 0)

        def own_rows(v):
            return lax.dynamic_slice_in_dim(v, me * piece, piece, 1)

        five = own_rows(vu[:5])
        two = own_rows(vec_sum[:2])
        vectors = [five[i] for i in range(5)]
        vectors.append(own(vu[5 : 5 + hidden // width].reshape(-1)))
        return (
            out[None],
            grad_tokens[None],
            two[0],
            two[1],
            grad_sample_qkv,
            grad_sout,
            vectors[0],
            vectors[1],
            grad_fqkv,
            grad_fout,
            vectors[2],
            vectors[3],
            grad_up,
            vectors[5],
            grad_down,
            vectors[4],
        )

    rep = P()
    data = P("grp", "samp", None, None)
    line = P("samp")
    flat = P("samp", None)
    in_specs = (data, P("grp", "samp"), data) + (rep,) * 14
    out_specs = (
        data,
        data,
        line,
        line,
        flat,
        flat,
        line,
        line,
        flat,
        flat,
        line,
        line,
        flat,
        line,
        flat,
        line,
    )
    return jax.shard_map(body, mesh=mesh, in_specs=in_specs, out_specs=out_specs, check_vma=False)
```

```python
import functools
import math

import jax
import jax.numpy as jnp
from jax import lax
from jax.experimental import pallas as pl
from jax.experimental.pallas import tpu as pltpu
from jax.sharding import PartitionSpec as P

H = 8
HD = 64
EPSILON = 1e-05
SCALING = 0.125
NEGATIVE = -1e30
BF = jnp.bfloat16
F32 = jnp.float32
TILE = 256
FT = 512
PB = 512
KB = 256
QB = 256
TQ = 256
TK = 256
LANES = 128
PAD = 8
GELU_C = math.sqrt(2.0 / math.pi)
GELU_A = 0.044715
MIB = 1024 * 1024
CLASSES = 5


def dot(a, b):
    return jnp.dot(a, b, preferred_element_type=F32)


def dot_nt(a, b):
    return lax.dot_general(a, b, (((1,), (1,)), ((), ())), preferred_element_type=F32)


def dot_tn(a, b):
    return lax.dot_general(a, b, (((0,), (0,)), ((), ())), preferred_element_type=F32)


def ln_parts(v):
    c = v - jnp.mean(v, -1, keepdims=True)
    r = lax.rsqrt(jnp.mean(c * c, -1, keepdims=True) + EPSILON)
    return c * r, r


def ln_back(dh, n, r, g):
    e = dh * g
    return r * (e - jnp.mean(e, -1, keepdims=True) - n * jnp.mean(e * n, -1, keepdims=True))


def flip(v):
    return jnp.transpose(v)


def head_columns(w, r, cl, which):
    first = which * (w.shape[1] // 3) + r * cl
    return w[:, pl.ds(pl.multiple_of(first, LANES), cl)]


def lay(scr, v):
    for a in range(scr.shape[0]):
        scr[a] = v[:, a * LANES : (a + 1) * LANES]


def lift(scr):
    return jnp.concatenate([scr[a] for a in range(scr.shape[0])], -1)


def take(scr, first, count, step):
    return jnp.concatenate(
        [scr[a, pl.ds(first, count, stride=step), :] for a in range(scr.shape[0])], -1
    )


def place(scr, first, count, step, v):
    for a in range(scr.shape[0]):
        scr[a, pl.ds(first, count, stride=step), :] = v[:, a * LANES : (a + 1) * LANES]


def iota(shape, dim):
    return lax.broadcasted_iota(jnp.int32, shape, dim).astype(F32)


def call(fn, outs, scratch, *args, smem=(), smem_out=(), hbm=(), hbm_out=(), vmem=16):
    def spec(space):
        return pl.BlockSpec(memory_space=space)

    def place_of(i, scalars, far):
        return spec(pltpu.SMEM if i in scalars else pl.ANY if i in far else pltpu.VMEM)

    in_specs = [place_of(i, smem, hbm) for i in range(len(args))]
    out_specs = [place_of(i, smem_out, hbm_out) for i in range(len(outs))]
    return pl.pallas_call(
        fn,
        out_shape=[jax.ShapeDtypeStruct(*o) for o in outs],
        in_specs=in_specs,
        out_specs=out_specs,
        scratch_shapes=scratch,
        compiler_params=pltpu.CompilerParams(vmem_limit_bytes=vmem * MIB),
        cost_estimate=pl.CostEstimate(flops=0, bytes_accessed=0, transcendentals=0),
    )(*args)


def pack_kernel(tok, seg, out, scr):
    count, feats, width = tok.shape
    lay(scr, tok[...].astype(F32).reshape(count * feats, width))
    row = seg[...].astype(F32)
    for f in range(feats):
        out[f, :count, :] = take(scr, f, count, feats).astype(BF)
        out[f, count:, :] = jnp.zeros((PAD, width), BF)
        out[f, count:, :count] = jnp.broadcast_to(row, (PAD, count)).astype(BF)


def codes(pos, starts):
    cls = jnp.zeros_like(pos)
    for st in starts:
        cls = cls + jnp.where(pos >= st, 1.0, 0.0)
    return jnp.where(cls >= CLASSES - 1, pos + CLASSES, cls)


def tile_range(start_ref, first, size, tile):
    last = first + size - 1
    lo = jnp.int32(0)
    hi = start_ref[1]
    for c in range(1, CLASSES - 1):
        st = start_ref[c]
        lo = jnp.where(first >= st, st, lo)
        hi = jnp.where(last >= st, start_ref[c + 1], hi)
    pad = start_ref[CLASSES - 1]
    lo = jnp.where(first >= pad, first, lo)
    hi = jnp.where(last >= pad, first + size, hi)
    return lo // tile, (hi + tile - 1) // tile


def permute_block(rank_row, first, rows, total):
    pos = iota((rows, LANES), 0) + first.astype(F32)
    parts = []
    for j in range(total // LANES):
        hit = rank_row[0:1, j * LANES : (j + 1) * LANES] == pos
        parts.append(jnp.where(hit, 1.0, 0.0).astype(BF))
    return jnp.concatenate(parts, -1)


def unpermute_block(rank_col, total):
    rows = rank_col.shape[0]
    parts = []
    for j in range(total // LANES):
        pos = iota((1, LANES), 1) + float(j * LANES)
        parts.append(jnp.where(rank_col == pos, 1.0, 0.0).astype(BF))
    return jnp.concatenate(parts, -1)


def fwd_kernel(hpd, hl, r_ref, *refs):
    xparts = refs[:hpd]
    (g1, b1, w_in) = refs[hpd : hpd + 3]
    (o_send, xs_out, ot_out, lse_out, rank_row, rank_col, start_ref) = refs[hpd + 3 : hpd + 10]
    (x_scr, seg_scr, qtz, k_scr, vt, o_scr, code_col, code_row, acc, top, s_scr) = refs[
        hpd + 10 : hpd + 21
    ]
    wqt, wvt = refs[hpd + 21 :]
    feats = xparts[0].shape[0]
    count = xparts[0].shape[1] - PAD
    total = x_scr.shape[0]
    cl = hl * HD
    r = r_ref[0]
    chunks = total // LANES
    wqt[...] = flip(head_columns(w_in, r, cl, 0)) * BF(SCALING)
    wvt[...] = flip(head_columns(w_in, r, cl, 2))

    for s in range(hpd):
        for k in range(feats):
            at = (s * feats + k) * count
            x_scr[at : at + count, :] = xparts[s][k, :count, :]
            row = xparts[s][k, count : count + PAD, :LANES].astype(F32)[0:1]
            col = jnp.transpose(jnp.broadcast_to(row, (LANES, LANES)))
            seg_scr[at : at + count, :] = col[:count, :]

    seg = seg_scr[...]
    cls = jnp.where(seg < 0.0, float(CLASSES - 1), seg)
    seg_scr[...] = cls * 8192.0 + iota((total, LANES), 0)
    key_rows = []
    for j in range(chunks):
        blk = seg_scr[j * LANES : (j + 1) * LANES, :]
        key_rows.append(jnp.transpose(blk)[0:8, :])

    def count_less(i, carry):
        blk = seg_scr[pl.ds(pl.multiple_of(i * 64, 64), 64), :]
        out = []
        for j in range(chunks):
            less = jnp.where(blk < key_rows[j][0:1], 1.0, 0.0)
            out.append(carry[j] + jnp.sum(less.reshape(8, 8, LANES), 0))
        return tuple(out)

    ranks = lax.fori_loop(
        0, total // 64, count_less, tuple(jnp.zeros((8, LANES), F32) for _ in range(chunks))
    )
    for j in range(chunks):
        row = jnp.sum(ranks[j], 0, keepdims=True)
        rank_row[:, j * LANES : (j + 1) * LANES] = jnp.broadcast_to(row, (8, LANES))
        rank_col[j * LANES : (j + 1) * LANES, :] = jnp.transpose(
            jnp.broadcast_to(row, (LANES, LANES))
        )
    starts = []
    keys = jnp.concatenate([k[0:1] for k in key_rows], 0)
    for c in range(1, CLASSES):
        st = jnp.sum(jnp.where(keys < c * 8192.0, 1.0, 0.0))
        starts.append(st)
        start_ref[c] = st.astype(jnp.int32)
    start_ref[0] = jnp.int32(0)
    for c in range(CLASSES, 8):
        start_ref[c] = jnp.int32(total)
    code_col[...] = codes(iota((total, LANES), 0), starts)
    code_row[...] = codes(iota((8, total), 1), starts)

    qtz[...] = jnp.zeros_like(qtz)
    ones = jnp.where(iota((16, total), 0) == 0.0, 1.0, 0.0).astype(BF)
    for h in range(hl):
        vt[h, HD:, :] = ones

    def project(b, _):
        at = pl.multiple_of(b * PB, PB)
        block = dot(permute_block(rank_row, at, PB, total), x_scr[...])
        xs_out[pl.ds(at, PB), :] = block.astype(BF)
        n, _r = ln_parts(block)
        h1 = (n * g1[...] + b1[...]).astype(BF)
        qt = dot_nt(wqt[...], h1).astype(BF)
        k_scr[pl.ds(at, PB), :] = dot(h1, head_columns(w_in, r, cl, 1)).astype(BF)
        vv = dot_nt(wvt[...], h1).astype(BF)
        for h in range(hl):
            sub = (h % 2) * HD
            qtz[h, sub : sub + HD, pl.ds(at, PB)] = qt[h * HD : (h + 1) * HD]
            vt[h, :HD, pl.ds(at, PB)] = vv[h * HD : (h + 1) * HD]
        return 0

    lax.fori_loop(0, total // PB, project, 0)

    def attend(b, _):
        at = pl.multiple_of(b * TQ, TQ)
        t0, t1 = tile_range(start_ref, at, TQ, TK)
        acc[...] = jnp.zeros_like(acc)
        top[...] = jnp.full_like(top, NEGATIVE)
        crow = code_row[0:1, pl.ds(at, TQ)]

        def score(t, _):
            kt = pl.multiple_of(t * TK, TK)
            ccol = code_col[pl.ds(kt, TK), :]
            ccol = jnp.concatenate([ccol] * (TQ // LANES), -1)
            seen = ccol == crow
            for h in range(hl):
                pair = (h // 2) * LANES
                s = dot(k_scr[pl.ds(kt, TK), pair : pair + LANES], qtz[h, :, pl.ds(at, TQ)])
                s = jnp.where(seen, s, NEGATIVE)
                s_scr[h, pl.ds(kt, TK), :] = s
                top[h] = jnp.maximum(top[h], jnp.max(s.reshape(TK // 8, 8, TQ), 0))
            return 0

        lax.fori_loop(t0, t1, score, 0)
        for h in range(hl):
            top[h] = jnp.broadcast_to(jnp.max(top[h], 0, keepdims=True), (8, TQ))

        def mix(t, _):
            kt = pl.multiple_of(t * TK, TK)
            for h in range(hl):
                p = jnp.exp(s_scr[h, pl.ds(kt, TK), :] - top[h, 0:1, :]).astype(BF)
                acc[h] += dot(vt[h, :, pl.ds(kt, TK)], p)
            return 0

        lax.fori_loop(t0, t1, mix, 0)
        outs = []
        for h in range(hl):
            total_h = acc[h, HD : HD + 1, :]
            outs.append(acc[h, :HD, :] / total_h)
            lse_out[h : h + 1, pl.ds(at, TQ)] = top[h, 0:1, :] + jnp.log(total_h)
        ot = jnp.concatenate(outs, 0)
        ot_out[:, pl.ds(at, TQ)] = ot.astype(BF)
        o_scr[pl.ds(at, TQ), :] = jnp.transpose(ot).astype(BF)
        return 0

    lax.fori_loop(0, total // TQ, attend, 0)

    group = feats // 2
    for blk in range(total // (group * count)):
        at = blk * group * count
        hot = unpermute_block(rank_col[at : at + group * count, :], total)
        o = dot(hot, o_scr[...]).astype(BF)
        for j in range(group):
            s, k = divmod(blk * group + j, feats)
            dest = k * hpd + lax.rem(r - s + hpd, hpd)
            o_send[dest] = o[j * count : (j + 1) * count]


def prep_kernel(
    hl,
    r_ref,
    xs,
    g1,
    b1,
    w_in,
    k_out,
    v_out,
    kt_out,
    qtz,
    nt,
    wqt,
    wkt,
):
    total = xs.shape[0]
    cl = hl * HD
    r = r_ref[0]
    wqt[...] = flip(head_columns(w_in, r, cl, 0)) * BF(SCALING)
    wkt[...] = flip(head_columns(w_in, r, cl, 1))
    qtz[...] = jnp.zeros_like(qtz)

    def project(b, _):
        at = pl.multiple_of(b * PB, PB)
        n, _r = ln_parts(xs[pl.ds(at, PB), :].astype(F32))
        h1 = (n * g1[...] + b1[...]).astype(BF)
        nt[:, pl.ds(at, PB)] = jnp.transpose(n.astype(BF))
        qt = dot_nt(wqt[...], h1).astype(BF)
        k_out[pl.ds(at, PB), :] = dot(h1, head_columns(w_in, r, cl, 1)).astype(BF)
        v_out[pl.ds(at, PB), :] = dot(h1, head_columns(w_in, r, cl, 2)).astype(BF)
        kt_out[:, pl.ds(at, PB)] = dot_nt(wkt[...], h1).astype(BF)
        for h in range(hl):
            sub = (h % 2) * HD
            qtz[h, sub : sub + HD, pl.ds(at, PB)] = qt[h * HD : (h + 1) * HD]
        return 0

    lax.fori_loop(0, total // PB, project, 0)


def plus(a, b):
    return (a.astype(F32) + b.astype(F32)).astype(BF)


def first_sums(x_ref, y_ref, a_keep, a_got, c_keep, c_got, a_mine, a_other, c_mine, c_other):
    half = a_mine.shape[1]
    mine = pl.multiple_of(x_ref[0] * half, half)
    other = pl.multiple_of((1 - x_ref[0]) * half, half)

    def step(i, _):
        for ref, first in ((a_mine, mine), (a_other, other)):
            ref[i] = plus(a_keep[i, pl.ds(first, half), :], a_got[i, pl.ds(first, half), :])
        return 0

    lax.fori_loop(0, a_mine.shape[0], step, 0)
    split_y(y_ref[0], c_keep, c_got, c_mine, c_other)


def split_y(y, keep, got, mine, other):
    def step(i, _):
        for ref, at in ((mine, 2 * i + y), (other, 2 * i + 1 - y)):
            ref[i] = plus(keep[at], got[at])
        return 0

    lax.fori_loop(0, mine.shape[0], step, 0)


def top_split(z_ref, keep, got, mine, other):
    chunks = mine.shape[0]
    top = z_ref[0] // chunks
    for j in range(chunks):
        mine[j] = plus(keep[top * chunks + j], got[top * chunks + j])
        other[j] = plus(keep[(1 - top) * chunks + j], got[(1 - top) * chunks + j])


def middle_sums(z_ref, a_keep, a_got, c_keep, c_got, *pieces):
    count = a_keep.shape[0]
    pick_z(z_ref, a_keep, a_got, *pieces[:count])
    for c, ref in enumerate(pieces[count:]):
        at = lax.bitwise_xor(lax.rem(z_ref[0], count // 2), c)
        ref[...] = plus(c_keep[at], c_got[at])


def add_all(terms):
    total = terms[0].astype(F32)
    for term in terms[1:]:
        total = total + term.astype(F32)
    return total.astype(BF)


def pick_y(y_ref, keep, got, mine, other):
    split_y(y_ref[0], keep, got, mine, other)


def pick_z(z_ref, keep, got, *pieces):
    for c, ref in enumerate(pieces):
        at = lax.bitwise_xor(z_ref[0], c)
        ref[...] = plus(keep[at], got[at])


def sum_kernel(*refs):
    refs[-1][...] = add_all([ref[...] for ref in refs[:-1]])


def bwd_kernel(
    hpd,
    hl,
    r_ref,
    start_ref,
    do_recv,
    k_hbm,
    v_hbm,
    kt_hbm,
    qtz_hbm,
    ot,
    lse,
    rank_row,
    dt_out,
    do_scr,
    dotz,
    dots,
    code_col,
    code_row,
    dq_acc,
    dk_acc,
    dv_acc,
    p_scr,
    ds_scr,
    pairs,
    k_in,
    v_in,
    kt_in,
    qtz,
    sems,
):
    loads = [
        pltpu.make_async_copy(src, dst, sems.at[i])
        for i, (src, dst) in enumerate(
            ((k_hbm, k_in), (v_hbm, v_in), (kt_hbm, kt_in), (qtz_hbm, qtz))
        )
    ]
    for load in loads:
        load.start()
    feats = do_recv.shape[0] // hpd
    count = do_recv.shape[1]
    total = do_scr.shape[0]
    cl = hl * HD
    r = r_ref[0]

    for s in range(hpd):
        for k in range(feats):
            at = (s * feats + k) * count
            do_scr[at : at + count, :] = do_recv[k * hpd + lax.rem(r - s + hpd, hpd)]
    starts = [start_ref[c].astype(F32) for c in range(1, CLASSES)]
    code_col[...] = codes(iota((total, LANES), 0), starts)
    code_row[...] = codes(iota((8, total), 1), starts)
    dotz[...] = jnp.zeros_like(dotz)

    def arrange(b, _):
        at = pl.multiple_of(b * PB, PB)
        block = jnp.transpose(dot(permute_block(rank_row, at, PB, total), do_scr[...]))
        prod = block * ot[:, pl.ds(at, PB)].astype(F32)
        for h in range(hl):
            sub = (h % 2) * HD
            rows = slice(h * HD, (h + 1) * HD)
            dotz[h, sub : sub + HD, pl.ds(at, PB)] = block[rows].astype(BF)
            dots[h : h + 1, pl.ds(at, PB)] = jnp.sum(prod[rows], 0, keepdims=True)
        return 0

    lax.fori_loop(0, total // PB, arrange, 0)
    dq_acc[...] = jnp.zeros_like(dq_acc)
    dk_acc[...] = jnp.zeros_like(dk_acc)
    dv_acc[...] = jnp.zeros_like(dv_acc)

    def list_keys(b, filled):
        t0, t1 = tile_range(start_ref, b * KB, KB, QB)

        def put(t, i):
            pairs[i] = b * 4096 + t
            return i + 1

        return lax.fori_loop(t0, t1, put, filled)

    filled = lax.fori_loop(0, total // KB, list_keys, jnp.int32(0))
    for load in loads:
        load.wait()

    def places(i):
        b, t = pairs[i] // 4096, lax.rem(pairs[i], 4096)
        return pl.ds(pl.multiple_of(b * KB, KB), KB), pl.ds(pl.multiple_of(t * QB, QB), QB)

    def scores(i):
        kt, at = places(i)
        ccol = code_col[kt, :]
        seen = jnp.concatenate([ccol] * (QB // LANES), -1) == code_row[0:1, at]
        for h in range(hl):
            cols = slice(h // 2 * LANES, (h // 2 + 1) * LANES)
            s = dot(k_in[kt, cols], qtz[h, :, at])
            p = jnp.where(seen, jnp.exp(s - lse[h : h + 1, at]), 0.0)
            dp = dot(v_in[kt, cols], dotz[h, :, at])
            p_scr[h] = p.astype(BF)
            ds_scr[h] = (p * (dp - dots[h : h + 1, at])).astype(BF)

    def collect(i):
        kt, at = places(i)
        for h in range(hl):
            rows = slice(h * HD, (h + 1) * HD)
            own = slice((h % 2) * HD, (h % 2 + 1) * HD)
            ds = ds_scr[h]
            dv_acc[rows, kt] += dot_nt(dotz[h, own, at], p_scr[h])
            dk_acc[rows, kt] += dot_nt(qtz[h, own, at], ds)
            dq_acc[rows, at] += dot(kt_in[rows, kt], ds)

    def step(i, _):
        scores(i)
        collect(i)
        return 0

    lax.fori_loop(0, filled, step, 0)
    dt_out[:cl, :] = (dq_acc[...] * SCALING).astype(BF)
    dt_out[cl : 2 * cl, :] = dk_acc[...].astype(BF)
    dt_out[2 * cl :, :] = dv_acc[...].astype(BF)


def dh_kernel(hpd, r_ref, dt, w_in, rank_col, *refs):
    dh_outs, dht = refs[:-1], refs[-1]
    part, count, width = dh_outs[0].shape
    cuts = len(dh_outs) // hpd
    feats = cuts * part
    total = dt.shape[1]
    cl = dt.shape[0] // 3
    w3 = jnp.concatenate([head_columns(w_in, r_ref[0], cl, j) for j in range(3)], 1)
    for b in range(total // PB):
        at = slice(b * PB, (b + 1) * PB)
        dht[:, at] = dot(w3, dt[:, at]).astype(BF)
    group = feats // 2
    for blk in range(total // (group * count)):
        at = blk * group * count
        hot = unpermute_block(rank_col[at : at + group * count, :], total)
        o = dot_nt(hot, dht[...]).astype(BF)
        for j in range(group):
            s, k = divmod(blk * group + j, feats)
            dh_outs[cuts * s + k // part][k % part] = o[j * count : (j + 1) * count]


SUB = 16
CUTS = 4


def q_rows(cl, width):
    return SUB * (-(-6 * cl // width)) + SUB


def dw_kernel(r_ref, x_ref, y_ref, z_ref, dt, nt, w_in, g1, b1, *refs):
    x = x_ref[0]
    width, total = nt.shape
    cols = dt.shape[0]
    cl = cols // 3
    a_keep, a_got, c_keep, c_got, q_keep, q_send, a_mine, a_other, c_mine, c_other = refs[:10]
    m_scr, dw_scr = refs[10:]
    split_y(y_ref[0], a_keep, a_got, a_mine, a_other)
    top_split(z_ref, c_keep, c_got, c_mine, c_other)
    feats = q_keep.shape[0]
    for c in range(3):
        rows = slice(c * cl, (c + 1) * cl)
        m_scr[:, rows] = dot_nt(nt[...], dt[rows, :])
    ones = jnp.ones((8, total), BF)
    sums_row = dot_nt(ones, dt[...])[0:1]
    gcol = jnp.transpose(jnp.broadcast_to(g1[...], (LANES, width)))
    bcol = jnp.transpose(jnp.broadcast_to(b1[...], (LANES, width)))
    gg = jnp.zeros((width, LANES), F32)
    gb = jnp.zeros((width, LANES), F32)
    for j in range(cols // LANES):
        lanes = slice(j * LANES, (j + 1) * LANES)
        first = (j * LANES // cl) * width + r_ref[0] * cl + j * LANES % cl
        w = w_in[:, pl.ds(pl.multiple_of(first, LANES), LANES)].astype(F32)
        m = m_scr[:, lanes]
        gg = gg + w * m
        gb = gb + w * sums_row[:, lanes]
        dw_scr[:, lanes] = (m * gcol + bcol * sums_row[:, lanes]).astype(BF)
    gg = jnp.sum(jnp.transpose(gg), 0, keepdims=True)
    gb = jnp.sum(jnp.transpose(gb), 0, keepdims=True)
    vec = jnp.concatenate([gg, gb, jnp.zeros((SUB - 2, width), F32)], 0).astype(BF)
    per = width // cl
    last = q_keep.shape[1] - SUB
    for e in range(feats):
        for ref, side in ((q_keep, x), (q_send, 1 - x)):
            for s in range(6):
                j, b = divmod(s, 2)
                src = pl.multiple_of((e * 4 + b) * SUB + side * 2 * SUB, SUB)
                to = (s // per) * SUB
                ref[e, to : to + SUB, (s % per) * cl : (s % per + 1) * cl] = dw_scr[
                    pl.ds(src, SUB), j * cl : (j + 1) * cl
                ]
            used = 6 % per
            if used:
                ref[e, last - SUB : last, used * cl :] = jnp.zeros((SUB, width - used * cl), BF)
            ref[e, last:, :] = vec


def gather_kernel(hpd, r_ref, x_ref, *refs):
    same, other = refs[:hpd], refs[hpd : 2 * hpd]
    a_side, a_pair, c_sum, c_pair = refs[2 * hpd : 2 * hpd + 4]
    out, vec, down, up, fqkv, fout, sout, vectors = refs[2 * hpd + 4 :]
    piece = out.shape[0]
    rows, width = same[0].shape
    cl = width // hpd
    r, x = r_ref[0], x_ref[0]
    blocks = piece // SUB
    first = lax.rem(r * blocks, 2)
    from_same = r * blocks // 2 == x
    for s in range(hpd):
        owner = lax.rem(r - s + hpd, hpd)
        for j in range(3):
            lo = 2 * j // hpd * SUB
            to = pl.ds(pl.multiple_of(j * width + owner * cl, LANES), cl)
            for b in range(blocks):
                col = pl.multiple_of((2 * j % hpd + first + b) * cl, LANES)
                at = (slice(lo, lo + SUB), pl.ds(col, cl))
                picked = jnp.where(from_same, same[s][at].astype(F32), other[s][at].astype(F32))
                out[b * SUB : (b + 1) * SUB, to] = picked
    total = same[0][rows - SUB : rows, :].astype(F32)
    for s in range(1, hpd):
        total = total + same[s][rows - SUB : rows, :].astype(F32)
    vec[...] = total[:8]

    down[...] = jnp.where(x == 0, a_side[...].astype(F32), a_pair[...].astype(F32))

    def both(first, size):
        at = slice(first, first + size)
        return c_sum[at, :].astype(F32) + c_pair[at, :].astype(F32)

    for b in range(up.shape[1] // width):
        at = slice(b * piece, (b + 1) * piece)
        block = jnp.where(x == 0, a_pair[at, :].astype(F32), a_side[at, :].astype(F32))
        up[:, b * width : (b + 1) * width] = block
    base = 0
    for ref in (fqkv, fout, sout):
        for b in range(ref.shape[1] // width):
            ref[:, b * width : (b + 1) * width] = both(base, piece)
            base += piece
    vectors[...] = both(base, vectors.shape[0])


def norm_kernel(hpd, *refs):
    parts = refs[:-5]
    x, g1, q_keep, q_got, out = refs[-5:]
    part, count, _w = parts[0].shape
    cuts = len(parts) // hpd
    feats = cuts * part
    for k in range(feats):
        dh = parts[k // part][k % part].astype(F32)
        for s in range(1, hpd):
            dh = dh + parts[cuts * s + k // part][k % part].astype(F32)
        n, r = ln_parts(x[k, :count, :].astype(F32))
        out[k, :count, :] = ln_back(dh, n, r, g1[...]).astype(BF)
        out[k, count:, :] = add_all((q_keep[k], q_got[k]))


def final_kernel(dx1, both, out, q_sum, scr):
    feats = both.shape[0]
    count, _f, width = out.shape
    q_sum[...] = add_all([both[k, count:, :] for k in range(feats)])
    for f in range(feats):
        val = dx1[f * count : (f + 1) * count, :] + both[f, :count, :].astype(F32)
        place(scr, f, count, feats, val)
    out[...] = lift(scr).reshape(count, feats, width)


def rows_kernel(
    hpd,
    me_ref,
    o_recv,
    xt,
    cot_hbm,
    g2,
    b2,
    g3,
    b3,
    ub,
    db,
    wso_hbm,
    wfq_hbm,
    wfo_hbm,
    wup_hbm,
    wdn_hbm,
    *refs,
):
    outs_hbm, scratch = refs[:7], refs[7:-2]
    (wso, wfq, wfo, wup, wdn, cot), scratch = scratch[:6], scratch[6:]
    outs_vmem, scratch = scratch[:7], scratch[7:]
    out, dx1, do_send, a_keep, a_send, b_keep, b_send = outs_vmem
    (
        wide,
        ct,
        o1,
        x1,
        h2,
        qkv,
        o2,
        x2,
        h3,
        u,
        dz,
        dx2,
        do2,
        dqkv,
        pscr,
        tr,
        wblk,
        ubg,
        wdn_scr,
    ) = scratch
    in_sem, out_sem = refs[-2:]
    loads = [
        pltpu.make_async_copy(src, dst, in_sem.at[i])
        for i, (src, dst) in enumerate(
            (
                (cot_hbm, cot),
                (wso_hbm, wso),
                (wfq_hbm, wfq),
                (wfo_hbm, wfo),
                (wup_hbm, wup),
                (wdn_hbm, wdn),
            )
        )
    ]
    for load in loads:
        load.start()
    stores = [
        pltpu.make_async_copy(src, dst, out_sem.at[i])
        for i, (src, dst) in enumerate(zip(outs_vmem, outs_hbm))
    ]
    feats = xt.shape[0]
    count = xt.shape[1] - PAD
    width = xt.shape[2]
    rows = feats * count
    hidden = wup.shape[1]
    n = o_recv.shape[0]
    cl = o_recv.shape[2]
    half = rows // 2
    me = me_ref[0]
    lane = iota((1, LANES), 1)
    part = 16
    tiles = count // part
    size = feats * part

    loads[0].wait()
    lay(wide, cot[...].astype(F32).reshape(rows, width))
    for f in range(feats):
        ct[f * count : (f + 1) * count, :] = take(wide, f, count, feats).astype(BF)
        for c in range(hpd):
            o1[f * count : (f + 1) * count, c * cl : (c + 1) * cl] = o_recv[f * hpd + c]

    loads[1].wait()
    for b in range(2):
        at = slice(b * half, (b + 1) * half)
        x = xt[b * feats // 2 : (b + 1) * feats // 2, :count, :].astype(F32).reshape(half, width)
        v = x + dot(o1[at, :], wso[...])
        x1[at, :] = v
        nn, _r = ln_parts(v)
        h2[at, :] = (nn * g2[...] + b2[...]).astype(BF)

    loads[2].wait()
    qkv3 = qkv

    def qkv_step(c, _):
        cols = pl.ds(pl.multiple_of(c * TILE, TILE), TILE)
        scale = jnp.where(c < width // TILE, SCALING, 1.0)
        y = dot(h2[...], wfq[:, cols])
        qkv3[:, :, cols] = (y * scale).astype(BF).reshape(feats, count, TILE)
        return 0

    lax.fori_loop(0, 3 * width // TILE, qkv_step, 0)

    ri = lax.broadcasted_iota(jnp.int32, (2 * size, size), 0)
    ci = lax.broadcasted_iota(jnp.int32, (2 * size, size), 1)
    same = lax.rem(ri, part) == lax.rem(ci, part)
    low_lane = jnp.where(iota((1, LANES), 1) < HD, 1.0, 0.0).astype(BF)
    high_lane = jnp.where(iota((1, LANES), 1) < HD, 0.0, 1.0).astype(BF)

    def tile_of(ref, at, lo):
        return ref[:, at, lo : lo + LANES].reshape(size, LANES)

    def by_head(v):
        return jnp.concatenate([v * low_lane, v * high_lane], 0)

    def by_head_t(v):
        vt = jnp.transpose(v)
        zero = jnp.zeros((HD, size), BF)
        return jnp.concatenate(
            [jnp.concatenate([vt[:HD], zero], 0), jnp.concatenate([zero, vt[HD:]], 0)], 1
        )

    def side(v):
        return jnp.concatenate([v[:size], v[size:]], 1)

    def per_head(v, fn):
        return jnp.concatenate(
            [jnp.broadcast_to(fn(v[i * size : (i + 1) * size]), (size, size)) for i in (0, 1)], 0
        )

    def feat_fwd(t, _):
        at = pl.ds(pl.multiple_of(t * part, part), part)
        for p2 in range(H // 2):
            lo = p2 * LANES
            q = tile_of(qkv3, at, lo)
            k = tile_of(qkv3, at, width + lo)
            v = tile_of(qkv3, at, 2 * width + lo)
            s = jnp.where(same, dot_nt(by_head(k), q), NEGATIVE)
            e = jnp.exp(s - per_head(s, lambda w: jnp.max(w, 0, keepdims=True)))
            p = (e * per_head(e, lambda w: 1.0 / jnp.sum(w, 0, keepdims=True))).astype(BF)
            pscr[t, p2] = p
            ot = dot(by_head_t(v), p)
            o2[:, at, lo : lo + LANES] = jnp.transpose(ot).astype(BF).reshape(feats, part, LANES)
        return 0

    lax.fori_loop(0, tiles, feat_fwd, 0, unroll=3)

    loads[3].wait()
    for b in range(2):
        at = slice(b * half, (b + 1) * half)
        o = o2[b * feats // 2 : (b + 1) * feats // 2, :, :].reshape(half, width)
        v = x1[at, :] + dot(o, wfo[...])
        x2[at, :] = v
        nn, _r = ln_parts(v)
        h3[at, :] = (nn * g3[...] + b3[...]).astype(BF)

    loads[4].wait()
    loads[5].wait()

    def ffn(c, _):
        cols = pl.ds(pl.multiple_of(c * FT, FT), FT)
        total = jnp.zeros((8, FT), F32)
        for b in range(2):
            at = slice(b * half, (b + 1) * half)
            z = dot(h3[at, :], wup[:, cols]) + ub[0:1, cols]
            w = GELU_C * GELU_A * (z * z) + GELU_C
            cdf = 0.5 * jnp.tanh(z * w) + 0.5
            g = z * cdf
            u[at, cols] = g.astype(BF)
            slope = cdf + g * (1.0 - cdf) * (6.0 * w - 4.0 * GELU_C)
            d = dot_nt(ct[at, :], wdn[cols, :]) * slope
            dz[at, cols] = d.astype(BF)
            total = total + jnp.sum(d.reshape(half // 8, 8, FT), 0)
        ubg[:, cols] = total
        return 0

    lax.fori_loop(0, hidden // FT, ffn, 0)

    vectors = []
    gg = jnp.zeros((1, width), F32)
    gb = jnp.zeros((1, width), F32)
    gd = jnp.zeros((1, width), F32)
    for b in range(2):
        at = slice(b * half, (b + 1) * half)
        y = x2[at, :] + dot(u[at, :], wdn[...]) + db[...]
        for j in range(feats // 2):
            f = b * (feats // 2) + j
            place(wide, f, count, feats, y[j * count : (j + 1) * count])
        dh = dot_nt(dz[at, :], wup[...])
        nn, r = ln_parts(x2[at, :])
        c = ct[at, :].astype(F32)
        gg = gg + jnp.sum(dh * nn, 0, keepdims=True)
        gb = gb + jnp.sum(dh, 0, keepdims=True)
        gd = gd + jnp.sum(c, 0, keepdims=True)
        v = c + ln_back(dh, nn, r, g3[...])
        dx2[at, :] = v
        do2[b * feats // 2 : (b + 1) * feats // 2, :, :] = (
            dot_nt(v.astype(BF), wfo[...]).astype(BF).reshape(feats // 2, count, width)
        )
    out[...] = lift(wide).reshape(count, feats, width).astype(BF)
    stores[0].start()
    vectors = [gg, gb, gd]

    core = lax.rem(me, 2)

    def slot(pos):
        at, other = divmod(pos, 2)
        refs = (a_send, b_send) if other else (a_keep, b_keep)
        return refs, at, 2 * at + (1 - core if other else core)

    piece = width // n
    fpiece = hidden // n

    def spread(group, base):
        for pos in range(n):
            refs, at, d = slot(pos)
            src = pl.multiple_of(d * piece, piece)
            refs[group][at, base : base + piece, :] = wblk[pl.ds(src, piece), :]

    base = 0
    for b in range(hidden // width):
        tr[...] = flip(u[:, b * width : (b + 1) * width])
        wdn_scr[b * width : (b + 1) * width, :] = dot(tr[...], ct[...]).astype(BF)
    for pos in range(n):
        refs, at, d = slot(pos)
        src = pl.multiple_of(d * fpiece, fpiece)
        refs[0][at, base : base + fpiece, :] = wdn_scr[pl.ds(src, fpiece), :]
    base += fpiece
    tr[...] = flip(h3[...])
    for b in range(hidden // width):
        wblk[...] = dot(tr[...], dz[:, b * width : (b + 1) * width]).astype(BF)
        spread(0, base)
        base += piece
    stores[3].start()
    stores[4].start()

    def feat_bwd(t, _):
        at = pl.ds(pl.multiple_of(t * part, part), part)
        for p2 in range(H // 2):
            lo = p2 * LANES
            q = tile_of(qkv3, at, lo)
            k = tile_of(qkv3, at, width + lo)
            v = tile_of(qkv3, at, 2 * width + lo)
            g = tile_of(do2, at, lo)
            p = pscr[t, p2]
            pf = p.astype(F32)
            dp = dot_nt(by_head(v), g)
            ds = pf * (dp - per_head(pf * dp, lambda w: jnp.sum(w, 0, keepdims=True)))
            ds = ds.astype(BF)
            dv = dot(side(p), by_head(g))
            dk = dot(side(ds), by_head(q))
            dq = jnp.transpose(dot(by_head_t(k), ds)) * SCALING
            for j, d in enumerate((dq, dk, dv)):
                dqkv[:, at, j * width + lo : j * width + lo + LANES] = d.astype(BF).reshape(
                    feats, part, LANES
                )
        return 0

    lax.fori_loop(0, tiles, feat_bwd, 0, unroll=3)

    gg = jnp.zeros((1, width), F32)
    gb = jnp.zeros((1, width), F32)
    for b in range(2):
        at = slice(b * half, (b + 1) * half)
        d = dqkv[b * feats // 2 : (b + 1) * feats // 2, :, :].reshape(half, 3 * width)
        dh = dot_nt(d, wfq[...])
        nn, r = ln_parts(x1[at, :])
        gg = gg + jnp.sum(dh * nn, 0, keepdims=True)
        gb = gb + jnp.sum(dh, 0, keepdims=True)
        v = dx2[at, :] + ln_back(dh, nn, r, g2[...])
        dx1[at, :] = v
        g = dot_nt(v.astype(BF), wso[...]).astype(BF)
        for j in range(feats // 2):
            f = b * (feats // 2) + j
            for c in range(hpd):
                do_send[f * hpd + c] = g[j * count : (j + 1) * count, c * cl : (c + 1) * cl]
    stores[1].start()
    stores[2].start()
    vectors = [gg, gb] + vectors

    base = 0
    tr[...] = flip(h2[...])
    for b in range(3):
        d = dqkv[:, :, b * width : (b + 1) * width].reshape(rows, width)
        wblk[...] = dot(tr[...], d).astype(BF)
        spread(1, base)
        base += piece
    tr[...] = flip(o2[...].reshape(rows, width))
    wblk[...] = dot(tr[...], dx2[...].astype(BF)).astype(BF)
    spread(1, base)
    base += piece
    tr[...] = flip(o1[...])
    wblk[...] = dot(tr[...], dx1[...].astype(BF)).astype(BF)
    spread(1, base)
    base += piece
    ubs = jnp.sum(ubg[...], 0, keepdims=True)
    vectors = vectors + [ubs[:, b * width : (b + 1) * width] for b in range(hidden // width)]
    vec = jnp.concatenate(vectors + [jnp.zeros((16 - len(vectors), width), F32)], 0).astype(BF)
    for pos in range(n):
        refs, at, _d = slot(pos)
        refs[1][at, base : base + 16, :] = vec
    stores[5].start()
    stores[6].start()
    for store in stores:
        store.wait()


def solution(mesh):
    n = mesh.shape["samp"]
    groups = mesh.shape["grp"]
    gbits = groups.bit_length() - 1
    tie = lax.optimization_barrier
    swap_core = [(d, d ^ 1) for d in range(n)]
    swap_y = [(d, d ^ 2) for d in range(n)]
    same_core = [[2 * k + c for k in range(n // 2)] for c in (0, 1)]

    def swap_grp(v, bit=0):
        return lax.ppermute(v, "grp", [(d, d ^ (1 << bit)) for d in range(groups)])

    def rest_of_grp(v):
        for bit in range(1, gbits):
            v = (v.astype(F32) + swap_grp(v, bit).astype(F32)).astype(BF)
        return v

    def body(
        tokens,
        segments,
        cotangent,
        first_gain,
        first_shift,
        sample_qkv,
        sample_out,
        second_gain,
        second_shift,
        feature_qkv,
        feature_out,
        third_gain,
        third_shift,
        up_weight,
        up_bias,
        down_weight,
        down_bias,
    ):
        count, feats, width = tokens.shape[1:]
        hidden = up_weight.shape[1]
        rows = count * feats
        hpd = n // feats
        hl = H // hpd
        cl = hl * HD
        total = n * count
        heads8 = 8
        me = lax.axis_index("samp")
        r = lax.rem(me, hpd)
        x = lax.rem(lax.axis_index("grp"), 2)
        y, z = (me >> 1) & 1, me >> 2
        r1, me1, x1, y1, z1 = (v.reshape(1).astype(jnp.int32) for v in (r, me, x, y, z))
        peers = [[q + hpd * k for k in range(feats)] for q in range(hpd)]
        g1, b1, g2, b2, g3, b3, ub, db = (
            v.reshape(1, -1)
            for v in (
                first_gain,
                first_shift,
                second_gain,
                second_shift,
                third_gain,
                third_shift,
                up_bias,
                down_bias,
            )
        )

        def shift(s):
            return [(d, d // hpd * hpd + (d % hpd + s) % hpd) for d in range(n)]

        (xt,) = call(
            pack_kernel,
            [((feats, count + PAD, width), BF)],
            [pltpu.VMEM((width // LANES, rows, LANES), F32)],
            tokens[0],
            segments,
        )
        mine = lax.all_to_all(xt, "samp", 0, 0, tiled=True, axis_index_groups=peers)
        xparts = [mine] + [lax.ppermute(mine, "samp", shift(s)) for s in range(1, hpd)]

        o_send, xs, ot, lse, rank_row, rank_col, starts = call(
            functools.partial(fwd_kernel, hpd, hl),
            [
                ((n, count, cl), BF),
                ((total, width), BF),
                ((cl, total), BF),
                ((heads8, total), F32),
                ((8, total), F32),
                ((total, LANES), F32),
                ((8,), jnp.int32),
            ],
            [
                pltpu.VMEM((total, width), BF),
                pltpu.VMEM((total, LANES), F32),
                pltpu.VMEM((hl, LANES, total), BF),
                pltpu.VMEM((total, cl), BF),
                pltpu.VMEM((hl, HD + 16, total), BF),
                pltpu.VMEM((total, cl), BF),
                pltpu.VMEM((total, LANES), F32),
                pltpu.VMEM((8, total), F32),
                pltpu.VMEM((hl, HD + 16, TQ), F32),
                pltpu.VMEM((hl, 8, TQ), F32),
                pltpu.VMEM((hl, total, TQ), F32),
                pltpu.VMEM((cl, width), BF),
                pltpu.VMEM((cl, width), BF),
            ],
            r1,
            *xparts,
            g1,
            b1,
            sample_qkv,
            smem=(0,),
            smem_out=(6,),
            vmem=58,
        )
        o_recv = lax.all_to_all(o_send, "samp", 0, 0, tiled=True)

        piece = width // n
        fpiece = hidden // n
        apieces = fpiece + piece * (hidden // width)
        bpieces = piece * 5 + 16
        vm = pltpu.VMEM
        out, dx1, do_send, a_keep, a_send, b_keep, b_send = call(
            functools.partial(rows_kernel, hpd),
            [
                ((count, feats, width), BF),
                ((rows, width), F32),
                ((n, count, cl), BF),
                ((n // 2, apieces, width), BF),
                ((n // 2, apieces, width), BF),
                ((n // 2, bpieces, width), BF),
                ((n // 2, bpieces, width), BF),
            ],
            [
                vm((width, width), BF),
                vm((width, 3 * width), BF),
                vm((width, width), BF),
                vm((width, hidden), BF),
                vm((hidden, width), BF),
                vm((count, feats, width), BF),
                vm((count, feats, width), BF),
                vm((rows, width), F32),
                vm((n, count, cl), BF),
                vm((n // 2, apieces, width), BF),
                vm((n // 2, apieces, width), BF),
                vm((n // 2, bpieces, width), BF),
                vm((n // 2, bpieces, width), BF),
                vm((width // LANES, rows, LANES), F32),
                vm((rows, width), BF),
                vm((rows, width), BF),
                vm((rows, width), F32),
                vm((rows, width), BF),
                vm((feats, count, 3 * width), BF),
                vm((feats, count, width), BF),
                vm((rows, width), F32),
                vm((rows, width), BF),
                vm((rows, hidden), BF),
                vm((rows, hidden), BF),
                vm((rows, width), F32),
                vm((feats, count, width), BF),
                vm((feats, count, 3 * width), BF),
                vm((count // 16, H // 2, 32 * feats, 16 * feats), BF),
                vm((width, rows), BF),
                vm((width, width), BF),
                vm((8, hidden), F32),
                vm((hidden, width), BF),
                pltpu.SemaphoreType.DMA((6,)),
                pltpu.SemaphoreType.DMA((7,)),
            ],
            me1,
            o_recv,
            xt,
            cotangent[0],
            g2,
            b2,
            g3,
            b3,
            ub,
            db,
            sample_out,
            feature_qkv,
            feature_out,
            up_weight,
            down_weight,
            smem=(0,),
            hbm=(3, 10, 11, 12, 13, 14),
            hbm_out=tuple(range(7)),
            vmem=48,
        )
        a_got = lax.ppermute(a_send, "samp", swap_core)
        b_got = lax.ppermute(b_send, "samp", swap_core)
        do_recv = lax.all_to_all(do_send, "samp", 0, 0, tiled=True)

        qr = q_rows(cl, width)
        half = apieces // 2
        zs = n // 4

        def along_z(pieces, unit):
            return [pieces[0]] + [
                lax.ppermute(pieces[c], "samp", [(d, d ^ (unit * c)) for d in range(n)])
                for c in range(1, len(pieces))
            ]

        am, ao, cm, co = call(
            first_sums,
            [((n // 2, half, width), BF)] * 2 + [((n // 4, bpieces, width), BF)] * 2,
            [],
            x1,
            y1,
            a_keep,
            a_got,
            b_keep,
            b_got,
            smem=(0, 1),
            vmem=16,
        )
        ag, cg = swap_grp(ao), lax.ppermute(co, "samp", swap_y)
        xs_after, _ = tie((xs, am))
        k_all, v_all, kt_all, qtz, nt = call(
            functools.partial(prep_kernel, hl),
            [
                ((total, cl), BF),
                ((total, cl), BF),
                ((cl, total), BF),
                ((hl, LANES, total), BF),
                ((width, total), BF),
            ],
            [vm((cl, width), BF), vm((cl, width), BF)],
            r1,
            xs_after,
            g1,
            b1,
            sample_qkv,
            smem=(0,),
            vmem=58,
        )
        (dt,) = call(
            functools.partial(bwd_kernel, hpd, hl),
            [((3 * cl, total), BF)],
            [
                vm((total, cl), BF),
                vm((hl, LANES, total), BF),
                vm((8, total), F32),
                vm((total, LANES), F32),
                vm((8, total), F32),
                vm((cl, total), F32),
                vm((cl, total), F32),
                vm((cl, total), F32),
                vm((hl, KB, QB), BF),
                vm((hl, KB, QB), BF),
                pltpu.SMEM(((total // KB) * (total // QB),), jnp.int32),
                vm((total, cl), BF),
                vm((total, cl), BF),
                vm((cl, total), BF),
                vm((hl, LANES, total), BF),
                pltpu.SemaphoreType.DMA((4,)),
            ],
            r1,
            starts,
            do_recv,
            k_all,
            v_all,
            kt_all,
            qtz,
            ot,
            lse,
            rank_row,
            smem=(0, 1),
            hbm=(3, 4, 5, 6),
            vmem=58,
        )
        am, ag, cm, cg, _ = tie((am, ag, cm, cg, dt))
        q_keep, q_send, am, ao, cm, co = call(
            dw_kernel,
            [((feats, qr, width), BF)] * 2
            + [((n // 4, half, width), BF)] * 2
            + [((zs // 2, bpieces, width), BF)] * 2,
            [vm((width, 3 * cl), F32), vm((width, 3 * cl), BF)],
            r1,
            x1,
            y1,
            z1,
            dt,
            nt,
            sample_qkv,
            g1,
            b1,
            am,
            ag,
            cm,
            cg,
            smem=(0, 1, 2, 3),
            vmem=16,
        )
        ag = lax.ppermute(ao, "samp", swap_y)
        cg = lax.ppermute(co, "samp", [(d, d ^ (n // 2)) for d in range(n)])
        dt, _ = tie((dt, q_send))
        dhs = call(
            functools.partial(dh_kernel, hpd),
            [((feats // CUTS, count, width), BF)] * (CUTS * hpd),
            [vm((width, total), BF)],
            r1,
            dt,
            sample_qkv,
            rank_col,
            smem=(0,),
            vmem=16,
        )
        parts = list(dhs[:CUTS])
        for s in range(1, hpd):
            parts += [lax.ppermute(v, "samp", shift(-s)) for v in dhs[CUTS * s : CUTS * s + CUTS]]
        pieces = call(
            middle_sums,
            [((half, width), BF)] * zs + [((bpieces, width), BF)] * (zs // 2),
            [],
            z1,
            am,
            ag,
            cm,
            cg,
            smem=(0,),
        )
        parts[0], _ = tie((parts[0], pieces[0]))
        a_pieces, c_pieces = along_z(pieces[:zs], 4), along_z(pieces[zs:], 4)
        (both,) = call(
            functools.partial(norm_kernel, hpd),
            [((feats, count + qr, width), BF)],
            [],
            *parts,
            mine,
            g1,
            q_keep,
            swap_grp(q_send),
            vmem=10,
        )
        both_send, *ends = tie((both, *a_pieces, *c_pieces))
        a_pieces, c_pieces = ends[:zs], ends[zs:]
        both = lax.all_to_all(both_send, "samp", 0, 0, tiled=True, axis_index_groups=peers)

        def last_steps(*pieces):
            (c_sum,) = call(sum_kernel, [((bpieces, width), BF)], [], *pieces[zs:])
            c_sum = rest_of_grp(c_sum)
            (a_side,) = call(sum_kernel, [((half, width), BF)], [], *pieces[:zs])
            a_side = rest_of_grp(a_side)
            return a_side, swap_grp(a_side), c_sum, swap_grp(c_sum)

        terms = (*a_pieces, *c_pieces)
        parts_summed = last_steps(*tie((*terms, both_send))[: len(terms)])
        grad_tokens, q_sum = call(
            final_kernel,
            [((count, feats, width), F32), ((qr, width), BF)],
            [vm((width // LANES, rows, LANES), F32)],
            dx1,
            both,
            vmem=12,
        )
        q_sum = rest_of_grp(q_sum)

        def from_peer(s, other):
            if not s and not other:
                return q_sum
            pairs = [
                (g * n + d, (g ^ other) * n + e) for g in range(groups) for d, e in shift(s)
            ]
            return lax.ppermute(q_sum, ("grp", "samp"), pairs)

        peers_same = [from_peer(s, 0) for s in range(hpd)]
        peers_other = [from_peer(s, 1) for s in range(hpd)]
        grad_sample_qkv, vec_sum, grad_down, grad_up, grad_fqkv, grad_fout, grad_sout, vu = call(
            functools.partial(gather_kernel, hpd),
            [
                ((piece, 3 * width), F32),
                ((8, width), F32),
                ((fpiece, width), F32),
                ((piece, hidden), F32),
                ((piece, 3 * width), F32),
                ((piece, width), F32),
                ((piece, width), F32),
                ((16, width), F32),
            ],
            [],
            r1,
            x1,
            *peers_same,
            *peers_other,
            *parts_summed,
            smem=(0, 1),
        )

        def own(v):
            return lax.dynamic_slice_in_dim(v, me * (v.shape[0] // n), v.shape[0] // n, 0)

        def own_rows(v):
            return lax.dynamic_slice_in_dim(v, me * piece, piece, 1)

        five = own_rows(vu[:5])
        two = own_rows(vec_sum[:2])
        vectors = [five[i] for i in range(5)]
        vectors.append(own(vu[5 : 5 + hidden // width].reshape(-1)))
        return (
            out[None],
            grad_tokens[None],
            two[0],
            two[1],
            grad_sample_qkv,
            grad_sout,
            vectors[0],
            vectors[1],
            grad_fqkv,
            grad_fout,
            vectors[2],
            vectors[3],
            grad_up,
            vectors[5],
            grad_down,
            vectors[4],
        )

    rep = P()
    data = P("grp", "samp", None, None)
    line = P("samp")
    flat = P("samp", None)
    in_specs = (data, P("grp", "samp"), data) + (rep,) * 14
    out_specs = (
        data,
        data,
        line,
        line,
        flat,
        flat,
        line,
        line,
        flat,
        flat,
        line,
        line,
        flat,
        line,
        flat,
        line,
    )
    return jax.shard_map(body, mesh=mesh, in_specs=in_specs, out_specs=out_specs, check_vma=False)
```
